32 devices in a mesh: groups: 2 (over y), row: 4 (over z), col: 4 (over x, core).
Axes of the slice: x: 2, y: 2, z: 4, core: 2. Of those that a mesh axis runs over, the one named last changes fastest.
Arguments:
- currents: float32 [2, 16, 8, 2048], P(None, ('groups', 'row'), 'col'), parts along dimension 1, may hold values from -6 to 6
- library: bfloat16 [32, 64, 128], replicated, may hold values from -0.0546875 to 0.0546875
- block_ids: int32 [16, 8, 25], P(('groups', 'row'), 'col'), parts along dimension 0, may hold values from 0 to 31
- dirs: float32 [2, 2048], replicated, may hold values from -0.7 to 0.7
- beam_dir: int32 [64], P('groups'), parts along dimension 0, may hold values from 0 to 2047
Outputs:
- new_currents: float32 [2, 16, 8, 2048], P(None, ('groups', 'row'), 'col'), parts along dimension 1
- far_pattern: float32 [4096, 64], P(('groups', 'row', 'col')), parts along dimension 0
The draws below stay inside these ranges and needn't reach their ends.
There are 2 independent parts, one for each index of `groups`. The reference program is written for one: setup_inputs(seed, part) draws one part's arguments, and reference() takes and returns one part's arrays. A program takes and returns all parts, laid end to end along the dimension named above; an argument that names none is the same for every part. Nothing has to cross between parts.
All inputs are finite; a program needn't handle non-finite values.
Results may differ from the reference program's by a relative error of at most 0.0065.
Values may be sent and summed in bfloat16 or wider, within the bound.
No kernel may reach another device: no remote copies, remote signals or barrier semaphores. Data moves between devices by JAX's collectives and lax.ppermute only.
A program may use at most 64 MiB of HBM per device.

```python
import math
import jax
import jax.numpy as jnp
from jax import lax

SUB = 8
E = 64
B = 32
DIR = 2048
NV = 32
ITERS = 1
NR = 8
NC = 8
NEL = 4096


def with_ends(array, stream_key, low, largest):
    dims = array.shape
    index_at = [jax.random.randint(jax.random.fold_in(stream_key, axis), (), 0, dims[axis]) for axis in range(len(dims))]
    array = array.at[tuple(index_at)].set(low)
    longest = dims.index(max(dims))
    index_at[longest] = (index_at[longest] + 1) % dims[longest]
    return array.at[tuple(index_at)].set(largest)


def block_scale(own_key, extent, shards, low, top_value):
    level = 1.0
    for position, parts in shards:
        steps = jax.random.uniform(jax.random.fold_in(jax.random.fold_in(own_key, 6), position), (parts,), jnp.float32, low / len(shards), top_value / len(shards))
        level = level * jnp.repeat(jnp.exp(steps), extent[position] // parts).reshape((-1,) + (1,) * (len(extent) - 1 - position))
    return level


def noise(own_key, shape, scale, limit, cuts=(), kind=jnp.bfloat16):
    result = scale * jax.random.normal(own_key, shape, jnp.float32)
    if cuts:
        result = result * block_scale(own_key, shape, cuts, -0.22, 0.18)
    return jnp.clip(result, -limit, limit).astype(kind)


def setup_inputs(seed: int = 0, part: int = 0) -> dict:
    key_of = jax.random.split(jax.random.key(seed), 6)
    own_keys = jax.random.split(jax.random.fold_in(key_of[5], part), 6)
    return {
        "currents": noise(own_keys[0], (2, NR, NC, E * B), 1.0, 6.0, ((1, 4), (2, 4)), jnp.float32),
        "library": noise(key_of[1], (NV, E, 2 * E), (200 * E) ** -0.5, 0.0546875),
        "block_ids": with_ends(jax.random.randint(own_keys[2], (NR, NC, 25), 0, NV), jax.random.fold_in(own_keys[2], 1), 0, NV - 1).astype(jnp.int32),
        "dirs": jnp.clip(jax.random.uniform(key_of[3], (2, DIR), jnp.float32, -0.7, 0.7), -0.7, 0.7),
        "beam_dir": with_ends(jax.random.randint(own_keys[4], (B,), 0, DIR), jax.random.fold_in(own_keys[4], 1), 0, DIR - 1).astype(jnp.int32),
    }


pi_value = 3.141592653589793
ref_block = 256

def phases(dir_rows, sub_pos, elem_pos):
    sub_angle = pi_value * (dir_rows[0][:, None] * sub_pos[0][None, :] + dir_rows[1][:, None] * sub_pos[1][None, :])
    elem_angle = pi_value * (dir_rows[0][:, None] * elem_pos[0][None, :] + dir_rows[1][:, None] * elem_pos[1][None, :])
    sub_cos = jnp.cos(sub_angle)[:, :, None]
    sub_sin = jnp.sin(sub_angle)[:, :, None]
    elem_cos = jnp.cos(elem_angle)[:, None, :]
    elem_sin = jnp.sin(elem_angle)[:, None, :]
    cosine = sub_cos * elem_cos - sub_sin * elem_sin
    sine = sub_sin * elem_cos + sub_cos * elem_sin
    count = dir_rows.shape[1]
    return (cosine.reshape(count, -1).astype(jnp.bfloat16), (-sine).reshape(count, -1).astype(jnp.bfloat16))

def positions():
    row_ids = jnp.arange(NR, dtype=jnp.int32)[:, None]
    col_ids = jnp.arange(NC, dtype=jnp.int32)[None, :]
    sub_x = (col_ids * SUB + 0 * row_ids).reshape(-1).astype(jnp.float32) - (NC * SUB - 1) / 2.0
    sub_y = (row_ids * SUB + 0 * col_ids).reshape(-1).astype(jnp.float32) - (NR * SUB - 1) / 2.0
    elem_ids = jnp.arange(E, dtype=jnp.int32)
    elem_x = (elem_ids % SUB).astype(jnp.float32)
    elem_y = (elem_ids // SUB).astype(jnp.float32)
    return ((sub_x, sub_y), (elem_x, elem_y))

def coupling(current_field, block_ids, library, adjoint):
    rounded = current_field.astype(jnp.bfloat16).reshape(2, NR, NC, E, B)
    padded = jnp.pad(rounded, ((0, 0), (2, 2), (2, 2), (0, 0), (0, 0)))
    padded_ids = jnp.pad(block_ids, ((2, 2), (2, 2), (0, 0)))
    blocks_wide = library.astype(jnp.float32)
    out_re = jnp.zeros((NR, NC, E, B), jnp.float32)
    out_im = jnp.zeros((NR, NC, E, B), jnp.float32)
    spec = 'rcji,rcjb->rcib' if adjoint else 'rcij,rcjb->rcib'
    for row_off in range(5):
        for col_off in range(5):
            slot_index = 5 * row_off + col_off
            if adjoint:
                row_start = 4 - row_off
                col_start = 4 - col_off
                chosen = padded_ids[row_start:row_start + NR, col_start:col_start + NC, slot_index]
            else:
                row_start = row_off
                col_start = col_off
                chosen = block_ids[:, :, slot_index]
            blocks = blocks_wide[chosen]
            block_re = blocks[..., :E]
            block_im = blocks[..., E:]
            source = padded[:, row_start:row_start + NR, col_start:col_start + NC].astype(jnp.float32)
            real_real = jnp.einsum(spec, block_re, source[0], precision=lax.Precision.HIGHEST)
            real_imag = jnp.einsum(spec, block_re, source[1], precision=lax.Precision.HIGHEST)
            imag_real = jnp.einsum(spec, block_im, source[0], precision=lax.Precision.HIGHEST)
            imag_imag = jnp.einsum(spec, block_im, source[1], precision=lax.Precision.HIGHEST)
            if adjoint:
                out_re = out_re + real_real + imag_imag
                out_im = out_im + real_imag - imag_real
            else:
                out_re = out_re + real_real - imag_imag
                out_im = out_im + real_imag + imag_real
    return jnp.stack([out_re, out_im]).reshape(2, NR, NC, E * B)

def radiate(current_field, block_ids, library):
    total_field = (current_field + coupling(current_field, block_ids, library, False)).astype(jnp.bfloat16)
    return jnp.concatenate([total_field[0].reshape(NEL, B), total_field[1].reshape(NEL, B)], axis=1)

def forward_pattern(radiated_cols, dirs, sub_pos, elem_pos):

    def one_block(row_begin):
        dir_rows = lax.dynamic_slice_in_dim(dirs, row_begin, ref_block, 1)
        cosine, sine = phases(dir_rows, sub_pos, elem_pos)
        cos_part = jnp.dot(cosine, radiated_cols, preferred_element_type=jnp.float32)
        sin_part = jnp.dot(sine, radiated_cols, preferred_element_type=jnp.float32)
        return jnp.concatenate([cos_part[:, :B] - sin_part[:, B:], cos_part[:, B:] + sin_part[:, :B]], axis=1)
    starts = jnp.arange(DIR // ref_block, dtype=jnp.int32) * ref_block
    stacked = lax.map(one_block, starts)
    return stacked.reshape(DIR, 2 * B) * (1.0 / math.sqrt(NEL))

def adjoint_pattern(residual_b, dirs, sub_pos, elem_pos):

    def add_block(totals, row_begin):
        piece_rows = lax.dynamic_slice_in_dim(residual_b, row_begin, ref_block, 0)
        dir_rows = lax.dynamic_slice_in_dim(dirs, row_begin, ref_block, 1)
        cosine, sine = phases(dir_rows, sub_pos, elem_pos)
        cos_part = jnp.dot(cosine.T, piece_rows, preferred_element_type=jnp.float32)
        sin_part = jnp.dot(sine.T, piece_rows, preferred_element_type=jnp.float32)
        return ((totals[0] + cos_part, totals[1] + sin_part), None)
    zero_acc = jnp.zeros((NEL, 2 * B), jnp.float32)
    starts = jnp.arange(DIR // ref_block, dtype=jnp.int32) * ref_block
    totals, unused = lax.scan(add_block, (zero_acc, zero_acc), starts)
    p_part, q_part = totals
    scale = 1.0 / math.sqrt(NEL)
    grad_re = (p_part[:, :B] + q_part[:, B:]) * scale
    grad_im = (p_part[:, B:] - q_part[:, :B]) * scale
    return jnp.stack([grad_re.reshape(NR, NC, E * B), grad_im.reshape(NR, NC, E * B)])

def reference(currents, library, block_ids, dirs, beam_dir):
    sub_pos, elem_pos = positions()
    amplitude = math.sqrt(NEL) / 16.0
    dir_ids = jnp.arange(DIR, dtype=jnp.int32)
    real_target = amplitude * (dir_ids[:, None] == beam_dir[None, :]).astype(jnp.float32)
    target = jnp.concatenate([real_target, jnp.zeros_like(real_target)], axis=1)
    pattern = forward_pattern(radiate(currents, block_ids, library), dirs, sub_pos, elem_pos)
    for iteration in range(ITERS):
        residual = pattern - target
        back = adjoint_pattern(residual.astype(jnp.bfloat16), dirs, sub_pos, elem_pos)
        gradient = back + coupling(back, block_ids, library, True)
        image_pattern = forward_pattern(radiate(gradient, block_ids, library), dirs, sub_pos, elem_pos)
        products = lax.optimization_barrier(jnp.sum(image_pattern * residual, axis=0))
        squares = lax.optimization_barrier(jnp.sum(image_pattern * image_pattern, axis=0))
        numerator = products[:B] + products[B:]
        denominator = squares[:B] + squares[B:] + 1e-06
        step_size = numerator / denominator
        currents = currents - (gradient.reshape(2, NR, NC, E, B) * step_size).reshape(currents.shape)
        pattern = pattern - image_pattern * jnp.concatenate([step_size, step_size])
    return (currents, pattern)
```

```python
import functools
import math

import jax
import jax.numpy as jnp
from jax import lax
from jax.experimental import pallas as pl
from jax.experimental.pallas import tpu as pltpu
from jax.sharding import PartitionSpec as P

pi_value = 3.141592653589793
dir_block = 512


def with_halo(cells, sides, width):
    for axis, dim in sides:
        count = lax.axis_size(axis)
        ends = count - 1
        head = lax.slice_in_dim(cells, 0, width, axis=dim)
        tail = lax.slice_in_dim(cells, cells.shape[dim] - width, cells.shape[dim], axis=dim)
        cells = jnp.concatenate(
            [
                lax.ppermute(tail, axis, [(i, (i + 1) % count) for i in range(ends)]),
                cells,
                lax.ppermute(head, axis, [((i + 1) % count, i) for i in range(ends)]),
            ],
            axis=dim,
        )
    return cells


def phases(dir_rows, sub_pos, elem_pos):
    sub_angle = pi_value * (
        dir_rows[0][:, None] * sub_pos[0][None, :] + dir_rows[1][:, None] * sub_pos[1][None, :]
    )
    elem_angle = pi_value * (
        dir_rows[0][:, None] * elem_pos[0][None, :] + dir_rows[1][:, None] * elem_pos[1][None, :]
    )
    sub_cos = jnp.cos(sub_angle)[:, :, None]
    sub_sin = jnp.sin(sub_angle)[:, :, None]
    elem_cos = jnp.cos(elem_angle)[:, None, :]
    elem_sin = jnp.sin(elem_angle)[:, None, :]
    cosine = sub_cos * elem_cos - sub_sin * elem_sin
    sine = sub_sin * elem_cos + sub_cos * elem_sin
    count = dir_rows.shape[1]
    return (
        cosine.reshape(count, -1).astype(jnp.bfloat16),
        (-sine).reshape(count, -1).astype(jnp.bfloat16),
    )


def coupling(padded, id_table, library, adjoint):
    rows_here = padded.shape[1] - 4
    cols_here = padded.shape[2] - 4
    elems = library.shape[1]
    field_view = padded.reshape(2, rows_here + 4, cols_here + 4, elems, -1)
    spec = "rcnji,rcnjb->rcib" if adjoint else "rcnij,rcnjb->rcib"
    out_re = jnp.zeros((rows_here, cols_here, elems, field_view.shape[4]), jnp.float32)
    out_im = jnp.zeros_like(out_re)
    for row_off in range(5):
        sources = []
        chosen = []
        for col_off in range(5):
            slot_index = 5 * row_off + col_off
            if adjoint:
                row_start = 4 - row_off
                col_start = 4 - col_off
                chosen.append(
                    id_table[
                        row_start : row_start + rows_here,
                        col_start : col_start + cols_here,
                        slot_index,
                    ]
                )
            else:
                row_start = row_off
                col_start = col_off
                chosen.append(id_table[:, :, slot_index])
            sources.append(
                field_view[:, row_start : row_start + rows_here, col_start : col_start + cols_here]
            )
        source_stack = jnp.stack(sources, axis=3)
        block_stack = library[jnp.stack(chosen, axis=2)]
        block_re = block_stack[..., :elems]
        block_im = block_stack[..., elems:]
        real_real = jnp.einsum(spec, block_re, source_stack[0], preferred_element_type=jnp.float32)
        real_imag = jnp.einsum(spec, block_re, source_stack[1], preferred_element_type=jnp.float32)
        imag_real = jnp.einsum(spec, block_im, source_stack[0], preferred_element_type=jnp.float32)
        imag_imag = jnp.einsum(spec, block_im, source_stack[1], preferred_element_type=jnp.float32)
        if adjoint:
            out_re = out_re + real_real + imag_imag
            out_im = out_im + real_imag - imag_real
        else:
            out_re = out_re + real_real - imag_imag
            out_im = out_im + real_imag + imag_real
    return jnp.stack([out_re, out_im])


def pattern_term(radiated_cols, dirs, sub_pos, elem_pos, row_count, scale):
    half_cols = radiated_cols.shape[1] // 2

    def one_block(begin_row, block_size):
        dir_rows = lax.dynamic_slice_in_dim(dirs, begin_row, block_size, 1)
        cosine, sine = phases(dir_rows, sub_pos, elem_pos)
        cos_part = jnp.dot(cosine, radiated_cols, preferred_element_type=jnp.float32)
        sin_part = jnp.dot(sine, radiated_cols, preferred_element_type=jnp.float32)
        return jnp.concatenate(
            [
                cos_part[:, :half_cols] - sin_part[:, half_cols:],
                cos_part[:, half_cols:] + sin_part[:, :half_cols],
            ],
            axis=1,
        )

    block_count = row_count // dir_block
    starts = jnp.arange(block_count, dtype=jnp.int32) * dir_block
    stacked = lax.map(lambda begin_row: one_block(begin_row, dir_block), starts)
    pieces = stacked.reshape(block_count * dir_block, 2 * half_cols)
    return pieces * scale


def adjoint_piece(carry, residual_rows, dirs, sub_pos, elem_pos):
    row_count = residual_rows.shape[0]
    dims_spec = (((0,), (0,)), ((), ()))

    def add_block(totals, local_start, block_size):
        piece_rows = lax.dynamic_slice_in_dim(residual_rows, local_start, block_size, 0)
        dir_rows = lax.dynamic_slice_in_dim(dirs, local_start, block_size, 1)
        cosine, sine = phases(dir_rows, sub_pos, elem_pos)
        cos_part = lax.dot_general(
            cosine, piece_rows, dims_spec, preferred_element_type=jnp.float32
        )
        sin_part = lax.dot_general(sine, piece_rows, dims_spec, preferred_element_type=jnp.float32)
        return (totals[0] + cos_part, totals[1] + sin_part)

    block_count = row_count // dir_block
    carry = lax.fori_loop(
        0,
        block_count,
        lambda number, totals: add_block(totals, number * dir_block, dir_block),
        carry,
    )
    return carry


def line_terms(image_pattern, residual, beams):
    products = jnp.sum(image_pattern * residual, axis=0)
    squares = jnp.sum(image_pattern * image_pattern, axis=0)
    return (products[:beams] + products[beams:], squares[:beams] + squares[beams:])


def by_elements(currents, library, block_ids, dirs, beam_dir):
    beams = beam_dir.shape[0]
    rows_here = currents.shape[1]
    cols_here = currents.shape[2]
    packed = currents.shape[3]
    elems = library.shape[1]
    side = math.isqrt(elems)
    local_elems = rows_here * cols_here * elems
    total_rows = rows_here * lax.axis_size("row")
    total_cols = cols_here * lax.axis_size("col")
    all_elems = total_rows * total_cols * elems
    scale = 1.0 / math.sqrt(all_elems)
    amplitude = math.sqrt(all_elems) / 16.0
    dir_total = dirs.shape[1]
    share_rows = dir_total // lax.axis_size(("row", "col"))
    row_ids = (lax.axis_index("row") * rows_here + jnp.arange(rows_here, dtype=jnp.int32))[:, None]
    col_ids = (lax.axis_index("col") * cols_here + jnp.arange(cols_here, dtype=jnp.int32))[None, :]
    sub_x = (col_ids * side + 0 * row_ids).reshape(-1).astype(jnp.float32) - (
        total_cols * side - 1
    ) / 2.0
    sub_y = (row_ids * side + 0 * col_ids).reshape(-1).astype(jnp.float32) - (
        total_rows * side - 1
    ) / 2.0
    elem_ids = jnp.arange(elems, dtype=jnp.int32)
    sub_pos = (sub_x, sub_y)
    elem_pos = ((elem_ids % side).astype(jnp.float32), (elem_ids // side).astype(jnp.float32))
    padded_ids = with_halo(block_ids, (("row", 0), ("col", 1)), 2)

    def radiate(current_field):
        rounded = current_field.astype(jnp.bfloat16)
        padded = with_halo(rounded, (("row", 1), ("col", 2)), 2)
        coupled = coupling(padded, block_ids, library, False)
        total_field = (current_field.reshape(coupled.shape) + coupled).astype(jnp.bfloat16)
        return jnp.concatenate(
            [
                total_field[0].reshape(local_elems, beams),
                total_field[1].reshape(local_elems, beams),
            ],
            axis=1,
        )

    zero_acc = jnp.zeros((local_elems, 2 * beams), jnp.float32)

    def share_pattern(current_field):
        radiated_cols = radiate(current_field)
        return lax.psum_scatter(
            pattern_term(
                radiated_cols,
                dirs,
                sub_pos,
                elem_pos,
                share_rows * lax.axis_size(("row", "col")),
                scale,
            ),
            ("row", "col"),
            scatter_dimension=0,
            tiled=True,
        )

    share = share_pattern(currents)
    dir_ids = lax.axis_index(("row", "col")) * share_rows + jnp.arange(share_rows, dtype=jnp.int32)
    real_part = amplitude * (dir_ids[:, None] == beam_dir[None, :]).astype(jnp.float32)
    target = jnp.concatenate([real_part, jnp.zeros_like(real_part)], axis=1)
    residual = share - target
    totals = adjoint_piece(
        (zero_acc, zero_acc),
        lax.all_gather(residual.astype(jnp.bfloat16), ("row", "col"), axis=0, tiled=True),
        dirs,
        sub_pos,
        elem_pos,
    )
    p_part, q_part = totals
    grad_re = (p_part[:, :beams] + q_part[:, beams:]) * scale
    grad_im = (p_part[:, beams:] - q_part[:, :beams]) * scale
    raw_gradient = jnp.stack(
        [
            grad_re.reshape(rows_here, cols_here, packed),
            grad_im.reshape(rows_here, cols_here, packed),
        ]
    )
    rounded = raw_gradient.astype(jnp.bfloat16)
    padded = with_halo(rounded, (("row", 1), ("col", 2)), 2)
    gradient = raw_gradient + coupling(padded, padded_ids, library, True).reshape(
        raw_gradient.shape
    )
    image_pattern = share_pattern(gradient)
    part_num, part_den = line_terms(image_pattern, residual, beams)
    numerator, denominator = lax.psum((part_num, part_den), ("row", "col"))
    step_size = numerator / (denominator + 1e-06)
    moved = gradient.reshape(2, rows_here, cols_here, elems, beams) * step_size
    currents = currents - moved.reshape(currents.shape)
    share = share - image_pattern * jnp.concatenate([step_size, step_size])
    return (currents, share)


lanes = 128
chunk = 256
sin_fit = (3.141592580044754, -5.167706878916943, 2.5500313770294833, -0.5980451722529145, 0.07722012475690251)
cos_fit = (0.9999999535196061, -4.934792861473954, 4.058411954029988, -1.3318803713197287, 0.21969716737372766)


def iota(shape, dim):
    return lax.broadcasted_iota(jnp.int32, shape, dim)


def turn(angle):
    whole = jnp.round(angle)
    rest = angle - whole
    half = 0.5 * whole
    sign = 1.0 - 4.0 * (half - jnp.floor(half))
    square = rest * rest
    sine = sin_fit[4]
    cosine = cos_fit[4]
    for k in (3, 2, 1, 0):
        sine = sine * square + sin_fit[k]
        cosine = cosine * square + cos_fit[k]
    return cosine * sign, sine * rest * sign


def shuffle(elems, places):
    size = 2 * elems * places
    row = iota((size, 1), 0)
    kept = 2 * places
    groups = size // lanes
    k = row // lanes
    q = (row % lanes) // kept
    half = (row % kept) // places
    p = row % places
    goal = p * (2 * elems) + half * elems + q * groups + k
    return (goal == iota((size, size), 1)).astype(jnp.float32).astype(jnp.bfloat16)


def split_kernel(ranks, beams, elems, currents, ids, out):
    _, rows, cols, packed = currents.shape
    places = rows * cols
    groups = lanes // beams
    field = jnp.concatenate([currents[a, b] for a in range(2) for b in range(rows)], axis=0)
    tiles = jnp.concatenate(
        [field[:, i * lanes : (i + 1) * lanes] for i in range(packed // lanes)], axis=0
    ).T
    high = tiles.astype(jnp.bfloat16)
    low = (tiles - high.astype(jnp.float32)).astype(jnp.bfloat16)
    stacked = jnp.concatenate(
        [
            jnp.concatenate([part[k * beams : (k + 1) * beams] for k in range(groups)], axis=1)
            for part in (high, low)
        ],
        axis=0,
    )
    moved = jnp.dot(stacked, shuffle(elems, places), preferred_element_type=jnp.float32)
    moved = moved[:beams] + moved[beams:]
    for bl in range(beams // ranks):
        for p in range(places):
            out[pl.ds(bl * places + p, ranks, stride=16), :] = moved[
                bl * ranks : (bl + 1) * ranks, p * lanes : (p + 1) * lanes
            ]
    slots = ids.shape[2]
    table = jnp.concatenate([ids[a] for a in range(rows)], axis=0).astype(jnp.float32)
    table = jnp.concatenate([table, jnp.zeros((places, lanes - slots), jnp.float32)], axis=1)
    table = jnp.concatenate([table, jnp.zeros_like(table)], axis=0)
    for m in range(ranks):
        out[m * 16 + 8 : m * 16 + 16, :] = table


def join_kernel(ranks, beams, elems, currents, moved_in, new_currents, far, work):
    _, rows, cols, packed = currents.shape
    places = rows * cols
    groups = lanes // beams
    share = beams // ranks
    work[...] = moved_in[...].astype(jnp.float32)

    def rows_of(first):
        return work[pl.ds(first, ranks, stride=16), :]

    stacked = jnp.concatenate(
        [
            jnp.concatenate([rows_of(bl * places + p) for p in range(places)], axis=1)
            for bl in range(share)
        ],
        axis=0,
    ).astype(jnp.bfloat16)
    back = lax.dot_general(
        stacked,
        shuffle(elems, places),
        (((1,), (1,)), ((), ())),
        preferred_element_type=jnp.float32,
    )
    tiles = jnp.concatenate([back[:, k * lanes : (k + 1) * lanes] for k in range(groups)], axis=0).T
    kept = 2 * places
    moved = jnp.concatenate(
        [tiles[i * kept : (i + 1) * kept] for i in range(packed // lanes)], axis=1
    )
    for a in range(2):
        for b in range(rows):
            first = (a * rows + b) * cols
            new_currents[a, b] = currents[a, b] - moved[first : first + cols]
    pattern = jnp.concatenate(
        [rows_of(8 + i) + rows_of(8 + 2 * share + i) for i in range(2 * share)], axis=0
    )
    far[...] = pattern.T


def beam_kernel(
    counts, beams, amplitude, scale, given, library, dirs, beam_dir, out,
    blocks_wide, blocks_tall, off, sub_re, sub_im, chosen, gathered, phased, pattern, image, work,
):
    row_count, col_count = counts
    ranks = row_count * col_count
    values, elems, _ = library.shape
    side = math.isqrt(elems)
    share = beams // ranks
    subs = chosen.shape[1]
    places = subs // ranks
    place_cols = 2
    place_rows = places // place_cols
    total = dirs.shape[1]
    chunks = total // chunk
    field_rows = share * subs
    me = lax.axis_index("row") * col_count + lax.axis_index("col")
    real_lane = iota((1, lanes), 1) < elems

    for v in range(values):
        block = library[v].astype(jnp.float32)
        upper = jnp.where(real_lane, block, -block).astype(jnp.bfloat16)
        lower = jnp.concatenate([block[:, elems:], block[:, :elems]], axis=1).astype(jnp.bfloat16)
        both = jnp.concatenate([upper, lower], axis=0)
        blocks_tall[v * lanes : (v + 1) * lanes, :] = both
        blocks_wide[:, v * lanes : (v + 1) * lanes] = both

    s = iota((subs, 1), 0)
    place, rank = s // ranks, s % ranks
    sub_row = (rank // col_count) * place_rows + place // place_cols
    sub_col = (rank % col_count) * place_cols + place % place_cols
    x_sub = (sub_col * side).astype(jnp.float32) - (col_count * place_cols * side - 1) / 2.0
    y_sub = (sub_row * side).astype(jnp.float32) - (row_count * place_rows * side - 1) / 2.0
    e = iota((elems, 1), 0)
    x_off = (e % side).astype(jnp.float32)
    y_off = (e // side).astype(jnp.float32)
    for i in range(chunks):
        cut = slice(i * chunk, (i + 1) * chunk)
        u, v = dirs[0:1, cut], dirs[1:2, cut]
        cosine, sine = turn(u * x_sub + v * y_sub)
        sub_re[:, cut] = cosine
        sub_im[:, cut] = -sine
        cosine, sine = turn(u * x_off + v * y_off)
        both = jnp.concatenate([cosine, -sine], axis=0)
        high = both.astype(jnp.bfloat16)
        off[0:lanes, cut] = high
        off[lanes : 2 * lanes, cut] = (both - high.astype(jnp.float32)).astype(jnp.bfloat16)

    def received(first):
        return given[pl.ds(first, ranks, stride=16), :]

    field = jnp.concatenate([received(i) for i in range(share * places)], axis=0)
    ids = jnp.concatenate([received(8 + p) for p in range(places)], axis=0).astype(jnp.int32)

    code = sub_row * 64 + sub_col
    t = iota((1, subs), 1)
    t_place, t_rank = t // ranks, t % ranks
    t_row = (t_rank // col_count) * place_rows + t_place // place_cols
    t_col = (t_rank % col_count) * place_cols + t_place % place_cols
    gap = t_row * 64 + t_col - code
    pair = jnp.full((subs, subs), -1, jnp.int32)
    for row_off in range(5):
        for col_off in range(5):
            slot = 5 * row_off + col_off
            pair = jnp.where(
                gap == (row_off - 2) * 64 + (col_off - 2), ids[:, slot : slot + 1], pair
            )
    pair_adjoint = pair.astype(jnp.float32).T.astype(jnp.int32)

    def choose(table):
        for v in range(values):
            chosen[v * subs : (v + 1) * subs, :] = (
                (table == v).astype(jnp.float32).astype(jnp.bfloat16)
            )

    def gather(x):
        xb = x.astype(jnp.bfloat16)
        beside = jnp.concatenate([xb[i * subs : (i + 1) * subs] for i in range(share)], axis=1)
        sums = jnp.dot(chosen[...], beside, preferred_element_type=jnp.float32)
        sums = sums.astype(jnp.bfloat16)
        for v in range(values):
            for i in range(share):
                gathered[i * subs : (i + 1) * subs, v * lanes : (v + 1) * lanes] = sums[
                    v * subs : (v + 1) * subs, i * lanes : (i + 1) * lanes
                ]

    def couple(x):
        choose(pair)
        gather(x)
        return lax.dot_general(
            gathered[...],
            blocks_wide[...],
            (((1,), (1,)), ((), ())),
            preferred_element_type=jnp.float32,
        )

    def couple_adj(x):
        choose(pair_adjoint)
        gather(x)
        return jnp.dot(gathered[...], blocks_tall[...], preferred_element_type=jnp.float32)

    def swap(x):
        return jnp.concatenate([x[:, elems:], x[:, :elems]], axis=1)

    def project(x, result):
        total_field = x + couple(x)
        real = jnp.where(real_lane, total_field, -total_field)
        both = jnp.concatenate([real, swap(total_field)], axis=0).astype(jnp.bfloat16)
        both = jnp.concatenate([both, both], axis=1)
        for i in range(chunks):
            cut = slice(i * chunk, (i + 1) * chunk)
            part = jnp.dot(both, off[:, cut], preferred_element_type=jnp.float32)
            s_re, s_im = sub_re[:, cut], sub_im[:, cut]
            for bl in range(share):
                p_re = part[bl * subs : (bl + 1) * subs]
                p_im = part[field_rows + bl * subs : field_rows + (bl + 1) * subs]
                result[bl : bl + 1, cut] = scale * jnp.sum(
                    s_re * p_re - s_im * p_im, axis=0, keepdims=True
                )
                result[share + bl : share + bl + 1, cut] = scale * jnp.sum(
                    s_re * p_im + s_im * p_re, axis=0, keepdims=True
                )

    project(field, pattern)

    d = iota((1, total), 1)
    target = jnp.concatenate(
        [jnp.where(d == beam_dir[bl * ranks + me], amplitude, 0.0) for bl in range(share)], axis=0
    )
    residual = pattern[...] - jnp.concatenate([target, jnp.zeros_like(target)], axis=0)
    rounded = residual.astype(jnp.bfloat16).astype(jnp.float32)
    for i in range(chunks):
        cut = slice(i * chunk, (i + 1) * chunk)
        s_re, s_im = sub_re[:, cut], sub_im[:, cut]
        for bl in range(share):
            r_re = rounded[bl : bl + 1, cut]
            r_im = rounded[share + bl : share + bl + 1, cut]
            phased[bl * subs : (bl + 1) * subs, cut] = (s_re * r_re + s_im * r_im).astype(
                jnp.bfloat16
            )
            phased[field_rows + bl * subs : field_rows + (bl + 1) * subs, cut] = (
                s_re * r_im - s_im * r_re
            ).astype(jnp.bfloat16)
    sums = lax.dot_general(
        phased[...], off[...], (((1,), (1,)), ((), ())), preferred_element_type=jnp.float32
    )
    sums = sums[:, :lanes] + sums[:, lanes:]
    upper, lower = sums[:field_rows], sums[field_rows:]
    back = scale * (jnp.where(real_lane, upper, -upper) + swap(lower))
    gradient = back + couple_adj(back)
    project(gradient, image)

    products = jnp.sum(image[...] * residual, axis=1, keepdims=True)
    squares = jnp.sum(image[...] * image[...], axis=1, keepdims=True)
    step = (products[:share] + products[share:]) / (squares[:share] + squares[share:] + 1e-06)
    for bl in range(share):
        for p in range(places):
            first = bl * subs + p * ranks
            work[pl.ds(bl * places + p, ranks, stride=16), :] = (
                gradient[first : first + ranks] * step[bl : bl + 1]
            )
    final = pattern[...] - image[...] * jnp.concatenate([step, step], axis=0)
    high = final.astype(jnp.bfloat16).astype(jnp.float32)
    both = jnp.concatenate([high, final - high], axis=0)
    piece = total // ranks
    for m in range(ranks):
        work[m * 16 + 8 : m * 16 + 16, :] = both[:, m * piece : (m + 1) * piece]
    out[...] = work[...].astype(jnp.bfloat16)


def by_beams(currents, library, block_ids, dirs, beam_dir):
    beams = beam_dir.shape[0]
    _, rows_here, cols_here, _ = currents.shape
    values, elems, _ = library.shape
    counts = (lax.axis_size("row"), lax.axis_size("col"))
    ranks = counts[0] * counts[1]
    share = beams // ranks
    subs = ranks * rows_here * cols_here
    all_elems = subs * elems
    total = dirs.shape[1]
    f32, bf16 = jnp.float32, jnp.bfloat16
    params = pltpu.CompilerParams(vmem_limit_bytes=40 * 2**20)

    def exchange(x):
        cut = x.reshape(ranks, 16, lanes)
        return lax.all_to_all(cut, ("row", "col"), 0, 0, tiled=False).reshape(x.shape)

    sent = pl.pallas_call(
        functools.partial(split_kernel, ranks, beams, elems),
        out_shape=jax.ShapeDtypeStruct((16 * ranks, lanes), f32),
        compiler_params=params,
    )(currents, block_ids)
    vmem = pl.BlockSpec(memory_space=pltpu.VMEM)
    results = pl.pallas_call(
        functools.partial(
            beam_kernel,
            counts,
            beams,
            math.sqrt(all_elems) / 16.0,
            1.0 / math.sqrt(all_elems),
        ),
        in_specs=[vmem, vmem, vmem, pl.BlockSpec(memory_space=pltpu.SMEM)],
        out_shape=jax.ShapeDtypeStruct((16 * ranks, lanes), bf16),
        scratch_shapes=[
            pltpu.VMEM((lanes, values * lanes), bf16),
            pltpu.VMEM((values * lanes, lanes), bf16),
            pltpu.VMEM((2 * lanes, total), bf16),
            pltpu.VMEM((subs, total), f32),
            pltpu.VMEM((subs, total), f32),
            pltpu.VMEM((values * subs, subs), bf16),
            pltpu.VMEM((share * subs, values * lanes), bf16),
            pltpu.VMEM((2 * share * subs, total), bf16),
            pltpu.VMEM((2 * share, total), f32),
            pltpu.VMEM((2 * share, total), f32),
            pltpu.VMEM((16 * ranks, lanes), f32),
        ],
        compiler_params=params,
    )(exchange(sent), library, dirs, beam_dir)
    return pl.pallas_call(
        functools.partial(join_kernel, ranks, beams, elems),
        out_shape=(
            jax.ShapeDtypeStruct(currents.shape, f32),
            jax.ShapeDtypeStruct((total // ranks, 2 * beams), f32),
        ),
        scratch_shapes=[pltpu.VMEM((16 * ranks, lanes), f32)],
        compiler_params=params,
    )(currents, exchange(results))


def local(currents, library, block_ids, dirs, beam_dir):
    beams = beam_dir.shape[0]
    _, rows_here, cols_here, packed = currents.shape
    elems = library.shape[1]
    ranks = lax.axis_size(("row", "col"))
    fits = (
        beams == 2 * ranks
        and (rows_here, cols_here) == (2, 2)
        and 2 * elems == lanes
        and 2 * packed * rows_here * cols_here == lanes * lanes
        and dirs.shape[1] == ranks * lanes
    )
    plan = by_beams if fits else by_elements
    return plan(currents, library, block_ids, dirs, beam_dir)


def solution(mesh):
    return jax.shard_map(
        local,
        mesh=mesh,
        in_specs=(
            P(None, ("groups", "row"), "col", None),
            P(),
            P(("groups", "row"), "col", None),
            P(),
            P("groups"),
        ),
        out_specs=(P(None, ("groups", "row"), "col", None), P(("groups", "row", "col"), None)),
        check_vma=False,
    )
```

```python
import functools
import math

import jax
import jax.numpy as jnp
from jax import lax
from jax.experimental import pallas as pl
from jax.experimental.pallas import tpu as pltpu
from jax.sharding import PartitionSpec as P

pi_value = 3.141592653589793
dir_block = 512


def with_halo(cells, sides, width):
    for axis, dim in sides:
        count = lax.axis_size(axis)
        ends = count - 1
        head = lax.slice_in_dim(cells, 0, width, axis=dim)
        tail = lax.slice_in_dim(cells, cells.shape[dim] - width, cells.shape[dim], axis=dim)
        cells = jnp.concatenate(
            [
                lax.ppermute(tail, axis, [(i, (i + 1) % count) for i in range(ends)]),
                cells,
                lax.ppermute(head, axis, [((i + 1) % count, i) for i in range(ends)]),
            ],
            axis=dim,
        )
    return cells


def phases(dir_rows, sub_pos, elem_pos):
    sub_angle = pi_value * (
        dir_rows[0][:, None] * sub_pos[0][None, :] + dir_rows[1][:, None] * sub_pos[1][None, :]
    )
    elem_angle = pi_value * (
        dir_rows[0][:, None] * elem_pos[0][None, :] + dir_rows[1][:, None] * elem_pos[1][None, :]
    )
    sub_cos = jnp.cos(sub_angle)[:, :, None]
    sub_sin = jnp.sin(sub_angle)[:, :, None]
    elem_cos = jnp.cos(elem_angle)[:, None, :]
    elem_sin = jnp.sin(elem_angle)[:, None, :]
    cosine = sub_cos * elem_cos - sub_sin * elem_sin
    sine = sub_sin * elem_cos + sub_cos * elem_sin
    count = dir_rows.shape[1]
    return (
        cosine.reshape(count, -1).astype(jnp.bfloat16),
        (-sine).reshape(count, -1).astype(jnp.bfloat16),
    )


def coupling(padded, id_table, library, adjoint):
    rows_here = padded.shape[1] - 4
    cols_here = padded.shape[2] - 4
    elems = library.shape[1]
    field_view = padded.reshape(2, rows_here + 4, cols_here + 4, elems, -1)
    spec = "rcnji,rcnjb->rcib" if adjoint else "rcnij,rcnjb->rcib"
    out_re = jnp.zeros((rows_here, cols_here, elems, field_view.shape[4]), jnp.float32)
    out_im = jnp.zeros_like(out_re)
    for row_off in range(5):
        sources = []
        chosen = []
        for col_off in range(5):
            slot_index = 5 * row_off + col_off
            if adjoint:
                row_start = 4 - row_off
                col_start = 4 - col_off
                chosen.append(
                    id_table[
                        row_start : row_start + rows_here,
                        col_start : col_start + cols_here,
                        slot_index,
                    ]
                )
            else:
                row_start = row_off
                col_start = col_off
                chosen.append(id_table[:, :, slot_index])
            sources.append(
                field_view[:, row_start : row_start + rows_here, col_start : col_start + cols_here]
            )
        source_stack = jnp.stack(sources, axis=3)
        block_stack = library[jnp.stack(chosen, axis=2)]
        block_re = block_stack[..., :elems]
        block_im = block_stack[..., elems:]
        real_real = jnp.einsum(spec, block_re, source_stack[0], preferred_element_type=jnp.float32)
        real_imag = jnp.einsum(spec, block_re, source_stack[1], preferred_element_type=jnp.float32)
        imag_real = jnp.einsum(spec, block_im, source_stack[0], preferred_element_type=jnp.float32)
        imag_imag = jnp.einsum(spec, block_im, source_stack[1], preferred_element_type=jnp.float32)
        if adjoint:
            out_re = out_re + real_real + imag_imag
            out_im = out_im + real_imag - imag_real
        else:
            out_re = out_re + real_real - imag_imag
            out_im = out_im + real_imag + imag_real
    return jnp.stack([out_re, out_im])


def pattern_term(radiated_cols, dirs, sub_pos, elem_pos, row_count, scale):
    half_cols = radiated_cols.shape[1] // 2

    def one_block(begin_row, block_size):
        dir_rows = lax.dynamic_slice_in_dim(dirs, begin_row, block_size, 1)
        cosine, sine = phases(dir_rows, sub_pos, elem_pos)
        cos_part = jnp.dot(cosine, radiated_cols, preferred_element_type=jnp.float32)
        sin_part = jnp.dot(sine, radiated_cols, preferred_element_type=jnp.float32)
        return jnp.concatenate(
            [
                cos_part[:, :half_cols] - sin_part[:, half_cols:],
                cos_part[:, half_cols:] + sin_part[:, :half_cols],
            ],
            axis=1,
        )

    block_count = row_count // dir_block
    starts = jnp.arange(block_count, dtype=jnp.int32) * dir_block
    stacked = lax.map(lambda begin_row: one_block(begin_row, dir_block), starts)
    pieces = stacked.reshape(block_count * dir_block, 2 * half_cols)
    return pieces * scale


def adjoint_piece(carry, residual_rows, dirs, sub_pos, elem_pos):
    row_count = residual_rows.shape[0]
    dims_spec = (((0,), (0,)), ((), ()))

    def add_block(totals, local_start, block_size):
        piece_rows = lax.dynamic_slice_in_dim(residual_rows, local_start, block_size, 0)
        dir_rows = lax.dynamic_slice_in_dim(dirs, local_start, block_size, 1)
        cosine, sine = phases(dir_rows, sub_pos, elem_pos)
        cos_part = lax.dot_general(
            cosine, piece_rows, dims_spec, preferred_element_type=jnp.float32
        )
        sin_part = lax.dot_general(sine, piece_rows, dims_spec, preferred_element_type=jnp.float32)
        return (totals[0] + cos_part, totals[1] + sin_part)

    block_count = row_count // dir_block
    carry = lax.fori_loop(
        0,
        block_count,
        lambda number, totals: add_block(totals, number * dir_block, dir_block),
        carry,
    )
    return carry


def line_terms(image_pattern, residual, beams):
    products = jnp.sum(image_pattern * residual, axis=0)
    squares = jnp.sum(image_pattern * image_pattern, axis=0)
    return (products[:beams] + products[beams:], squares[:beams] + squares[beams:])


def by_elements(currents, library, block_ids, dirs, beam_dir):
    beams = beam_dir.shape[0]
    rows_here = currents.shape[1]
    cols_here = currents.shape[2]
    packed = currents.shape[3]
    elems = library.shape[1]
    side = math.isqrt(elems)
    local_elems = rows_here * cols_here * elems
    total_rows = rows_here * lax.axis_size("row")
    total_cols = cols_here * lax.axis_size("col")
    all_elems = total_rows * total_cols * elems
    scale = 1.0 / math.sqrt(all_elems)
    amplitude = math.sqrt(all_elems) / 16.0
    dir_total = dirs.shape[1]
    share_rows = dir_total // lax.axis_size(("row", "col"))
    row_ids = (lax.axis_index("row") * rows_here + jnp.arange(rows_here, dtype=jnp.int32))[:, None]
    col_ids = (lax.axis_index("col") * cols_here + jnp.arange(cols_here, dtype=jnp.int32))[None, :]
    sub_x = (col_ids * side + 0 * row_ids).reshape(-1).astype(jnp.float32) - (
        total_cols * side - 1
    ) / 2.0
    sub_y = (row_ids * side + 0 * col_ids).reshape(-1).astype(jnp.float32) - (
        total_rows * side - 1
    ) / 2.0
    elem_ids = jnp.arange(elems, dtype=jnp.int32)
    sub_pos = (sub_x, sub_y)
    elem_pos = ((elem_ids % side).astype(jnp.float32), (elem_ids // side).astype(jnp.float32))
    padded_ids = with_halo(block_ids, (("row", 0), ("col", 1)), 2)

    def radiate(current_field):
        rounded = current_field.astype(jnp.bfloat16)
        padded = with_halo(rounded, (("row", 1), ("col", 2)), 2)
        coupled = coupling(padded, block_ids, library, False)
        total_field = (current_field.reshape(coupled.shape) + coupled).astype(jnp.bfloat16)
        return jnp.concatenate(
            [
                total_field[0].reshape(local_elems, beams),
                total_field[1].reshape(local_elems, beams),
            ],
            axis=1,
        )

    zero_acc = jnp.zeros((local_elems, 2 * beams), jnp.float32)

    def share_pattern(current_field):
        radiated_cols = radiate(current_field)
        return lax.psum_scatter(
            pattern_term(
                radiated_cols,
                dirs,
                sub_pos,
                elem_pos,
                share_rows * lax.axis_size(("row", "col")),
                scale,
            ),
            ("row", "col"),
            scatter_dimension=0,
            tiled=True,
        )

    share = share_pattern(currents)
    dir_ids = lax.axis_index(("row", "col")) * share_rows + jnp.arange(share_rows, dtype=jnp.int32)
    real_part = amplitude * (dir_ids[:, None] == beam_dir[None, :]).astype(jnp.float32)
    target = jnp.concatenate([real_part, jnp.zeros_like(real_part)], axis=1)
    residual = share - target
    totals = adjoint_piece(
        (zero_acc, zero_acc),
        lax.all_gather(residual.astype(jnp.bfloat16), ("row", "col"), axis=0, tiled=True),
        dirs,
        sub_pos,
        elem_pos,
    )
    p_part, q_part = totals
    grad_re = (p_part[:, :beams] + q_part[:, beams:]) * scale
    grad_im = (p_part[:, beams:] - q_part[:, :beams]) * scale
    raw_gradient = jnp.stack(
        [
            grad_re.reshape(rows_here, cols_here, packed),
            grad_im.reshape(rows_here, cols_here, packed),
        ]
    )
    rounded = raw_gradient.astype(jnp.bfloat16)
    padded = with_halo(rounded, (("row", 1), ("col", 2)), 2)
    gradient = raw_gradient + coupling(padded, padded_ids, library, True).reshape(
        raw_gradient.shape
    )
    image_pattern = share_pattern(gradient)
    part_num, part_den = line_terms(image_pattern, residual, beams)
    numerator, denominator = lax.psum((part_num, part_den), ("row", "col"))
    step_size = numerator / (denominator + 1e-06)
    moved = gradient.reshape(2, rows_here, cols_here, elems, beams) * step_size
    currents = currents - moved.reshape(currents.shape)
    share = share - image_pattern * jnp.concatenate([step_size, step_size])
    return (currents, share)


lanes = 128
chunk = 256
sin_fit = (3.141592580044754, -5.167706878916943, 2.5500313770294833, -0.5980451722529145, 0.07722012475690251)
cos_fit = (0.9999999535196061, -4.934792861473954, 4.058411954029988, -1.3318803713197287, 0.21969716737372766)


def iota(shape, dim):
    return lax.broadcasted_iota(jnp.int32, shape, dim)


def turn(angle):
    whole = jnp.round(angle)
    rest = angle - whole
    half = 0.5 * whole
    sign = 1.0 - 4.0 * (half - jnp.floor(half))
    square = rest * rest
    sine = sin_fit[4]
    cosine = cos_fit[4]
    for k in (3, 2, 1, 0):
        sine = sine * square + sin_fit[k]
        cosine = cosine * square + cos_fit[k]
    return cosine * sign, sine * rest * sign


def shuffle(elems, places):
    size = 2 * elems * places
    row = iota((size, 1), 0)
    kept = 2 * places
    groups = size // lanes
    k = row // lanes
    q = (row % lanes) // kept
    half = (row % kept) // places
    p = row % places
    goal = p * (2 * elems) + half * elems + q * groups + k
    return (goal == iota((size, size), 1)).astype(jnp.float32).astype(jnp.bfloat16)


def split_kernel(ranks, beams, elems, currents_far, ids_far, out, currents, ids, arrived):
    copies = [
        pltpu.make_async_copy(source, goal, arrived.at[i])
        for i, (source, goal) in enumerate(((currents_far, currents), (ids_far, ids)))
    ]
    for copy in copies:
        copy.start()
    _, rows, cols, packed = currents.shape
    places = rows * cols
    groups = lanes // beams
    order = shuffle(elems, places)
    for copy in copies:
        copy.wait()
    field = jnp.concatenate([currents[a, b] for a in range(2) for b in range(rows)], axis=0)
    tiles = jnp.concatenate(
        [field[:, i * lanes : (i + 1) * lanes] for i in range(packed // lanes)], axis=0
    ).T
    high = tiles.astype(jnp.bfloat16)
    low = (tiles - high.astype(jnp.float32)).astype(jnp.bfloat16)
    stacked = jnp.concatenate(
        [
            jnp.concatenate([part[k * beams : (k + 1) * beams] for k in range(groups)], axis=1)
            for part in (high, low)
        ],
        axis=0,
    )
    moved = jnp.dot(stacked, order, preferred_element_type=jnp.float32)
    moved = moved[:beams] + moved[beams:]
    for bl in range(beams // ranks):
        for p in range(places):
            out[pl.ds(bl * places + p, ranks, stride=16), :] = moved[
                bl * ranks : (bl + 1) * ranks, p * lanes : (p + 1) * lanes
            ]
    slots = ids.shape[2]
    table = jnp.concatenate([ids[a] for a in range(rows)], axis=0).astype(jnp.float32)
    table = jnp.concatenate([table, jnp.zeros((places, lanes - slots), jnp.float32)], axis=1)
    table = jnp.concatenate([table, jnp.zeros_like(table)], axis=0)
    for m in range(ranks):
        out[m * 16 + 8 : m * 16 + 16, :] = table


def join_kernel(ranks, beams, elems, currents, moved_in, new_currents, far, work):
    _, rows, cols, packed = currents.shape
    places = rows * cols
    groups = lanes // beams
    share = beams // ranks
    work[...] = moved_in[...].astype(jnp.float32)

    def rows_of(first):
        return work[pl.ds(first, ranks, stride=16), :]

    stacked = jnp.concatenate(
        [
            jnp.concatenate([rows_of(bl * places + p) for p in range(places)], axis=1)
            for bl in range(share)
        ],
        axis=0,
    ).astype(jnp.bfloat16)
    back = lax.dot_general(
        stacked,
        shuffle(elems, places),
        (((1,), (1,)), ((), ())),
        preferred_element_type=jnp.float32,
    )
    tiles = jnp.concatenate([back[:, k * lanes : (k + 1) * lanes] for k in range(groups)], axis=0).T
    kept = 2 * places
    moved = jnp.concatenate(
        [tiles[i * kept : (i + 1) * kept] for i in range(packed // lanes)], axis=1
    )
    for a in range(2):
        for b in range(rows):
            first = (a * rows + b) * cols
            new_currents[a, b] = currents[a, b] - moved[first : first + cols]
    pattern = jnp.concatenate(
        [rows_of(8 + i) + rows_of(8 + 2 * share + i) for i in range(2 * share)], axis=0
    )
    far[...] = pattern


def beam_kernel(
    counts, beams, amplitude, scale, given, library_far, dirs_far, beam_dir_far, out,
    library, dirs, beam_dir, arrived, blocks_wide, blocks_tall, off, sub_re, sub_im, chosen, chosen_adj, gathered, phased, pattern, residual, image, work,
):
    row_count, col_count = counts
    ranks = row_count * col_count
    copies = [
        pltpu.make_async_copy(source, goal, arrived.at[i])
        for i, (source, goal) in enumerate(
            ((dirs_far, dirs), (library_far, library), (beam_dir_far, beam_dir))
        )
    ]
    for copy in copies:
        copy.start()
    values, elems, _ = library.shape
    side = math.isqrt(elems)
    share = beams // ranks
    subs = chosen.shape[1]
    places = subs // ranks
    place_cols = 2
    place_rows = places // place_cols
    total = dirs.shape[1]
    chunks = total // chunk
    field_rows = share * subs
    me = lax.axis_index("row") * col_count + lax.axis_index("col")
    real_lane = iota((1, lanes), 1) < elems

    s = iota((subs, 1), 0)
    place, rank = s // ranks, s % ranks
    sub_row = (rank // col_count) * place_rows + place // place_cols
    sub_col = (rank % col_count) * place_cols + place % place_cols
    def received(first):
        return given[pl.ds(first, ranks, stride=16), :]

    field = jnp.concatenate([received(i) for i in range(share * places)], axis=0)
    ids = jnp.concatenate([received(8 + p) for p in range(places)], axis=0).astype(jnp.int32)

    code = sub_row * 64 + sub_col
    t = iota((1, subs), 1)
    t_place, t_rank = t // ranks, t % ranks
    t_row = (t_rank // col_count) * place_rows + t_place // place_cols
    t_col = (t_rank % col_count) * place_cols + t_place % place_cols
    gap = t_row * 64 + t_col - code
    pair = jnp.full((subs, subs), -1, jnp.int32)
    for row_off in range(5):
        for col_off in range(5):
            slot = 5 * row_off + col_off
            pair = jnp.where(
                gap == (row_off - 2) * 64 + (col_off - 2), ids[:, slot : slot + 1], pair
            )
    pair_adjoint = pair.astype(jnp.float32).T.astype(jnp.int32)

    def choose(goal, table):
        for v in range(values):
            goal[v * subs : (v + 1) * subs, :] = (
                (table == v).astype(jnp.float32).astype(jnp.bfloat16)
            )

    def gather(source, x):
        xb = x.astype(jnp.bfloat16)
        beside = jnp.concatenate([xb[i * subs : (i + 1) * subs] for i in range(share)], axis=1)
        sums = jnp.dot(source[...], beside, preferred_element_type=jnp.float32)
        sums = sums.astype(jnp.bfloat16)
        for v in range(values):
            for i in range(share):
                gathered[i * subs : (i + 1) * subs, v * lanes : (v + 1) * lanes] = sums[
                    v * subs : (v + 1) * subs, i * lanes : (i + 1) * lanes
                ]

    choose(chosen, pair)
    gather(chosen, field)
    choose(chosen_adj, pair_adjoint)

    x_sub = (sub_col * side).astype(jnp.float32) - (col_count * place_cols * side - 1) / 2.0
    y_sub = (sub_row * side).astype(jnp.float32) - (row_count * place_rows * side - 1) / 2.0
    e = iota((elems, 1), 0)
    x_off = (e % side).astype(jnp.float32)
    y_off = (e // side).astype(jnp.float32)
    copies[0].wait()
    for i in range(chunks):
        cut = slice(i * chunk, (i + 1) * chunk)
        u, v = dirs[0:1, cut], dirs[1:2, cut]
        cosine, sine = turn(u * x_sub + v * y_sub)
        sub_re[:, cut] = cosine
        sub_im[:, cut] = -sine
        cosine, sine = turn(u * x_off + v * y_off)
        both = jnp.concatenate([cosine, -sine], axis=0)
        high = both.astype(jnp.bfloat16)
        off[0:lanes, cut] = high
        off[lanes : 2 * lanes, cut] = (both - high.astype(jnp.float32)).astype(jnp.bfloat16)

    copies[1].wait()
    copies[2].wait()
    for v in range(values):
        block = library[v].astype(jnp.float32)
        upper = jnp.where(real_lane, block, -block).astype(jnp.bfloat16)
        lower = jnp.concatenate([block[:, elems:], block[:, :elems]], axis=1).astype(jnp.bfloat16)
        both = jnp.concatenate([upper, lower], axis=0)
        blocks_tall[v * lanes : (v + 1) * lanes, :] = both
        blocks_wide[:, v * lanes : (v + 1) * lanes] = both

    def couple():
        return lax.dot_general(
            gathered[...],
            blocks_wide[...],
            (((1,), (1,)), ((), ())),
            preferred_element_type=jnp.float32,
        )

    def couple_adj():
        return jnp.dot(gathered[...], blocks_tall[...], preferred_element_type=jnp.float32)

    def swap(x):
        return jnp.concatenate([x[:, elems:], x[:, :elems]], axis=1)

    def radiate(x):
        total_field = x + couple()
        real = jnp.where(real_lane, total_field, -total_field)
        both = jnp.concatenate([real, swap(total_field)], axis=0).astype(jnp.bfloat16)
        return jnp.concatenate([both, both], axis=1)

    def project(radiated, cut):
        part = jnp.dot(radiated, off[:, cut], preferred_element_type=jnp.float32)
        s_re, s_im = sub_re[:, cut], sub_im[:, cut]
        re, im = [], []
        for bl in range(share):
            p_re = part[bl * subs : (bl + 1) * subs]
            p_im = part[field_rows + bl * subs : field_rows + (bl + 1) * subs]
            re.append(jnp.sum(s_re * p_re - s_im * p_im, axis=0, keepdims=True))
            im.append(jnp.sum(s_re * p_im + s_im * p_re, axis=0, keepdims=True))
        return scale * jnp.concatenate(re + im, axis=0)

    radiated = radiate(field)
    beam = iota((2 * share, 1), 0)
    place = jnp.full((2 * share, 1), -1, jnp.int32)
    for bl in range(share):
        place = jnp.where(beam == bl, beam_dir[bl * ranks + me], place)
    for i in range(chunks):
        cut = slice(i * chunk, (i + 1) * chunk)
        found = project(radiated, cut)
        pattern[:, cut] = found
        rest = found - jnp.where(iota((1, chunk), 1) + i * chunk == place, amplitude, 0.0)
        residual[:, cut] = rest
        rounded = rest.astype(jnp.bfloat16).astype(jnp.float32)
        s_re, s_im = sub_re[:, cut], sub_im[:, cut]
        for bl in range(share):
            r_re = rounded[bl : bl + 1]
            r_im = rounded[share + bl : share + bl + 1]
            phased[bl * subs : (bl + 1) * subs, cut] = (s_re * r_re + s_im * r_im).astype(
                jnp.bfloat16
            )
            phased[field_rows + bl * subs : field_rows + (bl + 1) * subs, cut] = (
                s_re * r_im - s_im * r_re
            ).astype(jnp.bfloat16)
    sums = lax.dot_general(
        phased[...], off[...], (((1,), (1,)), ((), ())), preferred_element_type=jnp.float32
    )
    sums = sums[:, :lanes] + sums[:, lanes:]
    upper, lower = sums[:field_rows], sums[field_rows:]
    back = scale * (jnp.where(real_lane, upper, -upper) + swap(lower))
    gather(chosen_adj, back)
    gradient = back + couple_adj()
    gather(chosen, gradient)
    radiated = radiate(gradient)
    products = jnp.zeros((2 * share, chunk), jnp.float32)
    squares = jnp.zeros((2 * share, chunk), jnp.float32)
    for i in range(chunks):
        cut = slice(i * chunk, (i + 1) * chunk)
        found = project(radiated, cut)
        image[:, cut] = found
        products = products + found * residual[:, cut]
        squares = squares + found * found
    products = jnp.sum(products, axis=1, keepdims=True)
    squares = jnp.sum(squares, axis=1, keepdims=True)
    step = (products[:share] + products[share:]) / (squares[:share] + squares[share:] + 1e-06)
    for bl in range(share):
        for p in range(places):
            first = bl * subs + p * ranks
            work[pl.ds(bl * places + p, ranks, stride=16), :] = (
                gradient[first : first + ranks] * step[bl : bl + 1]
            )
    final = pattern[...] - image[...] * jnp.concatenate([step, step], axis=0)
    high = final.astype(jnp.bfloat16).astype(jnp.float32)
    both = jnp.concatenate([high, final - high], axis=0)
    piece = total // ranks
    for m in range(ranks):
        work[m * 16 + 8 : m * 16 + 16, :] = both[:, m * piece : (m + 1) * piece]
    out[...] = work[...].astype(jnp.bfloat16)


def by_beams(currents, library, block_ids, dirs, beam_dir):
    beams = beam_dir.shape[0]
    _, rows_here, cols_here, _ = currents.shape
    values, elems, _ = library.shape
    counts = (lax.axis_size("row"), lax.axis_size("col"))
    ranks = counts[0] * counts[1]
    share = beams // ranks
    subs = ranks * rows_here * cols_here
    all_elems = subs * elems
    total = dirs.shape[1]
    f32, bf16 = jnp.float32, jnp.bfloat16
    params = pltpu.CompilerParams(vmem_limit_bytes=40 * 2**20)

    anywhere = pl.BlockSpec(memory_space=pltpu.HBM)

    def keep(x):
        return pltpu.with_memory_space_constraint(x, pltpu.HBM)

    def exchange(x):
        cut = x.reshape(ranks, 16, lanes)
        return lax.all_to_all(cut, ("row", "col"), 0, 0, tiled=False).reshape(x.shape)

    sent = pl.pallas_call(
        functools.partial(split_kernel, ranks, beams, elems),
        in_specs=[anywhere, anywhere],
        out_shape=jax.ShapeDtypeStruct((16 * ranks, lanes), f32),
        scratch_shapes=[
            pltpu.VMEM(currents.shape, f32),
            pltpu.VMEM(block_ids.shape, jnp.int32),
            pltpu.SemaphoreType.DMA((2,)),
        ],
        compiler_params=params,
    )(keep(currents), keep(block_ids))
    vmem = pl.BlockSpec(memory_space=pltpu.VMEM)
    results = pl.pallas_call(
        functools.partial(
            beam_kernel,
            counts,
            beams,
            math.sqrt(all_elems) / 16.0,
            1.0 / math.sqrt(all_elems),
        ),
        in_specs=[vmem, anywhere, anywhere, anywhere],
        out_shape=jax.ShapeDtypeStruct((16 * ranks, lanes), bf16),
        scratch_shapes=[
            pltpu.VMEM(library.shape, bf16),
            pltpu.VMEM(dirs.shape, f32),
            pltpu.SMEM(beam_dir.shape, jnp.int32),
            pltpu.SemaphoreType.DMA((3,)),
            pltpu.VMEM((lanes, values * lanes), bf16),
            pltpu.VMEM((values * lanes, lanes), bf16),
            pltpu.VMEM((2 * lanes, total), bf16),
            pltpu.VMEM((subs, total), f32),
            pltpu.VMEM((subs, total), f32),
            pltpu.VMEM((values * subs, subs), bf16),
            pltpu.VMEM((values * subs, subs), bf16),
            pltpu.VMEM((share * subs, values * lanes), bf16),
            pltpu.VMEM((2 * share * subs, total), bf16),
            pltpu.VMEM((2 * share, total), f32),
            pltpu.VMEM((2 * share, total), f32),
            pltpu.VMEM((2 * share, total), f32),
            pltpu.VMEM((16 * ranks, lanes), f32),
        ],
        compiler_params=params,
    )(exchange(sent), keep(library), keep(dirs), keep(beam_dir))
    new_currents, far = pl.pallas_call(
        functools.partial(join_kernel, ranks, beams, elems),
        out_shape=(
            jax.ShapeDtypeStruct(currents.shape, f32),
            jax.ShapeDtypeStruct((2 * beams, total // ranks), f32),
        ),
        scratch_shapes=[pltpu.VMEM((16 * ranks, lanes), f32)],
        compiler_params=params,
    )(currents, exchange(results))
    return new_currents, far.T


def local(currents, library, block_ids, dirs, beam_dir):
    beams = beam_dir.shape[0]
    _, rows_here, cols_here, packed = currents.shape
    elems = library.shape[1]
    ranks = lax.axis_size(("row", "col"))
    fits = (
        beams == 2 * ranks
        and (rows_here, cols_here) == (2, 2)
        and 2 * elems == lanes
        and 2 * packed * rows_here * cols_here == lanes * lanes
        and dirs.shape[1] == ranks * lanes
    )
    plan = by_beams if fits else by_elements
    return plan(currents, library, block_ids, dirs, beam_dir)


def solution(mesh):
    return jax.shard_map(
        local,
        mesh=mesh,
        in_specs=(
            P(None, ("groups", "row"), "col", None),
            P(),
            P(("groups", "row"), "col", None),
            P(),
            P("groups"),
        ),
        out_specs=(P(None, ("groups", "row"), "col", None), P(("groups", "row", "col"), None)),
        check_vma=False,
    )
```

```python
import functools
import math

import jax
import jax.numpy as jnp
from jax import lax
from jax.experimental import pallas as pl
from jax.experimental.pallas import tpu as pltpu
from jax.sharding import PartitionSpec as P

pi_value = 3.141592653589793
dir_block = 512


def with_halo(cells, sides, width):
    for axis, dim in sides:
        count = lax.axis_size(axis)
        ends = count - 1
        head = lax.slice_in_dim(cells, 0, width, axis=dim)
        tail = lax.slice_in_dim(cells, cells.shape[dim] - width, cells.shape[dim], axis=dim)
        cells = jnp.concatenate(
            [
                lax.ppermute(tail, axis, [(i, (i + 1) % count) for i in range(ends)]),
                cells,
                lax.ppermute(head, axis, [((i + 1) % count, i) for i in range(ends)]),
            ],
            axis=dim,
        )
    return cells


def phases(dir_rows, sub_pos, elem_pos):
    sub_angle = pi_value * (
        dir_rows[0][:, None] * sub_pos[0][None, :] + dir_rows[1][:, None] * sub_pos[1][None, :]
    )
    elem_angle = pi_value * (
        dir_rows[0][:, None] * elem_pos[0][None, :] + dir_rows[1][:, None] * elem_pos[1][None, :]
    )
    sub_cos = jnp.cos(sub_angle)[:, :, None]
    sub_sin = jnp.sin(sub_angle)[:, :, None]
    elem_cos = jnp.cos(elem_angle)[:, None, :]
    elem_sin = jnp.sin(elem_angle)[:, None, :]
    cosine = sub_cos * elem_cos - sub_sin * elem_sin
    sine = sub_sin * elem_cos + sub_cos * elem_sin
    count = dir_rows.shape[1]
    return (
        cosine.reshape(count, -1).astype(jnp.bfloat16),
        (-sine).reshape(count, -1).astype(jnp.bfloat16),
    )


def coupling(padded, id_table, library, adjoint):
    rows_here = padded.shape[1] - 4
    cols_here = padded.shape[2] - 4
    elems = library.shape[1]
    field_view = padded.reshape(2, rows_here + 4, cols_here + 4, elems, -1)
    spec = "rcnji,rcnjb->rcib" if adjoint else "rcnij,rcnjb->rcib"
    out_re = jnp.zeros((rows_here, cols_here, elems, field_view.shape[4]), jnp.float32)
    out_im = jnp.zeros_like(out_re)
    for row_off in range(5):
        sources = []
        chosen = []
        for col_off in range(5):
            slot_index = 5 * row_off + col_off
            if adjoint:
                row_start = 4 - row_off
                col_start = 4 - col_off
                chosen.append(
                    id_table[
                        row_start : row_start + rows_here,
                        col_start : col_start + cols_here,
                        slot_index,
                    ]
                )
            else:
                row_start = row_off
                col_start = col_off
                chosen.append(id_table[:, :, slot_index])
            sources.append(
                field_view[:, row_start : row_start + rows_here, col_start : col_start + cols_here]
            )
        source_stack = jnp.stack(sources, axis=3)
        block_stack = library[jnp.stack(chosen, axis=2)]
        block_re = block_stack[..., :elems]
        block_im = block_stack[..., elems:]
        real_real = jnp.einsum(spec, block_re, source_stack[0], preferred_element_type=jnp.float32)
        real_imag = jnp.einsum(spec, block_re, source_stack[1], preferred_element_type=jnp.float32)
        imag_real = jnp.einsum(spec, block_im, source_stack[0], preferred_element_type=jnp.float32)
        imag_imag = jnp.einsum(spec, block_im, source_stack[1], preferred_element_type=jnp.float32)
        if adjoint:
            out_re = out_re + real_real + imag_imag
            out_im = out_im + real_imag - imag_real
        else:
            out_re = out_re + real_real - imag_imag
            out_im = out_im + real_imag + imag_real
    return jnp.stack([out_re, out_im])


def pattern_term(radiated_cols, dirs, sub_pos, elem_pos, row_count, scale):
    half_cols = radiated_cols.shape[1] // 2

    def one_block(begin_row, block_size):
        dir_rows = lax.dynamic_slice_in_dim(dirs, begin_row, block_size, 1)
        cosine, sine = phases(dir_rows, sub_pos, elem_pos)
        cos_part = jnp.dot(cosine, radiated_cols, preferred_element_type=jnp.float32)
        sin_part = jnp.dot(sine, radiated_cols, preferred_element_type=jnp.float32)
        return jnp.concatenate(
            [
                cos_part[:, :half_cols] - sin_part[:, half_cols:],
                cos_part[:, half_cols:] + sin_part[:, :half_cols],
            ],
            axis=1,
        )

    block_count = row_count // dir_block
    starts = jnp.arange(block_count, dtype=jnp.int32) * dir_block
    stacked = lax.map(lambda begin_row: one_block(begin_row, dir_block), starts)
    pieces = stacked.reshape(block_count * dir_block, 2 * half_cols)
    return pieces * scale


def adjoint_piece(carry, residual_rows, dirs, sub_pos, elem_pos):
    row_count = residual_rows.shape[0]
    dims_spec = (((0,), (0,)), ((), ()))

    def add_block(totals, local_start, block_size):
        piece_rows = lax.dynamic_slice_in_dim(residual_rows, local_start, block_size, 0)
        dir_rows = lax.dynamic_slice_in_dim(dirs, local_start, block_size, 1)
        cosine, sine = phases(dir_rows, sub_pos, elem_pos)
        cos_part = lax.dot_general(
            cosine, piece_rows, dims_spec, preferred_element_type=jnp.float32
        )
        sin_part = lax.dot_general(sine, piece_rows, dims_spec, preferred_element_type=jnp.float32)
        return (totals[0] + cos_part, totals[1] + sin_part)

    block_count = row_count // dir_block
    carry = lax.fori_loop(
        0,
        block_count,
        lambda number, totals: add_block(totals, number * dir_block, dir_block),
        carry,
    )
    return carry


def line_terms(image_pattern, residual, beams):
    products = jnp.sum(image_pattern * residual, axis=0)
    squares = jnp.sum(image_pattern * image_pattern, axis=0)
    return (products[:beams] + products[beams:], squares[:beams] + squares[beams:])


def by_elements(currents, library, block_ids, dirs, beam_dir):
    beams = beam_dir.shape[0]
    rows_here = currents.shape[1]
    cols_here = currents.shape[2]
    packed = currents.shape[3]
    elems = library.shape[1]
    side = math.isqrt(elems)
    local_elems = rows_here * cols_here * elems
    total_rows = rows_here * lax.axis_size("row")
    total_cols = cols_here * lax.axis_size("col")
    all_elems = total_rows * total_cols * elems
    scale = 1.0 / math.sqrt(all_elems)
    amplitude = math.sqrt(all_elems) / 16.0
    dir_total = dirs.shape[1]
    share_rows = dir_total // lax.axis_size(("row", "col"))
    row_ids = (lax.axis_index("row") * rows_here + jnp.arange(rows_here, dtype=jnp.int32))[:, None]
    col_ids = (lax.axis_index("col") * cols_here + jnp.arange(cols_here, dtype=jnp.int32))[None, :]
    sub_x = (col_ids * side + 0 * row_ids).reshape(-1).astype(jnp.float32) - (
        total_cols * side - 1
    ) / 2.0
    sub_y = (row_ids * side + 0 * col_ids).reshape(-1).astype(jnp.float32) - (
        total_rows * side - 1
    ) / 2.0
    elem_ids = jnp.arange(elems, dtype=jnp.int32)
    sub_pos = (sub_x, sub_y)
    elem_pos = ((elem_ids % side).astype(jnp.float32), (elem_ids // side).astype(jnp.float32))
    padded_ids = with_halo(block_ids, (("row", 0), ("col", 1)), 2)

    def radiate(current_field):
        rounded = current_field.astype(jnp.bfloat16)
        padded = with_halo(rounded, (("row", 1), ("col", 2)), 2)
        coupled = coupling(padded, block_ids, library, False)
        total_field = (current_field.reshape(coupled.shape) + coupled).astype(jnp.bfloat16)
        return jnp.concatenate(
            [
                total_field[0].reshape(local_elems, beams),
                total_field[1].reshape(local_elems, beams),
            ],
            axis=1,
        )

    zero_acc = jnp.zeros((local_elems, 2 * beams), jnp.float32)

    def share_pattern(current_field):
        radiated_cols = radiate(current_field)
        return lax.psum_scatter(
            pattern_term(
                radiated_cols,
                dirs,
                sub_pos,
                elem_pos,
                share_rows * lax.axis_size(("row", "col")),
                scale,
            ),
            ("row", "col"),
            scatter_dimension=0,
            tiled=True,
        )

    share = share_pattern(currents)
    dir_ids = lax.axis_index(("row", "col")) * share_rows + jnp.arange(share_rows, dtype=jnp.int32)
    real_part = amplitude * (dir_ids[:, None] == beam_dir[None, :]).astype(jnp.float32)
    target = jnp.concatenate([real_part, jnp.zeros_like(real_part)], axis=1)
    residual = share - target
    totals = adjoint_piece(
        (zero_acc, zero_acc),
        lax.all_gather(residual.astype(jnp.bfloat16), ("row", "col"), axis=0, tiled=True),
        dirs,
        sub_pos,
        elem_pos,
    )
    p_part, q_part = totals
    grad_re = (p_part[:, :beams] + q_part[:, beams:]) * scale
    grad_im = (p_part[:, beams:] - q_part[:, :beams]) * scale
    raw_gradient = jnp.stack(
        [
            grad_re.reshape(rows_here, cols_here, packed),
            grad_im.reshape(rows_here, cols_here, packed),
        ]
    )
    rounded = raw_gradient.astype(jnp.bfloat16)
    padded = with_halo(rounded, (("row", 1), ("col", 2)), 2)
    gradient = raw_gradient + coupling(padded, padded_ids, library, True).reshape(
        raw_gradient.shape
    )
    image_pattern = share_pattern(gradient)
    part_num, part_den = line_terms(image_pattern, residual, beams)
    numerator, denominator = lax.psum((part_num, part_den), ("row", "col"))
    step_size = numerator / (denominator + 1e-06)
    moved = gradient.reshape(2, rows_here, cols_here, elems, beams) * step_size
    currents = currents - moved.reshape(currents.shape)
    share = share - image_pattern * jnp.concatenate([step_size, step_size])
    return (currents, share)


lanes = 128
chunk = 256
message = 24
sin_fit = (3.141592580044754, -5.167706878916943, 2.5500313770294833, -0.5980451722529145, 0.07722012475690251)
cos_fit = (0.9999999535196061, -4.934792861473954, 4.058411954029988, -1.3318803713197287, 0.21969716737372766)


def iota(shape, dim):
    return lax.broadcasted_iota(jnp.int32, shape, dim)


def turn(angle):
    whole = jnp.round(angle)
    rest = angle - whole
    half = 0.5 * whole
    sign = 1.0 - 4.0 * (half - jnp.floor(half))
    square = rest * rest
    sine = sin_fit[4]
    cosine = cos_fit[4]
    for k in (3, 2, 1, 0):
        sine = sine * square + sin_fit[k]
        cosine = cosine * square + cos_fit[k]
    return cosine * sign, sine * rest * sign


def shuffle(elems, places):
    size = 2 * elems * places
    row = iota((size, 1), 0)
    kept = 2 * places
    groups = size // lanes
    k = row // lanes
    q = (row % lanes) // kept
    half = (row % kept) // places
    p = row % places
    goal = p * (2 * elems) + half * elems + q * groups + k
    return (goal == iota((size, size), 1)).astype(jnp.float32).astype(jnp.bfloat16)


def split_kernel(
    counts, beams, elems, currents_far, ids_far, library_far, dirs_far, beam_dir_far,
    out, library, dirs, aims, currents, ids, beam_dir, work, arrived,
):
    ranks = counts[0] * counts[1]
    me = lax.axis_index("row") * counts[1] + lax.axis_index("col")
    copies = [
        pltpu.make_async_copy(source, goal, arrived.at[i])
        for i, (source, goal) in enumerate(
            (
                (currents_far, currents),
                (ids_far, ids),
                (library_far, library),
                (dirs_far, dirs),
                (beam_dir_far, beam_dir),
            )
        )
    ]
    for copy in copies:
        copy.start()
    _, rows, cols, packed = currents.shape
    places = rows * cols
    groups = lanes // beams
    order = shuffle(elems, places)
    for copy in copies[:2]:
        copy.wait()
    field = jnp.concatenate([currents[a, b] for a in range(2) for b in range(rows)], axis=0)
    tiles = jnp.concatenate(
        [field[:, i * lanes : (i + 1) * lanes] for i in range(packed // lanes)], axis=0
    ).T
    high = tiles.astype(jnp.bfloat16)
    low = (tiles - high.astype(jnp.float32)).astype(jnp.bfloat16)
    stacked = jnp.concatenate(
        [
            jnp.concatenate([part[k * beams : (k + 1) * beams] for k in range(groups)], axis=1)
            for part in (high, low)
        ],
        axis=0,
    )
    moved = jnp.dot(stacked, order, preferred_element_type=jnp.float32)
    share = beams // ranks
    kept = share * places
    for half in range(2):
        for bl in range(share):
            first = half * beams + bl * ranks
            for p in range(places):
                row = half * kept + bl * places + p
                work[pl.ds(row, ranks, stride=message), :] = moved[
                    first : first + ranks, p * lanes : (p + 1) * lanes
                ]
    slots = ids.shape[2]
    table = jnp.concatenate([ids[a] for a in range(rows)], axis=0).astype(jnp.float32)
    table = jnp.concatenate([table, jnp.zeros((places, lanes - slots), jnp.float32)], axis=1)
    table = jnp.concatenate([table, jnp.zeros_like(table)], axis=0)
    for m in range(ranks):
        work[m * message + 2 * kept : (m + 1) * message, :] = table
    out[...] = work[...].astype(jnp.bfloat16)
    for copy in copies[2:]:
        copy.wait()
    row = iota(aims.shape, 0)
    aim = jnp.full(aims.shape, -1, jnp.int32)
    for bl in range(share):
        aim = jnp.where(row == bl, beam_dir[bl * ranks + me], aim)
    aims[...] = aim


def join_kernel(ranks, beams, elems, currents, moved_in, new_currents, far, work):
    _, rows, cols, packed = currents.shape
    places = rows * cols
    groups = lanes // beams
    share = beams // ranks
    work[...] = moved_in[...].astype(jnp.float32)

    def rows_of(first):
        return work[pl.ds(first, ranks, stride=16), :]

    stacked = jnp.concatenate(
        [
            jnp.concatenate([rows_of(bl * places + p) for p in range(places)], axis=1)
            for bl in range(share)
        ],
        axis=0,
    ).astype(jnp.bfloat16)
    back = lax.dot_general(
        stacked,
        shuffle(elems, places),
        (((1,), (1,)), ((), ())),
        preferred_element_type=jnp.float32,
    )
    tiles = jnp.concatenate([back[:, k * lanes : (k + 1) * lanes] for k in range(groups)], axis=0).T
    kept = 2 * places
    moved = jnp.concatenate(
        [tiles[i * kept : (i + 1) * kept] for i in range(packed // lanes)], axis=1
    )
    for a in range(2):
        for b in range(rows):
            first = (a * rows + b) * cols
            new_currents[a, b] = currents[a, b] - moved[first : first + cols]
    pattern = jnp.concatenate(
        [rows_of(8 + i) + rows_of(8 + 2 * share + i) for i in range(2 * share)], axis=0
    )
    far[...] = pattern


def beam_kernel(
    counts, beams, amplitude, scale, given, library, dirs, aims, out,
    blocks_wide, blocks_tall, off, sub_re, sub_im, chosen, chosen_adj, gathered, phased,
    pattern, residual, image, opened, work,
):
    row_count, col_count = counts
    ranks = row_count * col_count
    values, elems, _ = library.shape
    side = math.isqrt(elems)
    share = beams // ranks
    subs = chosen.shape[1]
    places = subs // ranks
    place_cols = 2
    place_rows = places // place_cols
    total = dirs.shape[1]
    chunks = total // chunk
    field_rows = share * subs
    real_lane = iota((1, lanes), 1) < elems

    s = iota((subs, 1), 0)
    place, rank = s // ranks, s % ranks
    sub_row = (rank // col_count) * place_rows + place // place_cols
    sub_col = (rank % col_count) * place_cols + place % place_cols
    def received(first):
        return opened[pl.ds(first, ranks, stride=message), :]

    opened[...] = given[...].astype(jnp.float32)
    kept = share * places
    field = jnp.concatenate([received(i) + received(kept + i) for i in range(kept)], axis=0)
    ids = jnp.concatenate([received(2 * kept + p) for p in range(places)], axis=0)
    ids = ids.astype(jnp.int32)

    code = sub_row * 64 + sub_col
    t = iota((1, subs), 1)
    t_place, t_rank = t // ranks, t % ranks
    t_row = (t_rank // col_count) * place_rows + t_place // place_cols
    t_col = (t_rank % col_count) * place_cols + t_place % place_cols
    gap = t_row * 64 + t_col - code
    pair = jnp.full((subs, subs), -1, jnp.int32)
    for row_off in range(5):
        for col_off in range(5):
            slot = 5 * row_off + col_off
            pair = jnp.where(
                gap == (row_off - 2) * 64 + (col_off - 2), ids[:, slot : slot + 1], pair
            )
    pair_adjoint = pair.astype(jnp.float32).T.astype(jnp.int32)

    def choose(goal, table):
        for v in range(values):
            goal[v * subs : (v + 1) * subs, :] = (
                (table == v).astype(jnp.float32).astype(jnp.bfloat16)
            )

    def gather(source, x):
        xb = x.astype(jnp.bfloat16)
        beside = jnp.concatenate([xb[i * subs : (i + 1) * subs] for i in range(share)], axis=1)
        sums = jnp.dot(source[...], beside, preferred_element_type=jnp.float32)
        sums = sums.astype(jnp.bfloat16)
        for v in range(values):
            for i in range(share):
                gathered[i * subs : (i + 1) * subs, v * lanes : (v + 1) * lanes] = sums[
                    v * subs : (v + 1) * subs, i * lanes : (i + 1) * lanes
                ]

    choose(chosen, pair)
    gather(chosen, field)
    choose(chosen_adj, pair_adjoint)

    x_sub = (sub_col * side).astype(jnp.float32) - (col_count * place_cols * side - 1) / 2.0
    y_sub = (sub_row * side).astype(jnp.float32) - (row_count * place_rows * side - 1) / 2.0
    e = iota((elems, 1), 0)
    x_off = (e % side).astype(jnp.float32)
    y_off = (e // side).astype(jnp.float32)
    for i in range(chunks):
        cut = slice(i * chunk, (i + 1) * chunk)
        u, v = dirs[0:1, cut], dirs[1:2, cut]
        cosine, sine = turn(u * x_sub + v * y_sub)
        sub_re[:, cut] = cosine
        sub_im[:, cut] = -sine
        cosine, sine = turn(u * x_off + v * y_off)
        both = jnp.concatenate([cosine, -sine], axis=0)
        high = both.astype(jnp.bfloat16)
        off[0:lanes, cut] = high
        off[lanes : 2 * lanes, cut] = (both - high.astype(jnp.float32)).astype(jnp.bfloat16)

    for v in range(values):
        block = library[v].astype(jnp.float32)
        upper = jnp.where(real_lane, block, -block).astype(jnp.bfloat16)
        lower = jnp.concatenate([block[:, elems:], block[:, :elems]], axis=1).astype(jnp.bfloat16)
        both = jnp.concatenate([upper, lower], axis=0)
        blocks_tall[v * lanes : (v + 1) * lanes, :] = both
        blocks_wide[:, v * lanes : (v + 1) * lanes] = both

    def couple():
        return lax.dot_general(
            gathered[...],
            blocks_wide[...],
            (((1,), (1,)), ((), ())),
            preferred_element_type=jnp.float32,
        )

    def couple_adj():
        return jnp.dot(gathered[...], blocks_tall[...], preferred_element_type=jnp.float32)

    def swap(x):
        return jnp.concatenate([x[:, elems:], x[:, :elems]], axis=1)

    def radiate(x):
        total_field = x + couple()
        real = jnp.where(real_lane, total_field, -total_field)
        both = jnp.concatenate([real, swap(total_field)], axis=0).astype(jnp.bfloat16)
        return jnp.concatenate([both, both], axis=1)

    def project(radiated, cut):
        part = jnp.dot(radiated, off[:, cut], preferred_element_type=jnp.float32)
        s_re, s_im = sub_re[:, cut], sub_im[:, cut]
        re, im = [], []
        for bl in range(share):
            p_re = part[bl * subs : (bl + 1) * subs]
            p_im = part[field_rows + bl * subs : field_rows + (bl + 1) * subs]
            re.append(jnp.sum(s_re * p_re - s_im * p_im, axis=0, keepdims=True))
            im.append(jnp.sum(s_re * p_im + s_im * p_re, axis=0, keepdims=True))
        return scale * jnp.concatenate(re + im, axis=0)

    radiated = radiate(field)
    place = aims[0 : 2 * share, 0:1]
    for i in range(chunks):
        cut = slice(i * chunk, (i + 1) * chunk)
        found = project(radiated, cut)
        pattern[:, cut] = found
        rest = found - jnp.where(iota((1, chunk), 1) + i * chunk == place, amplitude, 0.0)
        residual[:, cut] = rest
        rounded = rest.astype(jnp.bfloat16).astype(jnp.float32)
        s_re, s_im = sub_re[:, cut], sub_im[:, cut]
        for bl in range(share):
            r_re = rounded[bl : bl + 1]
            r_im = rounded[share + bl : share + bl + 1]
            phased[bl * subs : (bl + 1) * subs, cut] = (s_re * r_re + s_im * r_im).astype(
                jnp.bfloat16
            )
            phased[field_rows + bl * subs : field_rows + (bl + 1) * subs, cut] = (
                s_re * r_im - s_im * r_re
            ).astype(jnp.bfloat16)
    sums = lax.dot_general(
        phased[...], off[...], (((1,), (1,)), ((), ())), preferred_element_type=jnp.float32
    )
    sums = sums[:, :lanes] + sums[:, lanes:]
    upper, lower = sums[:field_rows], sums[field_rows:]
    back = scale * (jnp.where(real_lane, upper, -upper) + swap(lower))
    gather(chosen_adj, back)
    gradient = back + couple_adj()
    gather(chosen, gradient)
    radiated = radiate(gradient)
    products = jnp.zeros((2 * share, chunk), jnp.float32)
    squares = jnp.zeros((2 * share, chunk), jnp.float32)
    for i in range(chunks):
        cut = slice(i * chunk, (i + 1) * chunk)
        found = project(radiated, cut)
        image[:, cut] = found
        products = products + found * residual[:, cut]
        squares = squares + found * found
    products = jnp.sum(products, axis=1, keepdims=True)
    squares = jnp.sum(squares, axis=1, keepdims=True)
    step = (products[:share] + products[share:]) / (squares[:share] + squares[share:] + 1e-06)
    for bl in range(share):
        for p in range(places):
            first = bl * subs + p * ranks
            work[pl.ds(bl * places + p, ranks, stride=16), :] = (
                gradient[first : first + ranks] * step[bl : bl + 1]
            )
    final = pattern[...] - image[...] * jnp.concatenate([step, step], axis=0)
    high = final.astype(jnp.bfloat16).astype(jnp.float32)
    both = jnp.concatenate([high, final - high], axis=0)
    piece = total // ranks
    for m in range(ranks):
        work[m * 16 + 8 : m * 16 + 16, :] = both[:, m * piece : (m + 1) * piece]
    out[...] = work[...].astype(jnp.bfloat16)


def by_beams(currents, library, block_ids, dirs, beam_dir):
    beams = beam_dir.shape[0]
    _, rows_here, cols_here, _ = currents.shape
    values, elems, _ = library.shape
    counts = (lax.axis_size("row"), lax.axis_size("col"))
    ranks = counts[0] * counts[1]
    share = beams // ranks
    subs = ranks * rows_here * cols_here
    all_elems = subs * elems
    total = dirs.shape[1]
    f32, bf16 = jnp.float32, jnp.bfloat16
    params = pltpu.CompilerParams(vmem_limit_bytes=40 * 2**20)

    def keep(x):
        return pltpu.with_memory_space_constraint(x, pltpu.HBM)

    def exchange(x):
        cut = x.reshape(ranks, -1, lanes)
        return lax.all_to_all(cut, ("row", "col"), 0, 0, tiled=False).reshape(x.shape)

    sent, library_near, dirs_near, aims = pl.pallas_call(
        functools.partial(split_kernel, counts, beams, elems),
        in_specs=[pl.BlockSpec(memory_space=pltpu.HBM)] * 5,
        out_shape=(
            jax.ShapeDtypeStruct((message * ranks, lanes), bf16),
            jax.ShapeDtypeStruct(library.shape, bf16),
            jax.ShapeDtypeStruct(dirs.shape, f32),
            jax.ShapeDtypeStruct((8, lanes), jnp.int32),
        ),
        scratch_shapes=[
            pltpu.VMEM(currents.shape, f32),
            pltpu.VMEM(block_ids.shape, jnp.int32),
            pltpu.SMEM(beam_dir.shape, jnp.int32),
            pltpu.VMEM((message * ranks, lanes), f32),
            pltpu.SemaphoreType.DMA((5,)),
        ],
        compiler_params=params,
    )(keep(currents), keep(block_ids), keep(library), keep(dirs), keep(beam_dir))
    results = pl.pallas_call(
        functools.partial(
            beam_kernel,
            counts,
            beams,
            math.sqrt(all_elems) / 16.0,
            1.0 / math.sqrt(all_elems),
        ),
        out_shape=jax.ShapeDtypeStruct((16 * ranks, lanes), bf16),
        scratch_shapes=[
            pltpu.VMEM((lanes, values * lanes), bf16),
            pltpu.VMEM((values * lanes, lanes), bf16),
            pltpu.VMEM((2 * lanes, total), bf16),
            pltpu.VMEM((subs, total), f32),
            pltpu.VMEM((subs, total), f32),
            pltpu.VMEM((values * subs, subs), bf16),
            pltpu.VMEM((values * subs, subs), bf16),
            pltpu.VMEM((share * subs, values * lanes), bf16),
            pltpu.VMEM((2 * share * subs, total), bf16),
            pltpu.VMEM((2 * share, total), f32),
            pltpu.VMEM((2 * share, total), f32),
            pltpu.VMEM((2 * share, total), f32),
            pltpu.VMEM((message * ranks, lanes), f32),
            pltpu.VMEM((16 * ranks, lanes), f32),
        ],
        compiler_params=params,
    )(exchange(sent), library_near, dirs_near, aims)
    new_currents, far = pl.pallas_call(
        functools.partial(join_kernel, ranks, beams, elems),
        out_shape=(
            jax.ShapeDtypeStruct(currents.shape, f32),
            jax.ShapeDtypeStruct((2 * beams, total // ranks), f32),
        ),
        scratch_shapes=[pltpu.VMEM((16 * ranks, lanes), f32)],
        compiler_params=params,
    )(currents, exchange(results))
    return new_currents, far.T


def local(currents, library, block_ids, dirs, beam_dir):
    beams = beam_dir.shape[0]
    _, rows_here, cols_here, packed = currents.shape
    elems = library.shape[1]
    ranks = lax.axis_size(("row", "col"))
    fits = (
        beams == 2 * ranks
        and (rows_here, cols_here) == (2, 2)
        and 2 * elems == lanes
        and 2 * packed * rows_here * cols_here == lanes * lanes
        and dirs.shape[1] == ranks * lanes
    )
    plan = by_beams if fits else by_elements
    return plan(currents, library, block_ids, dirs, beam_dir)


def solution(mesh):
    return jax.shard_map(
        local,
        mesh=mesh,
        in_specs=(
            P(None, ("groups", "row"), "col", None),
            P(),
            P(("groups", "row"), "col", None),
            P(),
            P("groups"),
        ),
        out_specs=(P(None, ("groups", "row"), "col", None), P(("groups", "row", "col"), None)),
        check_vma=False,
    )
```

```python
import functools
import math

import jax
import jax.numpy as jnp
from jax import lax
from jax.experimental import pallas as pl
from jax.experimental.pallas import tpu as pltpu
from jax.sharding import PartitionSpec as P

pi_value = 3.141592653589793
dir_block = 512


def with_halo(cells, sides, width):
    for axis, dim in sides:
        count = lax.axis_size(axis)
        ends = count - 1
        head = lax.slice_in_dim(cells, 0, width, axis=dim)
        tail = lax.slice_in_dim(cells, cells.shape[dim] - width, cells.shape[dim], axis=dim)
        cells = jnp.concatenate(
            [
                lax.ppermute(tail, axis, [(i, (i + 1) % count) for i in range(ends)]),
                cells,
                lax.ppermute(head, axis, [((i + 1) % count, i) for i in range(ends)]),
            ],
            axis=dim,
        )
    return cells


def phases(dir_rows, sub_pos, elem_pos):
    sub_angle = pi_value * (
        dir_rows[0][:, None] * sub_pos[0][None, :] + dir_rows[1][:, None] * sub_pos[1][None, :]
    )
    elem_angle = pi_value * (
        dir_rows[0][:, None] * elem_pos[0][None, :] + dir_rows[1][:, None] * elem_pos[1][None, :]
    )
    sub_cos = jnp.cos(sub_angle)[:, :, None]
    sub_sin = jnp.sin(sub_angle)[:, :, None]
    elem_cos = jnp.cos(elem_angle)[:, None, :]
    elem_sin = jnp.sin(elem_angle)[:, None, :]
    cosine = sub_cos * elem_cos - sub_sin * elem_sin
    sine = sub_sin * elem_cos + sub_cos * elem_sin
    count = dir_rows.shape[1]
    return (
        cosine.reshape(count, -1).astype(jnp.bfloat16),
        (-sine).reshape(count, -1).astype(jnp.bfloat16),
    )


def coupling(padded, id_table, library, adjoint):
    rows_here = padded.shape[1] - 4
    cols_here = padded.shape[2] - 4
    elems = library.shape[1]
    field_view = padded.reshape(2, rows_here + 4, cols_here + 4, elems, -1)
    spec = "rcnji,rcnjb->rcib" if adjoint else "rcnij,rcnjb->rcib"
    out_re = jnp.zeros((rows_here, cols_here, elems, field_view.shape[4]), jnp.float32)
    out_im = jnp.zeros_like(out_re)
    for row_off in range(5):
        sources = []
        chosen = []
        for col_off in range(5):
            slot_index = 5 * row_off + col_off
            if adjoint:
                row_start = 4 - row_off
                col_start = 4 - col_off
                chosen.append(
                    id_table[
                        row_start : row_start + rows_here,
                        col_start : col_start + cols_here,
                        slot_index,
                    ]
                )
            else:
                row_start = row_off
                col_start = col_off
                chosen.append(id_table[:, :, slot_index])
            sources.append(
                field_view[:, row_start : row_start + rows_here, col_start : col_start + cols_here]
            )
        source_stack = jnp.stack(sources, axis=3)
        block_stack = library[jnp.stack(chosen, axis=2)]
        block_re = block_stack[..., :elems]
        block_im = block_stack[..., elems:]
        real_real = jnp.einsum(spec, block_re, source_stack[0], preferred_element_type=jnp.float32)
        real_imag = jnp.einsum(spec, block_re, source_stack[1], preferred_element_type=jnp.float32)
        imag_real = jnp.einsum(spec, block_im, source_stack[0], preferred_element_type=jnp.float32)
        imag_imag = jnp.einsum(spec, block_im, source_stack[1], preferred_element_type=jnp.float32)
        if adjoint:
            out_re = out_re + real_real + imag_imag
            out_im = out_im + real_imag - imag_real
        else:
            out_re = out_re + real_real - imag_imag
            out_im = out_im + real_imag + imag_real
    return jnp.stack([out_re, out_im])


def pattern_term(radiated_cols, dirs, sub_pos, elem_pos, row_count, scale):
    half_cols = radiated_cols.shape[1] // 2

    def one_block(begin_row, block_size):
        dir_rows = lax.dynamic_slice_in_dim(dirs, begin_row, block_size, 1)
        cosine, sine = phases(dir_rows, sub_pos, elem_pos)
        cos_part = jnp.dot(cosine, radiated_cols, preferred_element_type=jnp.float32)
        sin_part = jnp.dot(sine, radiated_cols, preferred_element_type=jnp.float32)
        return jnp.concatenate(
            [
                cos_part[:, :half_cols] - sin_part[:, half_cols:],
                cos_part[:, half_cols:] + sin_part[:, :half_cols],
            ],
            axis=1,
        )

    block_count = row_count // dir_block
    starts = jnp.arange(block_count, dtype=jnp.int32) * dir_block
    stacked = lax.map(lambda begin_row: one_block(begin_row, dir_block), starts)
    pieces = stacked.reshape(block_count * dir_block, 2 * half_cols)
    return pieces * scale


def adjoint_piece(carry, residual_rows, dirs, sub_pos, elem_pos):
    row_count = residual_rows.shape[0]
    dims_spec = (((0,), (0,)), ((), ()))

    def add_block(totals, local_start, block_size):
        piece_rows = lax.dynamic_slice_in_dim(residual_rows, local_start, block_size, 0)
        dir_rows = lax.dynamic_slice_in_dim(dirs, local_start, block_size, 1)
        cosine, sine = phases(dir_rows, sub_pos, elem_pos)
        cos_part = lax.dot_general(
            cosine, piece_rows, dims_spec, preferred_element_type=jnp.float32
        )
        sin_part = lax.dot_general(sine, piece_rows, dims_spec, preferred_element_type=jnp.float32)
        return (totals[0] + cos_part, totals[1] + sin_part)

    block_count = row_count // dir_block
    carry = lax.fori_loop(
        0,
        block_count,
        lambda number, totals: add_block(totals, number * dir_block, dir_block),
        carry,
    )
    return carry


def line_terms(image_pattern, residual, beams):
    products = jnp.sum(image_pattern * residual, axis=0)
    squares = jnp.sum(image_pattern * image_pattern, axis=0)
    return (products[:beams] + products[beams:], squares[:beams] + squares[beams:])


def by_elements(currents, library, block_ids, dirs, beam_dir):
    beams = beam_dir.shape[0]
    rows_here = currents.shape[1]
    cols_here = currents.shape[2]
    packed = currents.shape[3]
    elems = library.shape[1]
    side = math.isqrt(elems)
    local_elems = rows_here * cols_here * elems
    total_rows = rows_here * lax.axis_size("row")
    total_cols = cols_here * lax.axis_size("col")
    all_elems = total_rows * total_cols * elems
    scale = 1.0 / math.sqrt(all_elems)
    amplitude = math.sqrt(all_elems) / 16.0
    dir_total = dirs.shape[1]
    share_rows = dir_total // lax.axis_size(("row", "col"))
    row_ids = (lax.axis_index("row") * rows_here + jnp.arange(rows_here, dtype=jnp.int32))[:, None]
    col_ids = (lax.axis_index("col") * cols_here + jnp.arange(cols_here, dtype=jnp.int32))[None, :]
    sub_x = (col_ids * side + 0 * row_ids).reshape(-1).astype(jnp.float32) - (
        total_cols * side - 1
    ) / 2.0
    sub_y = (row_ids * side + 0 * col_ids).reshape(-1).astype(jnp.float32) - (
        total_rows * side - 1
    ) / 2.0
    elem_ids = jnp.arange(elems, dtype=jnp.int32)
    sub_pos = (sub_x, sub_y)
    elem_pos = ((elem_ids % side).astype(jnp.float32), (elem_ids // side).astype(jnp.float32))
    padded_ids = with_halo(block_ids, (("row", 0), ("col", 1)), 2)

    def radiate(current_field):
        rounded = current_field.astype(jnp.bfloat16)
        padded = with_halo(rounded, (("row", 1), ("col", 2)), 2)
        coupled = coupling(padded, block_ids, library, False)
        total_field = (current_field.reshape(coupled.shape) + coupled).astype(jnp.bfloat16)
        return jnp.concatenate(
            [
                total_field[0].reshape(local_elems, beams),
                total_field[1].reshape(local_elems, beams),
            ],
            axis=1,
        )

    zero_acc = jnp.zeros((local_elems, 2 * beams), jnp.float32)

    def share_pattern(current_field):
        radiated_cols = radiate(current_field)
        return lax.psum_scatter(
            pattern_term(
                radiated_cols,
                dirs,
                sub_pos,
                elem_pos,
                share_rows * lax.axis_size(("row", "col")),
                scale,
            ),
            ("row", "col"),
            scatter_dimension=0,
            tiled=True,
        )

    share = share_pattern(currents)
    dir_ids = lax.axis_index(("row", "col")) * share_rows + jnp.arange(share_rows, dtype=jnp.int32)
    real_part = amplitude * (dir_ids[:, None] == beam_dir[None, :]).astype(jnp.float32)
    target = jnp.concatenate([real_part, jnp.zeros_like(real_part)], axis=1)
    residual = share - target
    totals = adjoint_piece(
        (zero_acc, zero_acc),
        lax.all_gather(residual.astype(jnp.bfloat16), ("row", "col"), axis=0, tiled=True),
        dirs,
        sub_pos,
        elem_pos,
    )
    p_part, q_part = totals
    grad_re = (p_part[:, :beams] + q_part[:, beams:]) * scale
    grad_im = (p_part[:, beams:] - q_part[:, :beams]) * scale
    raw_gradient = jnp.stack(
        [
            grad_re.reshape(rows_here, cols_here, packed),
            grad_im.reshape(rows_here, cols_here, packed),
        ]
    )
    rounded = raw_gradient.astype(jnp.bfloat16)
    padded = with_halo(rounded, (("row", 1), ("col", 2)), 2)
    gradient = raw_gradient + coupling(padded, padded_ids, library, True).reshape(
        raw_gradient.shape
    )
    image_pattern = share_pattern(gradient)
    part_num, part_den = line_terms(image_pattern, residual, beams)
    numerator, denominator = lax.psum((part_num, part_den), ("row", "col"))
    step_size = numerator / (denominator + 1e-06)
    moved = gradient.reshape(2, rows_here, cols_here, elems, beams) * step_size
    currents = currents - moved.reshape(currents.shape)
    share = share - image_pattern * jnp.concatenate([step_size, step_size])
    return (currents, share)


lanes = 128
chunk = 256
message = 24
sin_fit = (3.141592580044754, -5.167706878916943, 2.5500313770294833, -0.5980451722529145, 0.07722012475690251)
cos_fit = (0.9999999535196061, -4.934792861473954, 4.058411954029988, -1.3318803713197287, 0.21969716737372766)


def iota(shape, dim):
    return lax.broadcasted_iota(jnp.int32, shape, dim)


def turn(angle):
    whole = jnp.round(angle)
    rest = angle - whole
    half = 0.5 * whole
    sign = 1.0 - 4.0 * (half - jnp.floor(half))
    square = rest * rest
    sine = sin_fit[4]
    cosine = cos_fit[4]
    for k in (3, 2, 1, 0):
        sine = sine * square + sin_fit[k]
        cosine = cosine * square + cos_fit[k]
    return cosine * sign, sine * rest * sign


def shuffle(elems, places):
    size = 2 * elems * places
    row = iota((size, 1), 0)
    kept = 2 * places
    groups = size // lanes
    k = row // lanes
    q = (row % lanes) // kept
    half = (row % kept) // places
    p = row % places
    goal = p * (2 * elems) + half * elems + q * groups + k
    return (goal == iota((size, size), 1)).astype(jnp.float32).astype(jnp.bfloat16)


def split_kernel(
    counts, beams, elems, currents_far, ids_far, library_far, dirs_far, beam_dir_far,
    out, library, dirs, aims, currents, ids, beam_dir, work, arrived,
):
    ranks = counts[0] * counts[1]
    me = lax.axis_index("row") * counts[1] + lax.axis_index("col")
    copies = [
        pltpu.make_async_copy(source, goal, arrived.at[i])
        for i, (source, goal) in enumerate(
            (
                (currents_far, currents),
                (ids_far, ids),
                (library_far, library),
                (dirs_far, dirs),
                (beam_dir_far, beam_dir),
            )
        )
    ]
    for copy in copies:
        copy.start()
    _, rows, cols, packed = currents.shape
    places = rows * cols
    groups = lanes // beams
    order = shuffle(elems, places)
    for copy in copies[:2]:
        copy.wait()
    field = jnp.concatenate([currents[a, b] for a in range(2) for b in range(rows)], axis=0)
    tiles = jnp.concatenate(
        [field[:, i * lanes : (i + 1) * lanes] for i in range(packed // lanes)], axis=0
    ).T
    high = tiles.astype(jnp.bfloat16)
    low = (tiles - high.astype(jnp.float32)).astype(jnp.bfloat16)
    stacked = jnp.concatenate(
        [
            jnp.concatenate([part[k * beams : (k + 1) * beams] for k in range(groups)], axis=1)
            for part in (high, low)
        ],
        axis=0,
    )
    moved = jnp.dot(stacked, order, preferred_element_type=jnp.float32)
    share = beams // ranks
    kept = share * places
    for half in range(2):
        for bl in range(share):
            first = half * beams + bl * ranks
            for p in range(places):
                row = half * kept + bl * places + p
                work[pl.ds(row, ranks, stride=message), :] = moved[
                    first : first + ranks, p * lanes : (p + 1) * lanes
                ]
    slots = ids.shape[2]
    table = jnp.concatenate([ids[a] for a in range(rows)], axis=0).astype(jnp.float32)
    table = jnp.concatenate([table, jnp.zeros((places, lanes - slots), jnp.float32)], axis=1)
    table = jnp.concatenate([table, jnp.zeros_like(table)], axis=0)
    for m in range(ranks):
        work[m * message + 2 * kept : (m + 1) * message, :] = table
    out[...] = work[...].astype(jnp.bfloat16)
    for copy in copies[2:]:
        copy.wait()
    row = iota(aims.shape, 0)
    aim = jnp.full(aims.shape, -1, jnp.int32)
    for bl in range(share):
        aim = jnp.where(row == bl, beam_dir[bl * ranks + me], aim)
    aims[...] = aim


def join_kernel(ranks, beams, elems, currents, moved_in, new_currents, far, work):
    _, rows, cols, packed = currents.shape
    places = rows * cols
    groups = lanes // beams
    share = beams // ranks
    work[...] = moved_in[...].astype(jnp.float32)

    def rows_of(first):
        return work[pl.ds(first, ranks, stride=16), :]

    stacked = jnp.concatenate(
        [
            jnp.concatenate([rows_of(bl * places + p) for p in range(places)], axis=1)
            for bl in range(share)
        ],
        axis=0,
    ).astype(jnp.bfloat16)
    back = lax.dot_general(
        stacked,
        shuffle(elems, places),
        (((1,), (1,)), ((), ())),
        preferred_element_type=jnp.float32,
    )
    tiles = jnp.concatenate([back[:, k * lanes : (k + 1) * lanes] for k in range(groups)], axis=0).T
    kept = 2 * places
    moved = jnp.concatenate(
        [tiles[i * kept : (i + 1) * kept] for i in range(packed // lanes)], axis=1
    )
    for a in range(2):
        for b in range(rows):
            first = (a * rows + b) * cols
            new_currents[a, b] = currents[a, b] - moved[first : first + cols]
    pattern = jnp.concatenate(
        [rows_of(8 + i) + rows_of(8 + 2 * share + i) for i in range(2 * share)], axis=0
    )
    far[...] = pattern


def beam_kernel(
    counts, beams, amplitude, scale, given, library, dirs, aims, out,
    blocks_wide, blocks_tall, off, sub_re, sub_im, chosen, chosen_adj, gathered, phased,
    pattern, residual, image, opened, work,
):
    row_count, col_count = counts
    ranks = row_count * col_count
    values, elems, _ = library.shape
    side = math.isqrt(elems)
    share = beams // ranks
    subs = chosen.shape[0]
    places = subs // ranks
    place_cols = 2
    place_rows = places // place_cols
    total = dirs.shape[1]
    chunks = total // chunk
    field_rows = share * subs
    real_lane = iota((1, lanes), 1) < elems

    s = iota((subs, 1), 0)
    place, rank = s // ranks, s % ranks
    sub_row = (rank // col_count) * place_rows + place // place_cols
    sub_col = (rank % col_count) * place_cols + place % place_cols
    def received(first):
        return opened[pl.ds(first, ranks, stride=message), :]

    opened[...] = given[...].astype(jnp.float32)
    kept = share * places
    field = jnp.concatenate([received(i) + received(kept + i) for i in range(kept)], axis=0)
    ids = jnp.concatenate([received(2 * kept + p) for p in range(places)], axis=0)
    ids = ids.astype(jnp.int32)

    code = sub_row * 64 + sub_col
    t = iota((1, subs), 1)
    t_place, t_rank = t // ranks, t % ranks
    t_row = (t_rank // col_count) * place_rows + t_place // place_cols
    t_col = (t_rank % col_count) * place_cols + t_place % place_cols
    gap = t_row * 64 + t_col - code
    pair = jnp.full((subs, subs), -1, jnp.int32)
    for row_off in range(5):
        for col_off in range(5):
            slot = 5 * row_off + col_off
            pair = jnp.where(
                gap == (row_off - 2) * 64 + (col_off - 2), ids[:, slot : slot + 1], pair
            )
    pair_adjoint = pair.astype(jnp.float32).T.astype(jnp.int32)

    def choose(goal, table):
        twice = jnp.concatenate([table, table], axis=1)
        value = iota((1, 2 * subs), 1) // subs
        for v in range(0, values, 2):
            goal[:, v * subs : (v + 2) * subs] = (
                (twice == value + v).astype(jnp.float32).astype(jnp.bfloat16)
            )

    choose(chosen, pair)
    choose(chosen_adj, pair_adjoint)

    def multiply(x, y):
        return x[0] * y[0] - x[1] * y[1], x[0] * y[1] + x[1] * y[0]

    half_x = (col_count * place_cols * side - 1) / 2.0
    half_y = (row_count * place_rows * side - 1) / 2.0

    def sub_turns(along, count, kept, half):
        r = iota((count * kept, 1), 0)
        position = ((r % count) * kept + r // count) * side
        return turn(along * (position.astype(jnp.float32) - half))

    for i in range(chunks):
        cut = slice(i * chunk, (i + 1) * chunk)
        u, v = dirs[0:1, cut], dirs[1:2, cut]
        x_turn = sub_turns(u, col_count, place_cols, half_x)
        y_turn = sub_turns(v, row_count, place_rows, half_y)
        for p in range(places):
            x0 = (p % place_cols) * col_count
            y0 = (p // place_cols) * row_count
            xs = [jnp.concatenate([t[x0 : x0 + col_count]] * row_count, axis=0) for t in x_turn]
            ys = [
                jnp.concatenate(
                    [
                        jnp.broadcast_to(t[y0 + k : y0 + k + 1], (col_count, chunk))
                        for k in range(row_count)
                    ],
                    axis=0,
                )
                for t in y_turn
            ]
            cosine, sine = multiply(xs, ys)
            sub_re[p * ranks : (p + 1) * ranks, cut] = cosine
            sub_im[p * ranks : (p + 1) * ranks, cut] = -sine
        steps = iota((side, 1), 0).astype(jnp.float32)
        x_turn, y_turn = turn(u * steps), turn(v * steps)
        cosine, sine = multiply(
            [jnp.concatenate([t] * side, axis=0) for t in x_turn],
            [
                jnp.concatenate(
                    [jnp.broadcast_to(t[k : k + 1], (side, chunk)) for k in range(side)], axis=0
                )
                for t in y_turn
            ],
        )
        both = jnp.concatenate([cosine, -sine], axis=0)
        high = both.astype(jnp.bfloat16)
        off[0:lanes, cut] = high
        off[lanes : 2 * lanes, cut] = (both - high.astype(jnp.float32)).astype(jnp.bfloat16)

    for v in range(values):
        block = library[v].astype(jnp.float32)
        upper = jnp.where(real_lane, block, -block).astype(jnp.bfloat16)
        lower = jnp.concatenate([block[:, elems:], block[:, :elems]], axis=1).astype(jnp.bfloat16)
        both = jnp.concatenate([upper, lower], axis=0)
        blocks_tall[v * lanes : (v + 1) * lanes, :] = both
        blocks_wide[:, v * lanes : (v + 1) * lanes] = both

    def spread(every):
        every = every.astype(jnp.bfloat16)
        for v in range(values):
            for i in range(share):
                gathered[v * subs : (v + 1) * subs, i * lanes : (i + 1) * lanes] = every[
                    i * subs : (i + 1) * subs, v * lanes : (v + 1) * lanes
                ]

    def collect(source):
        sums = jnp.dot(source[...], gathered[...], preferred_element_type=jnp.float32)
        return jnp.concatenate([sums[:, i * lanes : (i + 1) * lanes] for i in range(share)], axis=0)

    def couple(x):
        spread(
            lax.dot_general(
                x.astype(jnp.bfloat16),
                blocks_tall[...],
                (((1,), (1,)), ((), ())),
                preferred_element_type=jnp.float32,
            )
        )
        return collect(chosen)

    def couple_adj(x):
        spread(jnp.dot(x.astype(jnp.bfloat16), blocks_wide[...], preferred_element_type=jnp.float32))
        return collect(chosen_adj)

    def swap(x):
        return jnp.concatenate([x[:, elems:], x[:, :elems]], axis=1)

    def radiate(x):
        total_field = x + couple(x)
        real = jnp.where(real_lane, total_field, -total_field)
        both = jnp.concatenate([real, swap(total_field)], axis=0).astype(jnp.bfloat16)
        return jnp.concatenate([both, both], axis=1)

    def project(radiated, cut):
        part = jnp.dot(radiated, off[:, cut], preferred_element_type=jnp.float32)
        s_re, s_im = sub_re[:, cut], sub_im[:, cut]
        re, im = [], []
        for bl in range(share):
            p_re = part[bl * subs : (bl + 1) * subs]
            p_im = part[field_rows + bl * subs : field_rows + (bl + 1) * subs]
            re.append(jnp.sum(s_re * p_re - s_im * p_im, axis=0, keepdims=True))
            im.append(jnp.sum(s_re * p_im + s_im * p_re, axis=0, keepdims=True))
        return scale * jnp.concatenate(re + im, axis=0)

    radiated = radiate(field)
    place = aims[0 : 2 * share, 0:1]
    for i in range(chunks):
        cut = slice(i * chunk, (i + 1) * chunk)
        found = project(radiated, cut)
        pattern[:, cut] = found
        rest = found - jnp.where(iota((1, chunk), 1) + i * chunk == place, amplitude, 0.0)
        residual[:, cut] = rest
        rounded = rest.astype(jnp.bfloat16).astype(jnp.float32)
        s_re, s_im = sub_re[:, cut], sub_im[:, cut]
        for bl in range(share):
            r_re = rounded[bl : bl + 1]
            r_im = rounded[share + bl : share + bl + 1]
            phased[bl * subs : (bl + 1) * subs, cut] = (s_re * r_re + s_im * r_im).astype(
                jnp.bfloat16
            )
            phased[field_rows + bl * subs : field_rows + (bl + 1) * subs, cut] = (
                s_re * r_im - s_im * r_re
            ).astype(jnp.bfloat16)
    sums = lax.dot_general(
        phased[...], off[...], (((1,), (1,)), ((), ())), preferred_element_type=jnp.float32
    )
    sums = sums[:, :lanes] + sums[:, lanes:]
    upper, lower = sums[:field_rows], sums[field_rows:]
    back = scale * (jnp.where(real_lane, upper, -upper) + swap(lower))
    gradient = back + couple_adj(back)
    radiated = radiate(gradient)
    products = jnp.zeros((2 * share, chunk), jnp.float32)
    squares = jnp.zeros((2 * share, chunk), jnp.float32)
    for i in range(chunks):
        cut = slice(i * chunk, (i + 1) * chunk)
        found = project(radiated, cut)
        image[:, cut] = found
        products = products + found * residual[:, cut]
        squares = squares + found * found
    products = jnp.sum(products, axis=1, keepdims=True)
    squares = jnp.sum(squares, axis=1, keepdims=True)
    step = (products[:share] + products[share:]) / (squares[:share] + squares[share:] + 1e-06)
    for bl in range(share):
        for p in range(places):
            first = bl * subs + p * ranks
            work[pl.ds(bl * places + p, ranks, stride=16), :] = (
                gradient[first : first + ranks] * step[bl : bl + 1]
            )
    final = pattern[...] - image[...] * jnp.concatenate([step, step], axis=0)
    high = final.astype(jnp.bfloat16).astype(jnp.float32)
    both = jnp.concatenate([high, final - high], axis=0)
    piece = total // ranks
    for m in range(ranks):
        work[m * 16 + 8 : m * 16 + 16, :] = both[:, m * piece : (m + 1) * piece]
    out[...] = work[...].astype(jnp.bfloat16)


def by_beams(currents, library, block_ids, dirs, beam_dir):
    beams = beam_dir.shape[0]
    _, rows_here, cols_here, _ = currents.shape
    values, elems, _ = library.shape
    counts = (lax.axis_size("row"), lax.axis_size("col"))
    ranks = counts[0] * counts[1]
    share = beams // ranks
    subs = ranks * rows_here * cols_here
    all_elems = subs * elems
    total = dirs.shape[1]
    f32, bf16 = jnp.float32, jnp.bfloat16
    params = pltpu.CompilerParams(vmem_limit_bytes=40 * 2**20)

    def keep(x):
        return pltpu.with_memory_space_constraint(x, pltpu.HBM)

    def exchange(x):
        cut = x.reshape(ranks, -1, lanes)
        return lax.all_to_all(cut, ("row", "col"), 0, 0, tiled=False).reshape(x.shape)

    sent, library_near, dirs_near, aims = pl.pallas_call(
        functools.partial(split_kernel, counts, beams, elems),
        in_specs=[pl.BlockSpec(memory_space=pltpu.HBM)] * 5,
        out_shape=(
            jax.ShapeDtypeStruct((message * ranks, lanes), bf16),
            jax.ShapeDtypeStruct(library.shape, bf16),
            jax.ShapeDtypeStruct(dirs.shape, f32),
            jax.ShapeDtypeStruct((8, lanes), jnp.int32),
        ),
        scratch_shapes=[
            pltpu.VMEM(currents.shape, f32),
            pltpu.VMEM(block_ids.shape, jnp.int32),
            pltpu.SMEM(beam_dir.shape, jnp.int32),
            pltpu.VMEM((message * ranks, lanes), f32),
            pltpu.SemaphoreType.DMA((5,)),
        ],
        compiler_params=params,
    )(keep(currents), keep(block_ids), keep(library), keep(dirs), keep(beam_dir))
    results = pl.pallas_call(
        functools.partial(
            beam_kernel,
            counts,
            beams,
            math.sqrt(all_elems) / 16.0,
            1.0 / math.sqrt(all_elems),
        ),
        out_shape=jax.ShapeDtypeStruct((16 * ranks, lanes), bf16),
        scratch_shapes=[
            pltpu.VMEM((lanes, values * lanes), bf16),
            pltpu.VMEM((values * lanes, lanes), bf16),
            pltpu.VMEM((2 * lanes, total), bf16),
            pltpu.VMEM((subs, total), f32),
            pltpu.VMEM((subs, total), f32),
            pltpu.VMEM((subs, values * subs), bf16),
            pltpu.VMEM((subs, values * subs), bf16),
            pltpu.VMEM((values * subs, share * lanes), bf16),
            pltpu.VMEM((2 * share * subs, total), bf16),
            pltpu.VMEM((2 * share, total), f32),
            pltpu.VMEM((2 * share, total), f32),
            pltpu.VMEM((2 * share, total), f32),
            pltpu.VMEM((message * ranks, lanes), f32),
            pltpu.VMEM((16 * ranks, lanes), f32),
        ],
        compiler_params=params,
    )(exchange(sent), library_near, dirs_near, aims)
    new_currents, far = pl.pallas_call(
        functools.partial(join_kernel, ranks, beams, elems),
        out_shape=(
            jax.ShapeDtypeStruct(currents.shape, f32),
            jax.ShapeDtypeStruct((2 * beams, total // ranks), f32),
        ),
        scratch_shapes=[pltpu.VMEM((16 * ranks, lanes), f32)],
        compiler_params=params,
    )(currents, exchange(results))
    return new_currents, far.T


def local(currents, library, block_ids, dirs, beam_dir):
    beams = beam_dir.shape[0]
    _, rows_here, cols_here, packed = currents.shape
    elems = library.shape[1]
    ranks = lax.axis_size(("row", "col"))
    fits = (
        beams == 2 * ranks
        and (rows_here, cols_here) == (2, 2)
        and 2 * elems == lanes
        and 2 * packed * rows_here * cols_here == lanes * lanes
        and dirs.shape[1] == ranks * lanes
    )
    plan = by_beams if fits else by_elements
    return plan(currents, library, block_ids, dirs, beam_dir)


def solution(mesh):
    return jax.shard_map(
        local,
        mesh=mesh,
        in_specs=(
            P(None, ("groups", "row"), "col", None),
            P(),
            P(("groups", "row"), "col", None),
            P(),
            P("groups"),
        ),
        out_specs=(P(None, ("groups", "row"), "col", None), P(("groups", "row", "col"), None)),
        check_vma=False,
    )
```

```python
import functools
import math

import jax
import jax.numpy as jnp
from jax import lax
from jax.experimental import pallas as pl
from jax.experimental.pallas import tpu as pltpu
from jax.sharding import PartitionSpec as P

pi_value = 3.141592653589793
dir_block = 512


def with_halo(cells, sides, width):
    for axis, dim in sides:
        count = lax.axis_size(axis)
        ends = count - 1
        head = lax.slice_in_dim(cells, 0, width, axis=dim)
        tail = lax.slice_in_dim(cells, cells.shape[dim] - width, cells.shape[dim], axis=dim)
        cells = jnp.concatenate(
            [
                lax.ppermute(tail, axis, [(i, (i + 1) % count) for i in range(ends)]),
                cells,
                lax.ppermute(head, axis, [((i + 1) % count, i) for i in range(ends)]),
            ],
            axis=dim,
        )
    return cells


def phases(dir_rows, sub_pos, elem_pos):
    sub_angle = pi_value * (
        dir_rows[0][:, None] * sub_pos[0][None, :] + dir_rows[1][:, None] * sub_pos[1][None, :]
    )
    elem_angle = pi_value * (
        dir_rows[0][:, None] * elem_pos[0][None, :] + dir_rows[1][:, None] * elem_pos[1][None, :]
    )
    sub_cos = jnp.cos(sub_angle)[:, :, None]
    sub_sin = jnp.sin(sub_angle)[:, :, None]
    elem_cos = jnp.cos(elem_angle)[:, None, :]
    elem_sin = jnp.sin(elem_angle)[:, None, :]
    cosine = sub_cos * elem_cos - sub_sin * elem_sin
    sine = sub_sin * elem_cos + sub_cos * elem_sin
    count = dir_rows.shape[1]
    return (
        cosine.reshape(count, -1).astype(jnp.bfloat16),
        (-sine).reshape(count, -1).astype(jnp.bfloat16),
    )


def coupling(padded, id_table, library, adjoint):
    rows_here = padded.shape[1] - 4
    cols_here = padded.shape[2] - 4
    elems = library.shape[1]
    field_view = padded.reshape(2, rows_here + 4, cols_here + 4, elems, -1)
    spec = "rcnji,rcnjb->rcib" if adjoint else "rcnij,rcnjb->rcib"
    out_re = jnp.zeros((rows_here, cols_here, elems, field_view.shape[4]), jnp.float32)
    out_im = jnp.zeros_like(out_re)
    for row_off in range(5):
        sources = []
        chosen = []
        for col_off in range(5):
            slot_index = 5 * row_off + col_off
            if adjoint:
                row_start = 4 - row_off
                col_start = 4 - col_off
                chosen.append(
                    id_table[
                        row_start : row_start + rows_here,
                        col_start : col_start + cols_here,
                        slot_index,
                    ]
                )
            else:
                row_start = row_off
                col_start = col_off
                chosen.append(id_table[:, :, slot_index])
            sources.append(
                field_view[:, row_start : row_start + rows_here, col_start : col_start + cols_here]
            )
        source_stack = jnp.stack(sources, axis=3)
        block_stack = library[jnp.stack(chosen, axis=2)]
        block_re = block_stack[..., :elems]
        block_im = block_stack[..., elems:]
        real_real = jnp.einsum(spec, block_re, source_stack[0], preferred_element_type=jnp.float32)
        real_imag = jnp.einsum(spec, block_re, source_stack[1], preferred_element_type=jnp.float32)
        imag_real = jnp.einsum(spec, block_im, source_stack[0], preferred_element_type=jnp.float32)
        imag_imag = jnp.einsum(spec, block_im, source_stack[1], preferred_element_type=jnp.float32)
        if adjoint:
            out_re = out_re + real_real + imag_imag
            out_im = out_im + real_imag - imag_real
        else:
            out_re = out_re + real_real - imag_imag
            out_im = out_im + real_imag + imag_real
    return jnp.stack([out_re, out_im])


def pattern_term(radiated_cols, dirs, sub_pos, elem_pos, row_count, scale):
    half_cols = radiated_cols.shape[1] // 2

    def one_block(begin_row, block_size):
        dir_rows = lax.dynamic_slice_in_dim(dirs, begin_row, block_size, 1)
        cosine, sine = phases(dir_rows, sub_pos, elem_pos)
        cos_part = jnp.dot(cosine, radiated_cols, preferred_element_type=jnp.float32)
        sin_part = jnp.dot(sine, radiated_cols, preferred_element_type=jnp.float32)
        return jnp.concatenate(
            [
                cos_part[:, :half_cols] - sin_part[:, half_cols:],
                cos_part[:, half_cols:] + sin_part[:, :half_cols],
            ],
            axis=1,
        )

    block_count = row_count // dir_block
    starts = jnp.arange(block_count, dtype=jnp.int32) * dir_block
    stacked = lax.map(lambda begin_row: one_block(begin_row, dir_block), starts)
    pieces = stacked.reshape(block_count * dir_block, 2 * half_cols)
    return pieces * scale


def adjoint_piece(carry, residual_rows, dirs, sub_pos, elem_pos):
    row_count = residual_rows.shape[0]
    dims_spec = (((0,), (0,)), ((), ()))

    def add_block(totals, local_start, block_size):
        piece_rows = lax.dynamic_slice_in_dim(residual_rows, local_start, block_size, 0)
        dir_rows = lax.dynamic_slice_in_dim(dirs, local_start, block_size, 1)
        cosine, sine = phases(dir_rows, sub_pos, elem_pos)
        cos_part = lax.dot_general(
            cosine, piece_rows, dims_spec, preferred_element_type=jnp.float32
        )
        sin_part = lax.dot_general(sine, piece_rows, dims_spec, preferred_element_type=jnp.float32)
        return (totals[0] + cos_part, totals[1] + sin_part)

    block_count = row_count // dir_block
    carry = lax.fori_loop(
        0,
        block_count,
        lambda number, totals: add_block(totals, number * dir_block, dir_block),
        carry,
    )
    return carry


def line_terms(image_pattern, residual, beams):
    products = jnp.sum(image_pattern * residual, axis=0)
    squares = jnp.sum(image_pattern * image_pattern, axis=0)
    return (products[:beams] + products[beams:], squares[:beams] + squares[beams:])


def by_elements(currents, library, block_ids, dirs, beam_dir):
    beams = beam_dir.shape[0]
    rows_here = currents.shape[1]
    cols_here = currents.shape[2]
    packed = currents.shape[3]
    elems = library.shape[1]
    side = math.isqrt(elems)
    local_elems = rows_here * cols_here * elems
    total_rows = rows_here * lax.axis_size("row")
    total_cols = cols_here * lax.axis_size("col")
    all_elems = total_rows * total_cols * elems
    scale = 1.0 / math.sqrt(all_elems)
    amplitude = math.sqrt(all_elems) / 16.0
    dir_total = dirs.shape[1]
    share_rows = dir_total // lax.axis_size(("row", "col"))
    row_ids = (lax.axis_index("row") * rows_here + jnp.arange(rows_here, dtype=jnp.int32))[:, None]
    col_ids = (lax.axis_index("col") * cols_here + jnp.arange(cols_here, dtype=jnp.int32))[None, :]
    sub_x = (col_ids * side + 0 * row_ids).reshape(-1).astype(jnp.float32) - (
        total_cols * side - 1
    ) / 2.0
    sub_y = (row_ids * side + 0 * col_ids).reshape(-1).astype(jnp.float32) - (
        total_rows * side - 1
    ) / 2.0
    elem_ids = jnp.arange(elems, dtype=jnp.int32)
    sub_pos = (sub_x, sub_y)
    elem_pos = ((elem_ids % side).astype(jnp.float32), (elem_ids // side).astype(jnp.float32))
    padded_ids = with_halo(block_ids, (("row", 0), ("col", 1)), 2)

    def radiate(current_field):
        rounded = current_field.astype(jnp.bfloat16)
        padded = with_halo(rounded, (("row", 1), ("col", 2)), 2)
        coupled = coupling(padded, block_ids, library, False)
        total_field = (current_field.reshape(coupled.shape) + coupled).astype(jnp.bfloat16)
        return jnp.concatenate(
            [
                total_field[0].reshape(local_elems, beams),
                total_field[1].reshape(local_elems, beams),
            ],
            axis=1,
        )

    zero_acc = jnp.zeros((local_elems, 2 * beams), jnp.float32)

    def share_pattern(current_field):
        radiated_cols = radiate(current_field)
        return lax.psum_scatter(
            pattern_term(
                radiated_cols,
                dirs,
                sub_pos,
                elem_pos,
                share_rows * lax.axis_size(("row", "col")),
                scale,
            ),
            ("row", "col"),
            scatter_dimension=0,
            tiled=True,
        )

    share = share_pattern(currents)
    dir_ids = lax.axis_index(("row", "col")) * share_rows + jnp.arange(share_rows, dtype=jnp.int32)
    real_part = amplitude * (dir_ids[:, None] == beam_dir[None, :]).astype(jnp.float32)
    target = jnp.concatenate([real_part, jnp.zeros_like(real_part)], axis=1)
    residual = share - target
    totals = adjoint_piece(
        (zero_acc, zero_acc),
        lax.all_gather(residual.astype(jnp.bfloat16), ("row", "col"), axis=0, tiled=True),
        dirs,
        sub_pos,
        elem_pos,
    )
    p_part, q_part = totals
    grad_re = (p_part[:, :beams] + q_part[:, beams:]) * scale
    grad_im = (p_part[:, beams:] - q_part[:, :beams]) * scale
    raw_gradient = jnp.stack(
        [
            grad_re.reshape(rows_here, cols_here, packed),
            grad_im.reshape(rows_here, cols_here, packed),
        ]
    )
    rounded = raw_gradient.astype(jnp.bfloat16)
    padded = with_halo(rounded, (("row", 1), ("col", 2)), 2)
    gradient = raw_gradient + coupling(padded, padded_ids, library, True).reshape(
        raw_gradient.shape
    )
    image_pattern = share_pattern(gradient)
    part_num, part_den = line_terms(image_pattern, residual, beams)
    numerator, denominator = lax.psum((part_num, part_den), ("row", "col"))
    step_size = numerator / (denominator + 1e-06)
    moved = gradient.reshape(2, rows_here, cols_here, elems, beams) * step_size
    currents = currents - moved.reshape(currents.shape)
    share = share - image_pattern * jnp.concatenate([step_size, step_size])
    return (currents, share)


lanes = 128
chunk = 256
message = 24
sin_fit = (3.141592580044754, -5.167706878916943, 2.5500313770294833, -0.5980451722529145, 0.07722012475690251)
cos_fit = (0.9999999535196061, -4.934792861473954, 4.058411954029988, -1.3318803713197287, 0.21969716737372766)


def iota(shape, dim):
    return lax.broadcasted_iota(jnp.int32, shape, dim)


def turn(angle):
    whole = jnp.round(angle)
    rest = angle - whole
    half = 0.5 * whole
    sign = 1.0 - 4.0 * (half - jnp.floor(half))
    square = rest * rest
    sine = sin_fit[4]
    cosine = cos_fit[4]
    for k in (3, 2, 1, 0):
        sine = sine * square + sin_fit[k]
        cosine = cosine * square + cos_fit[k]
    return cosine * sign, sine * rest * sign


def shuffle(elems, places):
    size = 2 * elems * places
    row = iota((size, 1), 0)
    kept = 2 * places
    groups = size // lanes
    k = row // lanes
    q = (row % lanes) // kept
    half = (row % kept) // places
    p = row % places
    goal = p * (2 * elems) + half * elems + q * groups + k
    return (goal == iota((size, size), 1)).astype(jnp.float32).astype(jnp.bfloat16)


def split_kernel(
    counts, beams, elems, currents_far, ids_far, library_far, dirs_far, beam_dir_far,
    out, library, dirs, aims, order, currents, ids, beam_dir, work, arrived,
):
    ranks = counts[0] * counts[1]
    me = lax.axis_index("row") * counts[1] + lax.axis_index("col")
    copies = [
        pltpu.make_async_copy(source, goal, arrived.at[i])
        for i, (source, goal) in enumerate(
            (
                (currents_far, currents),
                (ids_far, ids),
                (library_far, library),
                (dirs_far, dirs),
                (beam_dir_far, beam_dir),
            )
        )
    ]
    for copy in copies:
        copy.start()
    _, rows, cols, packed = currents.shape
    places = rows * cols
    groups = lanes // beams
    order[...] = shuffle(elems, places)
    for copy in copies[:2]:
        copy.wait()
    field = jnp.concatenate([currents[a, b] for a in range(2) for b in range(rows)], axis=0)
    tiles = jnp.concatenate(
        [field[:, i * lanes : (i + 1) * lanes] for i in range(packed // lanes)], axis=0
    ).T
    high = tiles.astype(jnp.bfloat16)
    low = (tiles - high.astype(jnp.float32)).astype(jnp.bfloat16)
    stacked = jnp.concatenate(
        [
            jnp.concatenate([part[k * beams : (k + 1) * beams] for k in range(groups)], axis=1)
            for part in (high, low)
        ],
        axis=0,
    )
    moved = jnp.dot(stacked, order[...], preferred_element_type=jnp.float32)
    share = beams // ranks
    kept = share * places
    for half in range(2):
        for bl in range(share):
            first = half * beams + bl * ranks
            for p in range(places):
                row = half * kept + bl * places + p
                work[pl.ds(row, ranks, stride=message), :] = moved[
                    first : first + ranks, p * lanes : (p + 1) * lanes
                ]
    table = jnp.concatenate([ids[a] for a in range(rows)], axis=0)
    table = jnp.concatenate([table, table], axis=0)
    o = iota((2 * places, 1), 0) % places
    subs = ranks * places
    t = iota((1, lanes), 1) % subs
    t_place, t_rank = t // ranks, t % ranks
    t_row = (t_rank // counts[1]) * rows + t_place // cols
    t_col = (t_rank % counts[1]) * cols + t_place % cols
    row_gap = t_row - (lax.axis_index("row") * rows + o // cols)
    col_gap = t_col - (lax.axis_index("col") * cols + o % cols)
    gap = row_gap * 64 + col_gap
    pair = jnp.full((2 * places, lanes), -1, jnp.int32)
    for row_off in range(5):
        for col_off in range(5):
            slot = 5 * row_off + col_off
            pair = jnp.where(
                gap == (row_off - 2) * 64 + (col_off - 2), table[:, slot : slot + 1], pair
            )
    pair = pair.astype(jnp.float32)
    for m in range(ranks):
        work[m * message + 2 * kept : (m + 1) * message, :] = pair
    out[...] = work[...].astype(jnp.bfloat16)
    for copy in copies[2:]:
        copy.wait()
    row = iota(aims.shape, 0)
    aim = jnp.full(aims.shape, -1, jnp.int32)
    for bl in range(share):
        aim = jnp.where(row == bl, beam_dir[bl * ranks + me], aim)
    aims[...] = aim


def join_kernel(ranks, beams, currents, moved_in, order, new_currents, far, work):
    _, rows, cols, packed = currents.shape
    places = rows * cols
    groups = lanes // beams
    share = beams // ranks
    work[...] = moved_in[...].astype(jnp.float32)

    def rows_of(first):
        return work[pl.ds(first, ranks, stride=16), :]

    stacked = jnp.concatenate(
        [
            jnp.concatenate([rows_of(bl * places + p) for p in range(places)], axis=1)
            for bl in range(share)
        ],
        axis=0,
    ).astype(jnp.bfloat16)
    back = lax.dot_general(
        stacked,
        order[...],
        (((1,), (1,)), ((), ())),
        preferred_element_type=jnp.float32,
    )
    tiles = jnp.concatenate([back[:, k * lanes : (k + 1) * lanes] for k in range(groups)], axis=0).T
    kept = 2 * places
    moved = jnp.concatenate(
        [tiles[i * kept : (i + 1) * kept] for i in range(packed // lanes)], axis=1
    )
    for a in range(2):
        for b in range(rows):
            first = (a * rows + b) * cols
            new_currents[a, b] = currents[a, b] - moved[first : first + cols]
    pattern = jnp.concatenate(
        [rows_of(8 + i) + rows_of(8 + 2 * share + i) for i in range(2 * share)], axis=0
    )
    far[...] = pattern


def beam_kernel(
    counts, beams, amplitude, scale, given, library, dirs, aims, out,
    blocks_wide, blocks_tall, off, sub_re, sub_im, chosen, chosen_adj, gathered, phased,
    pattern, residual, image, opened, work,
):
    row_count, col_count = counts
    ranks = row_count * col_count
    values, elems, _ = library.shape
    side = math.isqrt(elems)
    share = beams // ranks
    subs = chosen.shape[0]
    places = subs // ranks
    place_cols = 2
    place_rows = places // place_cols
    total = dirs.shape[1]
    chunks = total // chunk
    field_rows = share * subs
    real_lane = iota((1, lanes), 1) < elems

    def received(first):
        return opened[pl.ds(first, ranks, stride=message), :]

    opened[...] = given[...].astype(jnp.float32)
    kept = share * places
    field = jnp.concatenate([received(i) + received(kept + i) for i in range(kept)], axis=0)
    pair = jnp.concatenate([received(2 * kept + p) for p in range(places)], axis=0)
    adjoint = pair[:, :subs].T
    pair_adjoint = jnp.concatenate([adjoint, adjoint], axis=1)

    def choose(goal, table):
        value = (iota((1, 2 * subs), 1) // subs).astype(jnp.float32)
        for v in range(0, values, 2):
            goal[:, v * subs : (v + 2) * subs] = (
                (table == value + v).astype(jnp.float32).astype(jnp.bfloat16)
            )

    choose(chosen, pair)
    choose(chosen_adj, pair_adjoint)

    def multiply(x, y):
        return x[0] * y[0] - x[1] * y[1], x[0] * y[1] + x[1] * y[0]

    half_x = (col_count * place_cols * side - 1) / 2.0
    half_y = (row_count * place_rows * side - 1) / 2.0

    def sub_turns(along, count, kept, half):
        r = iota((count * kept, 1), 0)
        position = ((r % count) * kept + r // count) * side
        return turn(along * (position.astype(jnp.float32) - half))

    for i in range(chunks):
        cut = slice(i * chunk, (i + 1) * chunk)
        u, v = dirs[0:1, cut], dirs[1:2, cut]
        x_turn = sub_turns(u, col_count, place_cols, half_x)
        y_turn = sub_turns(v, row_count, place_rows, half_y)
        for p in range(places):
            x0 = (p % place_cols) * col_count
            y0 = (p // place_cols) * row_count
            xs = [jnp.concatenate([t[x0 : x0 + col_count]] * row_count, axis=0) for t in x_turn]
            ys = [
                jnp.concatenate(
                    [
                        jnp.broadcast_to(t[y0 + k : y0 + k + 1], (col_count, chunk))
                        for k in range(row_count)
                    ],
                    axis=0,
                )
                for t in y_turn
            ]
            cosine, sine = multiply(xs, ys)
            sub_re[p * ranks : (p + 1) * ranks, cut] = cosine
            sub_im[p * ranks : (p + 1) * ranks, cut] = -sine
        steps = iota((side, 1), 0).astype(jnp.float32)
        x_turn, y_turn = turn(u * steps), turn(v * steps)
        cosine, sine = multiply(
            [jnp.concatenate([t] * side, axis=0) for t in x_turn],
            [
                jnp.concatenate(
                    [jnp.broadcast_to(t[k : k + 1], (side, chunk)) for k in range(side)], axis=0
                )
                for t in y_turn
            ],
        )
        both = jnp.concatenate([cosine, -sine], axis=0)
        high = both.astype(jnp.bfloat16)
        off[0:lanes, cut] = high
        off[lanes : 2 * lanes, cut] = (both - high.astype(jnp.float32)).astype(jnp.bfloat16)

    for v in range(values):
        block = library[v].astype(jnp.float32)
        upper = jnp.where(real_lane, block, -block).astype(jnp.bfloat16)
        lower = jnp.concatenate([block[:, elems:], block[:, :elems]], axis=1).astype(jnp.bfloat16)
        both = jnp.concatenate([upper, lower], axis=0)
        blocks_tall[v * lanes : (v + 1) * lanes, :] = both
        blocks_wide[:, v * lanes : (v + 1) * lanes] = both

    def spread(every):
        every = every.astype(jnp.bfloat16)
        for v in range(values):
            for i in range(share):
                gathered[v * subs : (v + 1) * subs, i * lanes : (i + 1) * lanes] = every[
                    i * subs : (i + 1) * subs, v * lanes : (v + 1) * lanes
                ]

    def collect(source):
        sums = jnp.dot(source[...], gathered[...], preferred_element_type=jnp.float32)
        return jnp.concatenate([sums[:, i * lanes : (i + 1) * lanes] for i in range(share)], axis=0)

    def couple(x):
        spread(
            lax.dot_general(
                x.astype(jnp.bfloat16),
                blocks_tall[...],
                (((1,), (1,)), ((), ())),
                preferred_element_type=jnp.float32,
            )
        )
        return collect(chosen)

    def couple_adj(x):
        spread(jnp.dot(x.astype(jnp.bfloat16), blocks_wide[...], preferred_element_type=jnp.float32))
        return collect(chosen_adj)

    def swap(x):
        return jnp.concatenate([x[:, elems:], x[:, :elems]], axis=1)

    def radiate(x):
        total_field = x + couple(x)
        real = jnp.where(real_lane, total_field, -total_field)
        both = jnp.concatenate([real, swap(total_field)], axis=0).astype(jnp.bfloat16)
        return jnp.concatenate([both, both], axis=1)

    def project(radiated, cut):
        part = jnp.dot(radiated, off[:, cut], preferred_element_type=jnp.float32)
        s_re, s_im = sub_re[:, cut], sub_im[:, cut]
        re, im = [], []
        for bl in range(share):
            p_re = part[bl * subs : (bl + 1) * subs]
            p_im = part[field_rows + bl * subs : field_rows + (bl + 1) * subs]
            re.append(jnp.sum(s_re * p_re - s_im * p_im, axis=0, keepdims=True))
            im.append(jnp.sum(s_re * p_im + s_im * p_re, axis=0, keepdims=True))
        return scale * jnp.concatenate(re + im, axis=0)

    radiated = radiate(field)
    place = aims[0 : 2 * share, 0:1]
    for i in range(chunks):
        cut = slice(i * chunk, (i + 1) * chunk)
        found = project(radiated, cut)
        pattern[:, cut] = found
        rest = found - jnp.where(iota((1, chunk), 1) + i * chunk == place, amplitude, 0.0)
        residual[:, cut] = rest
        rounded = rest.astype(jnp.bfloat16).astype(jnp.float32)
        s_re, s_im = sub_re[:, cut], sub_im[:, cut]
        for bl in range(share):
            r_re = rounded[bl : bl + 1]
            r_im = rounded[share + bl : share + bl + 1]
            phased[bl * subs : (bl + 1) * subs, cut] = (s_re * r_re + s_im * r_im).astype(
                jnp.bfloat16
            )
            phased[field_rows + bl * subs : field_rows + (bl + 1) * subs, cut] = (
                s_re * r_im - s_im * r_re
            ).astype(jnp.bfloat16)
    sums = lax.dot_general(
        phased[...], off[...], (((1,), (1,)), ((), ())), preferred_element_type=jnp.float32
    )
    sums = sums[:, :lanes] + sums[:, lanes:]
    upper, lower = sums[:field_rows], sums[field_rows:]
    back = scale * (jnp.where(real_lane, upper, -upper) + swap(lower))
    gradient = back + couple_adj(back)
    radiated = radiate(gradient)
    products = jnp.zeros((2 * share, chunk), jnp.float32)
    squares = jnp.zeros((2 * share, chunk), jnp.float32)
    for i in range(chunks):
        cut = slice(i * chunk, (i + 1) * chunk)
        found = project(radiated, cut)
        image[:, cut] = found
        products = products + found * residual[:, cut]
        squares = squares + found * found
    products = jnp.sum(products, axis=1, keepdims=True)
    squares = jnp.sum(squares, axis=1, keepdims=True)
    step = (products[:share] + products[share:]) / (squares[:share] + squares[share:] + 1e-06)
    for bl in range(share):
        for p in range(places):
            first = bl * subs + p * ranks
            work[pl.ds(bl * places + p, ranks, stride=16), :] = (
                gradient[first : first + ranks] * step[bl : bl + 1]
            )
    final = pattern[...] - image[...] * jnp.concatenate([step, step], axis=0)
    high = final.astype(jnp.bfloat16).astype(jnp.float32)
    both = jnp.concatenate([high, final - high], axis=0)
    piece = total // ranks
    for m in range(ranks):
        work[m * 16 + 8 : m * 16 + 16, :] = both[:, m * piece : (m + 1) * piece]
    out[...] = work[...].astype(jnp.bfloat16)


def by_beams(currents, library, block_ids, dirs, beam_dir):
    beams = beam_dir.shape[0]
    _, rows_here, cols_here, packed = currents.shape
    values, elems, _ = library.shape
    counts = (lax.axis_size("row"), lax.axis_size("col"))
    ranks = counts[0] * counts[1]
    share = beams // ranks
    subs = ranks * rows_here * cols_here
    all_elems = subs * elems
    total = dirs.shape[1]
    f32, bf16 = jnp.float32, jnp.bfloat16
    params = pltpu.CompilerParams(vmem_limit_bytes=24 * 2**20)

    def keep(x):
        return pltpu.with_memory_space_constraint(x, pltpu.HBM)

    def exchange(x):
        cut = x.reshape(ranks, -1, lanes)
        return lax.all_to_all(cut, ("row", "col"), 0, 0, tiled=False).reshape(x.shape)

    sent, library_near, dirs_near, aims, order = pl.pallas_call(
        functools.partial(split_kernel, counts, beams, elems),
        in_specs=[pl.BlockSpec(memory_space=pltpu.HBM)] * 5,
        out_shape=(
            jax.ShapeDtypeStruct((message * ranks, lanes), bf16),
            jax.ShapeDtypeStruct(library.shape, bf16),
            jax.ShapeDtypeStruct(dirs.shape, f32),
            jax.ShapeDtypeStruct((8, lanes), jnp.int32),
            jax.ShapeDtypeStruct((2 * packed // beams * rows_here * cols_here,) * 2, bf16),
        ),
        scratch_shapes=[
            pltpu.VMEM(currents.shape, f32),
            pltpu.VMEM(block_ids.shape, jnp.int32),
            pltpu.SMEM(beam_dir.shape, jnp.int32),
            pltpu.VMEM((message * ranks, lanes), f32),
            pltpu.SemaphoreType.DMA((5,)),
        ],
        compiler_params=params,
    )(keep(currents), keep(block_ids), keep(library), keep(dirs), keep(beam_dir))
    results = pl.pallas_call(
        functools.partial(
            beam_kernel,
            counts,
            beams,
            math.sqrt(all_elems) / 16.0,
            1.0 / math.sqrt(all_elems),
        ),
        out_shape=jax.ShapeDtypeStruct((16 * ranks, lanes), bf16),
        scratch_shapes=[
            pltpu.VMEM((lanes, values * lanes), bf16),
            pltpu.VMEM((values * lanes, lanes), bf16),
            pltpu.VMEM((2 * lanes, total), bf16),
            pltpu.VMEM((subs, total), f32),
            pltpu.VMEM((subs, total), f32),
            pltpu.VMEM((subs, values * subs), bf16),
            pltpu.VMEM((subs, values * subs), bf16),
            pltpu.VMEM((values * subs, share * lanes), bf16),
            pltpu.VMEM((2 * share * subs, total), bf16),
            pltpu.VMEM((2 * share, total), f32),
            pltpu.VMEM((2 * share, total), f32),
            pltpu.VMEM((2 * share, total), f32),
            pltpu.VMEM((message * ranks, lanes), f32),
            pltpu.VMEM((16 * ranks, lanes), f32),
        ],
        compiler_params=params,
    )(exchange(sent), library_near, dirs_near, aims)
    new_currents, far = pl.pallas_call(
        functools.partial(join_kernel, ranks, beams),
        out_shape=(
            jax.ShapeDtypeStruct(currents.shape, f32),
            jax.ShapeDtypeStruct((2 * beams, total // ranks), f32),
        ),
        scratch_shapes=[pltpu.VMEM((16 * ranks, lanes), f32)],
        compiler_params=params,
    )(currents, exchange(results), order)
    return new_currents, far.T


def local(currents, library, block_ids, dirs, beam_dir):
    beams = beam_dir.shape[0]
    _, rows_here, cols_here, packed = currents.shape
    elems = library.shape[1]
    ranks = lax.axis_size(("row", "col"))
    fits = (
        beams == 2 * ranks
        and (rows_here, cols_here) == (2, 2)
        and 2 * elems == lanes
        and 2 * packed * rows_here * cols_here == lanes * lanes
        and dirs.shape[1] == ranks * lanes
    )
    plan = by_beams if fits else by_elements
    return plan(currents, library, block_ids, dirs, beam_dir)


def solution(mesh):
    return jax.shard_map(
        local,
        mesh=mesh,
        in_specs=(
            P(None, ("groups", "row"), "col", None),
            P(),
            P(("groups", "row"), "col", None),
            P(),
            P("groups"),
        ),
        out_specs=(P(None, ("groups", "row"), "col", None), P(("groups", "row", "col"), None)),
        check_vma=False,
    )
```

```python
import functools
import math

import jax
import jax.numpy as jnp
from jax import lax
from jax.experimental import pallas as pl
from jax.experimental.pallas import tpu as pltpu
from jax.sharding import PartitionSpec as P

pi_value = 3.141592653589793
dir_block = 512


def with_halo(cells, sides, width):
    for axis, dim in sides:
        count = lax.axis_size(axis)
        ends = count - 1
        head = lax.slice_in_dim(cells, 0, width, axis=dim)
        tail = lax.slice_in_dim(cells, cells.shape[dim] - width, cells.shape[dim], axis=dim)
        cells = jnp.concatenate(
            [
                lax.ppermute(tail, axis, [(i, (i + 1) % count) for i in range(ends)]),
                cells,
                lax.ppermute(head, axis, [((i + 1) % count, i) for i in range(ends)]),
            ],
            axis=dim,
        )
    return cells


def phases(dir_rows, sub_pos, elem_pos):
    sub_angle = pi_value * (
        dir_rows[0][:, None] * sub_pos[0][None, :] + dir_rows[1][:, None] * sub_pos[1][None, :]
    )
    elem_angle = pi_value * (
        dir_rows[0][:, None] * elem_pos[0][None, :] + dir_rows[1][:, None] * elem_pos[1][None, :]
    )
    sub_cos = jnp.cos(sub_angle)[:, :, None]
    sub_sin = jnp.sin(sub_angle)[:, :, None]
    elem_cos = jnp.cos(elem_angle)[:, None, :]
    elem_sin = jnp.sin(elem_angle)[:, None, :]
    cosine = sub_cos * elem_cos - sub_sin * elem_sin
    sine = sub_sin * elem_cos + sub_cos * elem_sin
    count = dir_rows.shape[1]
    return (
        cosine.reshape(count, -1).astype(jnp.bfloat16),
        (-sine).reshape(count, -1).astype(jnp.bfloat16),
    )


def coupling(padded, id_table, library, adjoint):
    rows_here = padded.shape[1] - 4
    cols_here = padded.shape[2] - 4
    elems = library.shape[1]
    field_view = padded.reshape(2, rows_here + 4, cols_here + 4, elems, -1)
    spec = "rcnji,rcnjb->rcib" if adjoint else "rcnij,rcnjb->rcib"
    out_re = jnp.zeros((rows_here, cols_here, elems, field_view.shape[4]), jnp.float32)
    out_im = jnp.zeros_like(out_re)
    for row_off in range(5):
        sources = []
        chosen = []
        for col_off in range(5):
            slot_index = 5 * row_off + col_off
            if adjoint:
                row_start = 4 - row_off
                col_start = 4 - col_off
                chosen.append(
                    id_table[
                        row_start : row_start + rows_here,
                        col_start : col_start + cols_here,
                        slot_index,
                    ]
                )
            else:
                row_start = row_off
                col_start = col_off
                chosen.append(id_table[:, :, slot_index])
            sources.append(
                field_view[:, row_start : row_start + rows_here, col_start : col_start + cols_here]
            )
        source_stack = jnp.stack(sources, axis=3)
        block_stack = library[jnp.stack(chosen, axis=2)]
        block_re = block_stack[..., :elems]
        block_im = block_stack[..., elems:]
        real_real = jnp.einsum(spec, block_re, source_stack[0], preferred_element_type=jnp.float32)
        real_imag = jnp.einsum(spec, block_re, source_stack[1], preferred_element_type=jnp.float32)
        imag_real = jnp.einsum(spec, block_im, source_stack[0], preferred_element_type=jnp.float32)
        imag_imag = jnp.einsum(spec, block_im, source_stack[1], preferred_element_type=jnp.float32)
        if adjoint:
            out_re = out_re + real_real + imag_imag
            out_im = out_im + real_imag - imag_real
        else:
            out_re = out_re + real_real - imag_imag
            out_im = out_im + real_imag + imag_real
    return jnp.stack([out_re, out_im])


def pattern_term(radiated_cols, dirs, sub_pos, elem_pos, row_count, scale):
    half_cols = radiated_cols.shape[1] // 2

    def one_block(begin_row, block_size):
        dir_rows = lax.dynamic_slice_in_dim(dirs, begin_row, block_size, 1)
        cosine, sine = phases(dir_rows, sub_pos, elem_pos)
        cos_part = jnp.dot(cosine, radiated_cols, preferred_element_type=jnp.float32)
        sin_part = jnp.dot(sine, radiated_cols, preferred_element_type=jnp.float32)
        return jnp.concatenate(
            [
                cos_part[:, :half_cols] - sin_part[:, half_cols:],
                cos_part[:, half_cols:] + sin_part[:, :half_cols],
            ],
            axis=1,
        )

    block_count = row_count // dir_block
    starts = jnp.arange(block_count, dtype=jnp.int32) * dir_block
    stacked = lax.map(lambda begin_row: one_block(begin_row, dir_block), starts)
    pieces = stacked.reshape(block_count * dir_block, 2 * half_cols)
    return pieces * scale


def adjoint_piece(carry, residual_rows, dirs, sub_pos, elem_pos):
    row_count = residual_rows.shape[0]
    dims_spec = (((0,), (0,)), ((), ()))

    def add_block(totals, local_start, block_size):
        piece_rows = lax.dynamic_slice_in_dim(residual_rows, local_start, block_size, 0)
        dir_rows = lax.dynamic_slice_in_dim(dirs, local_start, block_size, 1)
        cosine, sine = phases(dir_rows, sub_pos, elem_pos)
        cos_part = lax.dot_general(
            cosine, piece_rows, dims_spec, preferred_element_type=jnp.float32
        )
        sin_part = lax.dot_general(sine, piece_rows, dims_spec, preferred_element_type=jnp.float32)
        return (totals[0] + cos_part, totals[1] + sin_part)

    block_count = row_count // dir_block
    carry = lax.fori_loop(
        0,
        block_count,
        lambda number, totals: add_block(totals, number * dir_block, dir_block),
        carry,
    )
    return carry


def line_terms(image_pattern, residual, beams):
    products = jnp.sum(image_pattern * residual, axis=0)
    squares = jnp.sum(image_pattern * image_pattern, axis=0)
    return (products[:beams] + products[beams:], squares[:beams] + squares[beams:])


def by_elements(currents, library, block_ids, dirs, beam_dir):
    beams = beam_dir.shape[0]
    rows_here = currents.shape[1]
    cols_here = currents.shape[2]
    packed = currents.shape[3]
    elems = library.shape[1]
    side = math.isqrt(elems)
    local_elems = rows_here * cols_here * elems
    total_rows = rows_here * lax.axis_size("row")
    total_cols = cols_here * lax.axis_size("col")
    all_elems = total_rows * total_cols * elems
    scale = 1.0 / math.sqrt(all_elems)
    amplitude = math.sqrt(all_elems) / 16.0
    dir_total = dirs.shape[1]
    share_rows = dir_total // lax.axis_size(("row", "col"))
    row_ids = (lax.axis_index("row") * rows_here + jnp.arange(rows_here, dtype=jnp.int32))[:, None]
    col_ids = (lax.axis_index("col") * cols_here + jnp.arange(cols_here, dtype=jnp.int32))[None, :]
    sub_x = (col_ids * side + 0 * row_ids).reshape(-1).astype(jnp.float32) - (
        total_cols * side - 1
    ) / 2.0
    sub_y = (row_ids * side + 0 * col_ids).reshape(-1).astype(jnp.float32) - (
        total_rows * side - 1
    ) / 2.0
    elem_ids = jnp.arange(elems, dtype=jnp.int32)
    sub_pos = (sub_x, sub_y)
    elem_pos = ((elem_ids % side).astype(jnp.float32), (elem_ids // side).astype(jnp.float32))
    padded_ids = with_halo(block_ids, (("row", 0), ("col", 1)), 2)

    def radiate(current_field):
        rounded = current_field.astype(jnp.bfloat16)
        padded = with_halo(rounded, (("row", 1), ("col", 2)), 2)
        coupled = coupling(padded, block_ids, library, False)
        total_field = (current_field.reshape(coupled.shape) + coupled).astype(jnp.bfloat16)
        return jnp.concatenate(
            [
                total_field[0].reshape(local_elems, beams),
                total_field[1].reshape(local_elems, beams),
            ],
            axis=1,
        )

    zero_acc = jnp.zeros((local_elems, 2 * beams), jnp.float32)

    def share_pattern(current_field):
        radiated_cols = radiate(current_field)
        return lax.psum_scatter(
            pattern_term(
                radiated_cols,
                dirs,
                sub_pos,
                elem_pos,
                share_rows * lax.axis_size(("row", "col")),
                scale,
            ),
            ("row", "col"),
            scatter_dimension=0,
            tiled=True,
        )

    share = share_pattern(currents)
    dir_ids = lax.axis_index(("row", "col")) * share_rows + jnp.arange(share_rows, dtype=jnp.int32)
    real_part = amplitude * (dir_ids[:, None] == beam_dir[None, :]).astype(jnp.float32)
    target = jnp.concatenate([real_part, jnp.zeros_like(real_part)], axis=1)
    residual = share - target
    totals = adjoint_piece(
        (zero_acc, zero_acc),
        lax.all_gather(residual.astype(jnp.bfloat16), ("row", "col"), axis=0, tiled=True),
        dirs,
        sub_pos,
        elem_pos,
    )
    p_part, q_part = totals
    grad_re = (p_part[:, :beams] + q_part[:, beams:]) * scale
    grad_im = (p_part[:, beams:] - q_part[:, :beams]) * scale
    raw_gradient = jnp.stack(
        [
            grad_re.reshape(rows_here, cols_here, packed),
            grad_im.reshape(rows_here, cols_here, packed),
        ]
    )
    rounded = raw_gradient.astype(jnp.bfloat16)
    padded = with_halo(rounded, (("row", 1), ("col", 2)), 2)
    gradient = raw_gradient + coupling(padded, padded_ids, library, True).reshape(
        raw_gradient.shape
    )
    image_pattern = share_pattern(gradient)
    part_num, part_den = line_terms(image_pattern, residual, beams)
    numerator, denominator = lax.psum((part_num, part_den), ("row", "col"))
    step_size = numerator / (denominator + 1e-06)
    moved = gradient.reshape(2, rows_here, cols_here, elems, beams) * step_size
    currents = currents - moved.reshape(currents.shape)
    share = share - image_pattern * jnp.concatenate([step_size, step_size])
    return (currents, share)


lanes = 128
chunk = 256
message = 24
sin_fit = (3.141592580044754, -5.167706878916943, 2.5500313770294833, -0.5980451722529145, 0.07722012475690251)
cos_fit = (0.9999999535196061, -4.934792861473954, 4.058411954029988, -1.3318803713197287, 0.21969716737372766)


def iota(shape, dim):
    return lax.broadcasted_iota(jnp.int32, shape, dim)


def turn(angle):
    whole = jnp.round(angle)
    rest = angle - whole
    half = 0.5 * whole
    sign = 1.0 - 4.0 * (half - jnp.floor(half))
    square = rest * rest
    sine = sin_fit[4]
    cosine = cos_fit[4]
    for k in (3, 2, 1, 0):
        sine = sine * square + sin_fit[k]
        cosine = cosine * square + cos_fit[k]
    return cosine * sign, sine * rest * sign


def shuffle(elems, places):
    size = 2 * elems * places
    row = iota((size, 1), 0)
    kept = 2 * places
    groups = size // lanes
    k = row // lanes
    q = (row % lanes) // kept
    half = (row % kept) // places
    p = row % places
    goal = p * (2 * elems) + half * elems + q * groups + k
    return (goal == iota((size, size), 1)).astype(jnp.float32).astype(jnp.bfloat16)


def split_kernel(
    counts, beams, elems, currents_far, ids_far, library_far, dirs_far, beam_dir_far,
    out, library, dirs, aims, order, currents, ids, beam_dir, work, arrived,
):
    ranks = counts[0] * counts[1]
    me = lax.axis_index("col") * counts[0] + lax.axis_index("row")
    copies = [
        pltpu.make_async_copy(source, goal, arrived.at[i])
        for i, (source, goal) in enumerate(
            (
                (currents_far, currents),
                (ids_far, ids),
                (library_far, library),
                (dirs_far, dirs),
                (beam_dir_far, beam_dir),
            )
        )
    ]
    for copy in copies:
        copy.start()
    _, rows, cols, packed = currents.shape
    places = rows * cols
    groups = lanes // beams
    order[...] = shuffle(elems, places)
    for copy in copies[:2]:
        copy.wait()
    field = jnp.concatenate([currents[a, b] for a in range(2) for b in range(rows)], axis=0)
    tiles = jnp.concatenate(
        [field[:, i * lanes : (i + 1) * lanes] for i in range(packed // lanes)], axis=0
    ).T
    high = tiles.astype(jnp.bfloat16)
    low = (tiles - high.astype(jnp.float32)).astype(jnp.bfloat16)
    stacked = jnp.concatenate(
        [
            jnp.concatenate([part[k * beams : (k + 1) * beams] for k in range(groups)], axis=1)
            for part in (high, low)
        ],
        axis=0,
    )
    moved = jnp.dot(stacked, order[...], preferred_element_type=jnp.float32)
    share = beams // ranks
    kept = share * places
    for half in range(2):
        for bl in range(share):
            first = half * beams + bl * ranks
            for p in range(places):
                row = half * kept + bl * places + p
                work[pl.ds(row, ranks, stride=message), :] = moved[
                    first : first + ranks, p * lanes : (p + 1) * lanes
                ]
    table = jnp.concatenate([ids[a] for a in range(rows)], axis=0)
    table = jnp.concatenate([table, table], axis=0)
    o = iota((2 * places, 1), 0) % places
    subs = ranks * places
    t = iota((1, lanes), 1) % subs
    t_place, t_rank = t // ranks, t % ranks
    t_row = (t_rank % counts[0]) * rows + t_place // cols
    t_col = (t_rank // counts[0]) * cols + t_place % cols
    row_gap = t_row - (lax.axis_index("row") * rows + o // cols)
    col_gap = t_col - (lax.axis_index("col") * cols + o % cols)
    gap = row_gap * 64 + col_gap
    pair = jnp.full((2 * places, lanes), -1, jnp.int32)
    for row_off in range(5):
        for col_off in range(5):
            slot = 5 * row_off + col_off
            pair = jnp.where(
                gap == (row_off - 2) * 64 + (col_off - 2), table[:, slot : slot + 1], pair
            )
    pair = pair.astype(jnp.float32)
    for m in range(ranks):
        work[m * message + 2 * kept : (m + 1) * message, :] = pair
    out[...] = work[...].astype(jnp.bfloat16)
    for copy in copies[2:]:
        copy.wait()
    row = iota(aims.shape, 0)
    aim = jnp.full(aims.shape, -1, jnp.int32)
    for bl in range(share):
        aim = jnp.where(row == bl, beam_dir[bl * ranks + me], aim)
    aims[...] = aim


def join_kernel(ranks, beams, currents, moved_in, order, new_currents, far, work):
    _, rows, cols, packed = currents.shape
    places = rows * cols
    groups = lanes // beams
    share = beams // ranks
    work[...] = moved_in[...].astype(jnp.float32)

    def rows_of(first):
        return work[pl.ds(first, ranks, stride=16), :]

    stacked = jnp.concatenate(
        [
            jnp.concatenate([rows_of(bl * places + p) for p in range(places)], axis=1)
            for bl in range(share)
        ],
        axis=0,
    ).astype(jnp.bfloat16)
    back = lax.dot_general(
        stacked,
        order[...],
        (((1,), (1,)), ((), ())),
        preferred_element_type=jnp.float32,
    )
    tiles = jnp.concatenate([back[:, k * lanes : (k + 1) * lanes] for k in range(groups)], axis=0).T
    kept = 2 * places
    moved = jnp.concatenate(
        [tiles[i * kept : (i + 1) * kept] for i in range(packed // lanes)], axis=1
    )
    for a in range(2):
        for b in range(rows):
            first = (a * rows + b) * cols
            new_currents[a, b] = currents[a, b] - moved[first : first + cols]
    pattern = jnp.concatenate(
        [rows_of(8 + i) + rows_of(8 + 2 * share + i) for i in range(2 * share)], axis=0
    )
    far[...] = pattern


def beam_kernel(
    counts, beams, amplitude, scale, given, library, dirs, aims, out,
    blocks_wide, blocks_tall, off, sub_re, sub_im, chosen, chosen_adj, gathered, phased,
    pattern, residual, image, opened, work,
):
    row_count, col_count = counts
    ranks = row_count * col_count
    values, elems, _ = library.shape
    side = math.isqrt(elems)
    share = beams // ranks
    subs = chosen.shape[0]
    places = subs // ranks
    place_cols = 2
    place_rows = places // place_cols
    total = dirs.shape[1]
    chunks = total // chunk
    field_rows = share * subs
    real_lane = iota((1, lanes), 1) < elems

    def received(first):
        return opened[pl.ds(first, ranks, stride=message), :]

    opened[...] = given[...].astype(jnp.float32)
    kept = share * places
    field = jnp.concatenate([received(i) + received(kept + i) for i in range(kept)], axis=0)
    pair = jnp.concatenate([received(2 * kept + p) for p in range(places)], axis=0)
    adjoint = pair[:, :subs].T
    pair_adjoint = jnp.concatenate([adjoint, adjoint], axis=1)

    def choose(goal, table):
        value = (iota((1, 2 * subs), 1) // subs).astype(jnp.float32)
        for v in range(0, values, 2):
            goal[:, v * subs : (v + 2) * subs] = (
                (table == value + v).astype(jnp.float32).astype(jnp.bfloat16)
            )

    choose(chosen, pair)
    choose(chosen_adj, pair_adjoint)

    def multiply(x, y):
        return x[0] * y[0] - x[1] * y[1], x[0] * y[1] + x[1] * y[0]

    half_x = (col_count * place_cols * side - 1) / 2.0
    half_y = (row_count * place_rows * side - 1) / 2.0

    def sub_turns(along, count, kept, half):
        r = iota((count * kept, 1), 0)
        position = ((r % count) * kept + r // count) * side
        return turn(along * (position.astype(jnp.float32) - half))

    for i in range(chunks):
        cut = slice(i * chunk, (i + 1) * chunk)
        u, v = dirs[0:1, cut], dirs[1:2, cut]
        x_turn = sub_turns(u, col_count, place_cols, half_x)
        y_turn = sub_turns(v, row_count, place_rows, half_y)
        for p in range(places):
            x0 = (p % place_cols) * col_count
            y0 = (p // place_cols) * row_count
            xs = [
                jnp.concatenate(
                    [
                        jnp.broadcast_to(t[x0 + k : x0 + k + 1], (row_count, chunk))
                        for k in range(col_count)
                    ],
                    axis=0,
                )
                for t in x_turn
            ]
            ys = [jnp.concatenate([t[y0 : y0 + row_count]] * col_count, axis=0) for t in y_turn]
            cosine, sine = multiply(xs, ys)
            sub_re[p * ranks : (p + 1) * ranks, cut] = cosine
            sub_im[p * ranks : (p + 1) * ranks, cut] = -sine
        steps = iota((side, 1), 0).astype(jnp.float32)
        x_turn, y_turn = turn(u * steps), turn(v * steps)
        cosine, sine = multiply(
            [jnp.concatenate([t] * side, axis=0) for t in x_turn],
            [
                jnp.concatenate(
                    [jnp.broadcast_to(t[k : k + 1], (side, chunk)) for k in range(side)], axis=0
                )
                for t in y_turn
            ],
        )
        both = jnp.concatenate([cosine, -sine], axis=0)
        high = both.astype(jnp.bfloat16)
        off[0:lanes, cut] = high
        off[lanes : 2 * lanes, cut] = (both - high.astype(jnp.float32)).astype(jnp.bfloat16)

    for v in range(values):
        block = library[v].astype(jnp.float32)
        upper = jnp.where(real_lane, block, -block).astype(jnp.bfloat16)
        lower = jnp.concatenate([block[:, elems:], block[:, :elems]], axis=1).astype(jnp.bfloat16)
        both = jnp.concatenate([upper, lower], axis=0)
        blocks_tall[v * lanes : (v + 1) * lanes, :] = both
        blocks_wide[:, v * lanes : (v + 1) * lanes] = both

    def spread(every):
        every = every.astype(jnp.bfloat16)
        for v in range(values):
            for i in range(share):
                gathered[v * subs : (v + 1) * subs, i * lanes : (i + 1) * lanes] = every[
                    i * subs : (i + 1) * subs, v * lanes : (v + 1) * lanes
                ]

    def collect(source):
        sums = jnp.dot(source[...], gathered[...], preferred_element_type=jnp.float32)
        return jnp.concatenate([sums[:, i * lanes : (i + 1) * lanes] for i in range(share)], axis=0)

    def couple(x):
        spread(
            lax.dot_general(
                x.astype(jnp.bfloat16),
                blocks_tall[...],
                (((1,), (1,)), ((), ())),
                preferred_element_type=jnp.float32,
            )
        )
        return collect(chosen)

    def couple_adj(x):
        spread(jnp.dot(x.astype(jnp.bfloat16), blocks_wide[...], preferred_element_type=jnp.float32))
        return collect(chosen_adj)

    def swap(x):
        return jnp.concatenate([x[:, elems:], x[:, :elems]], axis=1)

    def radiate(x):
        total_field = x + couple(x)
        real = jnp.where(real_lane, total_field, -total_field)
        both = jnp.concatenate([real, swap(total_field)], axis=0).astype(jnp.bfloat16)
        return jnp.concatenate([both, both], axis=1)

    def project(radiated, cut):
        part = jnp.dot(radiated, off[:, cut], preferred_element_type=jnp.float32)
        s_re, s_im = sub_re[:, cut], sub_im[:, cut]
        re, im = [], []
        for bl in range(share):
            p_re = part[bl * subs : (bl + 1) * subs]
            p_im = part[field_rows + bl * subs : field_rows + (bl + 1) * subs]
            re.append(jnp.sum(s_re * p_re - s_im * p_im, axis=0, keepdims=True))
            im.append(jnp.sum(s_re * p_im + s_im * p_re, axis=0, keepdims=True))
        return scale * jnp.concatenate(re + im, axis=0)

    radiated = radiate(field)
    place = aims[0 : 2 * share, 0:1]
    for i in range(chunks):
        cut = slice(i * chunk, (i + 1) * chunk)
        found = project(radiated, cut)
        pattern[:, cut] = found
        rest = found - jnp.where(iota((1, chunk), 1) + i * chunk == place, amplitude, 0.0)
        residual[:, cut] = rest
        rounded = rest.astype(jnp.bfloat16).astype(jnp.float32)
        s_re, s_im = sub_re[:, cut], sub_im[:, cut]
        for bl in range(share):
            r_re = rounded[bl : bl + 1]
            r_im = rounded[share + bl : share + bl + 1]
            phased[bl * subs : (bl + 1) * subs, cut] = (s_re * r_re + s_im * r_im).astype(
                jnp.bfloat16
            )
            phased[field_rows + bl * subs : field_rows + (bl + 1) * subs, cut] = (
                s_re * r_im - s_im * r_re
            ).astype(jnp.bfloat16)
    sums = lax.dot_general(
        phased[...], off[...], (((1,), (1,)), ((), ())), preferred_element_type=jnp.float32
    )
    sums = sums[:, :lanes] + sums[:, lanes:]
    upper, lower = sums[:field_rows], sums[field_rows:]
    back = scale * (jnp.where(real_lane, upper, -upper) + swap(lower))
    gradient = back + couple_adj(back)
    radiated = radiate(gradient)
    products = jnp.zeros((2 * share, chunk), jnp.float32)
    squares = jnp.zeros((2 * share, chunk), jnp.float32)
    for i in range(chunks):
        cut = slice(i * chunk, (i + 1) * chunk)
        found = project(radiated, cut)
        image[:, cut] = found
        products = products + found * residual[:, cut]
        squares = squares + found * found
    products = jnp.sum(products, axis=1, keepdims=True)
    squares = jnp.sum(squares, axis=1, keepdims=True)
    step = (products[:share] + products[share:]) / (squares[:share] + squares[share:] + 1e-06)
    for bl in range(share):
        for p in range(places):
            first = bl * subs + p * ranks
            work[pl.ds(bl * places + p, ranks, stride=16), :] = (
                gradient[first : first + ranks] * step[bl : bl + 1]
            )
    final = pattern[...] - image[...] * jnp.concatenate([step, step], axis=0)
    high = final.astype(jnp.bfloat16).astype(jnp.float32)
    both = jnp.concatenate([high, final - high], axis=0)
    piece = total // ranks
    for m in range(ranks):
        owner = (m % row_count) * col_count + m // row_count
        work[m * 16 + 8 : m * 16 + 16, :] = both[:, owner * piece : (owner + 1) * piece]
    out[...] = work[...].astype(jnp.bfloat16)


def by_beams(currents, library, block_ids, dirs, beam_dir):
    beams = beam_dir.shape[0]
    _, rows_here, cols_here, packed = currents.shape
    values, elems, _ = library.shape
    counts = (lax.axis_size("row"), lax.axis_size("col"))
    ranks = counts[0] * counts[1]
    share = beams // ranks
    subs = ranks * rows_here * cols_here
    all_elems = subs * elems
    total = dirs.shape[1]
    f32, bf16 = jnp.float32, jnp.bfloat16
    params = pltpu.CompilerParams(vmem_limit_bytes=24 * 2**20)

    def keep(x):
        return pltpu.with_memory_space_constraint(x, pltpu.HBM)

    def exchange(x):
        cut = x.reshape(ranks, -1, lanes)
        return lax.all_to_all(cut, ("col", "row"), 0, 0, tiled=False).reshape(x.shape)

    sent, library_near, dirs_near, aims, order = pl.pallas_call(
        functools.partial(split_kernel, counts, beams, elems),
        in_specs=[pl.BlockSpec(memory_space=pltpu.HBM)] * 5,
        out_shape=(
            jax.ShapeDtypeStruct((message * ranks, lanes), bf16),
            jax.ShapeDtypeStruct(library.shape, bf16),
            jax.ShapeDtypeStruct(dirs.shape, f32),
            jax.ShapeDtypeStruct((8, lanes), jnp.int32),
            jax.ShapeDtypeStruct((2 * packed // beams * rows_here * cols_here,) * 2, bf16),
        ),
        scratch_shapes=[
            pltpu.VMEM(currents.shape, f32),
            pltpu.VMEM(block_ids.shape, jnp.int32),
            pltpu.SMEM(beam_dir.shape, jnp.int32),
            pltpu.VMEM((message * ranks, lanes), f32),
            pltpu.SemaphoreType.DMA((5,)),
        ],
        compiler_params=params,
    )(keep(currents), keep(block_ids), keep(library), keep(dirs), keep(beam_dir))
    results = pl.pallas_call(
        functools.partial(
            beam_kernel,
            counts,
            beams,
            math.sqrt(all_elems) / 16.0,
            1.0 / math.sqrt(all_elems),
        ),
        out_shape=jax.ShapeDtypeStruct((16 * ranks, lanes), bf16),
        scratch_shapes=[
            pltpu.VMEM((lanes, values * lanes), bf16),
            pltpu.VMEM((values * lanes, lanes), bf16),
            pltpu.VMEM((2 * lanes, total), bf16),
            pltpu.VMEM((subs, total), f32),
            pltpu.VMEM((subs, total), f32),
            pltpu.VMEM((subs, values * subs), bf16),
            pltpu.VMEM((subs, values * subs), bf16),
            pltpu.VMEM((values * subs, share * lanes), bf16),
            pltpu.VMEM((2 * share * subs, total), bf16),
            pltpu.VMEM((2 * share, total), f32),
            pltpu.VMEM((2 * share, total), f32),
            pltpu.VMEM((2 * share, total), f32),
            pltpu.VMEM((message * ranks, lanes), f32),
            pltpu.VMEM((16 * ranks, lanes), f32),
        ],
        compiler_params=params,
    )(exchange(sent), library_near, dirs_near, aims)
    new_currents, far = pl.pallas_call(
        functools.partial(join_kernel, ranks, beams),
        out_shape=(
            jax.ShapeDtypeStruct(currents.shape, f32),
            jax.ShapeDtypeStruct((2 * beams, total // ranks), f32),
        ),
        scratch_shapes=[pltpu.VMEM((16 * ranks, lanes), f32)],
        compiler_params=params,
    )(currents, exchange(results), order)
    return new_currents, far.T


def local(currents, library, block_ids, dirs, beam_dir):
    beams = beam_dir.shape[0]
    _, rows_here, cols_here, packed = currents.shape
    elems = library.shape[1]
    ranks = lax.axis_size(("row", "col"))
    fits = (
        beams == 2 * ranks
        and (rows_here, cols_here) == (2, 2)
        and 2 * elems == lanes
        and 2 * packed * rows_here * cols_here == lanes * lanes
        and dirs.shape[1] == ranks * lanes
    )
    plan = by_beams if fits else by_elements
    return plan(currents, library, block_ids, dirs, beam_dir)


def solution(mesh):
    return jax.shard_map(
        local,
        mesh=mesh,
        in_specs=(
            P(None, ("groups", "row"), "col", None),
            P(),
            P(("groups", "row"), "col", None),
            P(),
            P("groups"),
        ),
        out_specs=(P(None, ("groups", "row"), "col", None), P(("groups", "row", "col"), None)),
        check_vma=False,
    )
```

```python
import functools
import math

import jax
import jax.numpy as jnp
from jax import lax
from jax.experimental import pallas as pl
from jax.experimental.pallas import tpu as pltpu
from jax.sharding import PartitionSpec as P

pi_value = 3.141592653589793
dir_block = 512


def with_halo(cells, sides, width):
    for axis, dim in sides:
        count = lax.axis_size(axis)
        ends = count - 1
        head = lax.slice_in_dim(cells, 0, width, axis=dim)
        tail = lax.slice_in_dim(cells, cells.shape[dim] - width, cells.shape[dim], axis=dim)
        cells = jnp.concatenate(
            [
                lax.ppermute(tail, axis, [(i, (i + 1) % count) for i in range(ends)]),
                cells,
                lax.ppermute(head, axis, [((i + 1) % count, i) for i in range(ends)]),
            ],
            axis=dim,
        )
    return cells


def phases(dir_rows, sub_pos, elem_pos):
    sub_angle = pi_value * (
        dir_rows[0][:, None] * sub_pos[0][None, :] + dir_rows[1][:, None] * sub_pos[1][None, :]
    )
    elem_angle = pi_value * (
        dir_rows[0][:, None] * elem_pos[0][None, :] + dir_rows[1][:, None] * elem_pos[1][None, :]
    )
    sub_cos = jnp.cos(sub_angle)[:, :, None]
    sub_sin = jnp.sin(sub_angle)[:, :, None]
    elem_cos = jnp.cos(elem_angle)[:, None, :]
    elem_sin = jnp.sin(elem_angle)[:, None, :]
    cosine = sub_cos * elem_cos - sub_sin * elem_sin
    sine = sub_sin * elem_cos + sub_cos * elem_sin
    count = dir_rows.shape[1]
    return (
        cosine.reshape(count, -1).astype(jnp.bfloat16),
        (-sine).reshape(count, -1).astype(jnp.bfloat16),
    )


def coupling(padded, id_table, library, adjoint):
    rows_here = padded.shape[1] - 4
    cols_here = padded.shape[2] - 4
    elems = library.shape[1]
    field_view = padded.reshape(2, rows_here + 4, cols_here + 4, elems, -1)
    spec = "rcnji,rcnjb->rcib" if adjoint else "rcnij,rcnjb->rcib"
    out_re = jnp.zeros((rows_here, cols_here, elems, field_view.shape[4]), jnp.float32)
    out_im = jnp.zeros_like(out_re)
    for row_off in range(5):
        sources = []
        chosen = []
        for col_off in range(5):
            slot_index = 5 * row_off + col_off
            if adjoint:
                row_start = 4 - row_off
                col_start = 4 - col_off
                chosen.append(
                    id_table[
                        row_start : row_start + rows_here,
                        col_start : col_start + cols_here,
                        slot_index,
                    ]
                )
            else:
                row_start = row_off
                col_start = col_off
                chosen.append(id_table[:, :, slot_index])
            sources.append(
                field_view[:, row_start : row_start + rows_here, col_start : col_start + cols_here]
            )
        source_stack = jnp.stack(sources, axis=3)
        block_stack = library[jnp.stack(chosen, axis=2)]
        block_re = block_stack[..., :elems]
        block_im = block_stack[..., elems:]
        real_real = jnp.einsum(spec, block_re, source_stack[0], preferred_element_type=jnp.float32)
        real_imag = jnp.einsum(spec, block_re, source_stack[1], preferred_element_type=jnp.float32)
        imag_real = jnp.einsum(spec, block_im, source_stack[0], preferred_element_type=jnp.float32)
        imag_imag = jnp.einsum(spec, block_im, source_stack[1], preferred_element_type=jnp.float32)
        if adjoint:
            out_re = out_re + real_real + imag_imag
            out_im = out_im + real_imag - imag_real
        else:
            out_re = out_re + real_real - imag_imag
            out_im = out_im + real_imag + imag_real
    return jnp.stack([out_re, out_im])


def pattern_term(radiated_cols, dirs, sub_pos, elem_pos, row_count, scale):
    half_cols = radiated_cols.shape[1] // 2

    def one_block(begin_row, block_size):
        dir_rows = lax.dynamic_slice_in_dim(dirs, begin_row, block_size, 1)
        cosine, sine = phases(dir_rows, sub_pos, elem_pos)
        cos_part = jnp.dot(cosine, radiated_cols, preferred_element_type=jnp.float32)
        sin_part = jnp.dot(sine, radiated_cols, preferred_element_type=jnp.float32)
        return jnp.concatenate(
            [
                cos_part[:, :half_cols] - sin_part[:, half_cols:],
                cos_part[:, half_cols:] + sin_part[:, :half_cols],
            ],
            axis=1,
        )

    block_count = row_count // dir_block
    starts = jnp.arange(block_count, dtype=jnp.int32) * dir_block
    stacked = lax.map(lambda begin_row: one_block(begin_row, dir_block), starts)
    pieces = stacked.reshape(block_count * dir_block, 2 * half_cols)
    return pieces * scale


def adjoint_piece(carry, residual_rows, dirs, sub_pos, elem_pos):
    row_count = residual_rows.shape[0]
    dims_spec = (((0,), (0,)), ((), ()))

    def add_block(totals, local_start, block_size):
        piece_rows = lax.dynamic_slice_in_dim(residual_rows, local_start, block_size, 0)
        dir_rows = lax.dynamic_slice_in_dim(dirs, local_start, block_size, 1)
        cosine, sine = phases(dir_rows, sub_pos, elem_pos)
        cos_part = lax.dot_general(
            cosine, piece_rows, dims_spec, preferred_element_type=jnp.float32
        )
        sin_part = lax.dot_general(sine, piece_rows, dims_spec, preferred_element_type=jnp.float32)
        return (totals[0] + cos_part, totals[1] + sin_part)

    block_count = row_count // dir_block
    carry = lax.fori_loop(
        0,
        block_count,
        lambda number, totals: add_block(totals, number * dir_block, dir_block),
        carry,
    )
    return carry


def line_terms(image_pattern, residual, beams):
    products = jnp.sum(image_pattern * residual, axis=0)
    squares = jnp.sum(image_pattern * image_pattern, axis=0)
    return (products[:beams] + products[beams:], squares[:beams] + squares[beams:])


def by_elements(currents, library, block_ids, dirs, beam_dir):
    beams = beam_dir.shape[0]
    rows_here = currents.shape[1]
    cols_here = currents.shape[2]
    packed = currents.shape[3]
    elems = library.shape[1]
    side = math.isqrt(elems)
    local_elems = rows_here * cols_here * elems
    total_rows = rows_here * lax.axis_size("row")
    total_cols = cols_here * lax.axis_size("col")
    all_elems = total_rows * total_cols * elems
    scale = 1.0 / math.sqrt(all_elems)
    amplitude = math.sqrt(all_elems) / 16.0
    dir_total = dirs.shape[1]
    share_rows = dir_total // lax.axis_size(("row", "col"))
    row_ids = (lax.axis_index("row") * rows_here + jnp.arange(rows_here, dtype=jnp.int32))[:, None]
    col_ids = (lax.axis_index("col") * cols_here + jnp.arange(cols_here, dtype=jnp.int32))[None, :]
    sub_x = (col_ids * side + 0 * row_ids).reshape(-1).astype(jnp.float32) - (
        total_cols * side - 1
    ) / 2.0
    sub_y = (row_ids * side + 0 * col_ids).reshape(-1).astype(jnp.float32) - (
        total_rows * side - 1
    ) / 2.0
    elem_ids = jnp.arange(elems, dtype=jnp.int32)
    sub_pos = (sub_x, sub_y)
    elem_pos = ((elem_ids % side).astype(jnp.float32), (elem_ids // side).astype(jnp.float32))
    padded_ids = with_halo(block_ids, (("row", 0), ("col", 1)), 2)

    def radiate(current_field):
        rounded = current_field.astype(jnp.bfloat16)
        padded = with_halo(rounded, (("row", 1), ("col", 2)), 2)
        coupled = coupling(padded, block_ids, library, False)
        total_field = (current_field.reshape(coupled.shape) + coupled).astype(jnp.bfloat16)
        return jnp.concatenate(
            [
                total_field[0].reshape(local_elems, beams),
                total_field[1].reshape(local_elems, beams),
            ],
            axis=1,
        )

    zero_acc = jnp.zeros((local_elems, 2 * beams), jnp.float32)

    def share_pattern(current_field):
        radiated_cols = radiate(current_field)
        return lax.psum_scatter(
            pattern_term(
                radiated_cols,
                dirs,
                sub_pos,
                elem_pos,
                share_rows * lax.axis_size(("row", "col")),
                scale,
            ),
            ("row", "col"),
            scatter_dimension=0,
            tiled=True,
        )

    share = share_pattern(currents)
    dir_ids = lax.axis_index(("row", "col")) * share_rows + jnp.arange(share_rows, dtype=jnp.int32)
    real_part = amplitude * (dir_ids[:, None] == beam_dir[None, :]).astype(jnp.float32)
    target = jnp.concatenate([real_part, jnp.zeros_like(real_part)], axis=1)
    residual = share - target
    totals = adjoint_piece(
        (zero_acc, zero_acc),
        lax.all_gather(residual.astype(jnp.bfloat16), ("row", "col"), axis=0, tiled=True),
        dirs,
        sub_pos,
        elem_pos,
    )
    p_part, q_part = totals
    grad_re = (p_part[:, :beams] + q_part[:, beams:]) * scale
    grad_im = (p_part[:, beams:] - q_part[:, :beams]) * scale
    raw_gradient = jnp.stack(
        [
            grad_re.reshape(rows_here, cols_here, packed),
            grad_im.reshape(rows_here, cols_here, packed),
        ]
    )
    rounded = raw_gradient.astype(jnp.bfloat16)
    padded = with_halo(rounded, (("row", 1), ("col", 2)), 2)
    gradient = raw_gradient + coupling(padded, padded_ids, library, True).reshape(
        raw_gradient.shape
    )
    image_pattern = share_pattern(gradient)
    part_num, part_den = line_terms(image_pattern, residual, beams)
    numerator, denominator = lax.psum((part_num, part_den), ("row", "col"))
    step_size = numerator / (denominator + 1e-06)
    moved = gradient.reshape(2, rows_here, cols_here, elems, beams) * step_size
    currents = currents - moved.reshape(currents.shape)
    share = share - image_pattern * jnp.concatenate([step_size, step_size])
    return (currents, share)


lanes = 128
chunk = 256
message = 24
span = 4
sin_fit = (3.141592580044754, -5.167706878916943, 2.5500313770294833, -0.5980451722529145, 0.07722012475690251)
cos_fit = (0.9999999535196061, -4.934792861473954, 4.058411954029988, -1.3318803713197287, 0.21969716737372766)


def iota(shape, dim):
    return lax.broadcasted_iota(jnp.int32, shape, dim)


def turn(angle):
    whole = jnp.round(angle)
    rest = angle - whole
    half = 0.5 * whole
    sign = 1.0 - 4.0 * (half - jnp.floor(half))
    square = rest * rest
    sine = sin_fit[4]
    cosine = cos_fit[4]
    for k in (3, 2, 1, 0):
        sine = sine * square + sin_fit[k]
        cosine = cosine * square + cos_fit[k]
    return cosine * sign, sine * rest * sign


def shuffle(elems, places):
    size = 2 * elems * places
    row = iota((size, 1), 0)
    kept = 2 * places
    groups = size // lanes
    k = row // lanes
    q = (row % lanes) // kept
    half = (row % kept) // places
    p = row % places
    goal = p * (2 * elems) + half * elems + q * groups + k
    return (goal == iota((size, size), 1)).astype(jnp.float32).astype(jnp.bfloat16)


def split_kernel(
    counts, beams, elems, currents_far, ids_far, library_far, dirs_far, beam_dir_far,
    out, library, dirs, aims, order, currents, ids, beam_dir, work, arrived,
):
    ranks = counts[0] * counts[1]
    me = lax.axis_index("col") * counts[0] + lax.axis_index("row")
    copies = [
        pltpu.make_async_copy(source, goal, arrived.at[i])
        for i, (source, goal) in enumerate(
            (
                (currents_far, currents),
                (ids_far, ids),
                (library_far, library),
                (dirs_far, dirs),
                (beam_dir_far, beam_dir),
            )
        )
    ]
    for copy in copies:
        copy.start()
    _, rows, cols, packed = currents.shape
    places = rows * cols
    groups = lanes // beams
    order[...] = shuffle(elems, places)
    for copy in copies[:2]:
        copy.wait()
    field = jnp.concatenate([currents[a, b] for a in range(2) for b in range(rows)], axis=0)
    tiles = jnp.concatenate(
        [field[:, i * lanes : (i + 1) * lanes] for i in range(packed // lanes)], axis=0
    ).T
    high = tiles.astype(jnp.bfloat16)
    low = (tiles - high.astype(jnp.float32)).astype(jnp.bfloat16)
    stacked = jnp.concatenate(
        [
            jnp.concatenate([part[k * beams : (k + 1) * beams] for k in range(groups)], axis=1)
            for part in (high, low)
        ],
        axis=0,
    )
    moved = jnp.dot(stacked, order[...], preferred_element_type=jnp.float32)
    share = beams // ranks
    kept = share * places
    for half in range(2):
        for bl in range(share):
            first = half * beams + bl * ranks
            for p in range(places):
                row = half * kept + bl * places + p
                work[pl.ds(row, ranks, stride=message), :] = moved[
                    first : first + ranks, p * lanes : (p + 1) * lanes
                ]
    table = jnp.concatenate([ids[a] for a in range(rows)], axis=0)
    table = jnp.concatenate([table, table], axis=0)
    o = iota((2 * places, 1), 0) % places
    subs = ranks * places
    t = iota((1, lanes), 1) % subs
    t_place, t_rank = t // ranks, t % ranks
    t_row = (t_rank % counts[0]) * rows + t_place // cols
    t_col = (t_rank // counts[0]) * cols + t_place % cols
    row_gap = t_row - (lax.axis_index("row") * rows + o // cols)
    col_gap = t_col - (lax.axis_index("col") * cols + o % cols)
    gap = row_gap * 64 + col_gap
    pair = jnp.full((2 * places, lanes), -1, jnp.int32)
    for row_off in range(5):
        for col_off in range(5):
            slot = 5 * row_off + col_off
            pair = jnp.where(
                gap == (row_off - 2) * 64 + (col_off - 2), table[:, slot : slot + 1], pair
            )
    pair = pair.astype(jnp.float32)
    for m in range(ranks):
        work[m * message + 2 * kept : (m + 1) * message, :] = pair
    out[...] = work[...].astype(jnp.bfloat16)
    for copy in copies[2:]:
        copy.wait()
    row = iota(aims.shape, 0)
    aim = jnp.full(aims.shape, -1, jnp.int32)
    for bl in range(share):
        aim = jnp.where(row == bl, beam_dir[bl * ranks + me], aim)
    aims[...] = aim


def join_kernel(
    ranks, beams, currents, moved_in, order, new_currents_out, far_out, work, new_currents, far, gone
):
    _, rows, cols, packed = currents.shape
    places = rows * cols
    groups = lanes // beams
    share = beams // ranks
    work[...] = moved_in[...].astype(jnp.float32)

    def rows_of(first):
        return work[pl.ds(first, ranks, stride=16), :]

    pattern = jnp.concatenate(
        [rows_of(8 + i) + rows_of(8 + 2 * share + i) for i in range(2 * share)], axis=0
    )
    far[...] = pattern
    sent_far = pltpu.make_async_copy(far, far_out, gone.at[0])
    sent_far.start()
    stacked = jnp.concatenate(
        [
            jnp.concatenate([rows_of(bl * places + p) for p in range(places)], axis=1)
            for bl in range(share)
        ],
        axis=0,
    ).astype(jnp.bfloat16)
    back = lax.dot_general(
        stacked,
        order[...],
        (((1,), (1,)), ((), ())),
        preferred_element_type=jnp.float32,
    )
    tiles = jnp.concatenate([back[:, k * lanes : (k + 1) * lanes] for k in range(groups)], axis=0).T
    kept = 2 * places
    moved = jnp.concatenate(
        [tiles[i * kept : (i + 1) * kept] for i in range(packed // lanes)], axis=1
    )
    for a in range(2):
        for b in range(rows):
            first = (a * rows + b) * cols
            new_currents[a, b] = currents[a, b] - moved[first : first + cols]
    sent_currents = pltpu.make_async_copy(new_currents, new_currents_out, gone.at[1])
    sent_currents.start()
    sent_far.wait()
    sent_currents.wait()


def beam_kernel(
    counts, beams, amplitude, scale, given, library, dirs, aims, out,
    blocks_wide, blocks_tall, off, sub_re, sub_im, chosen, chosen_adj, gathered, phased,
    pattern, residual, image, opened, work,
):
    row_count, col_count = counts
    ranks = row_count * col_count
    values, elems, _ = library.shape
    side = math.isqrt(elems)
    share = beams // ranks
    subs = chosen.shape[0]
    places = subs // ranks
    place_cols = 2
    place_rows = places // place_cols
    total = dirs.shape[1]
    chunks = total // chunk
    field_rows = share * subs
    real_lane = iota((1, lanes), 1) < elems

    def received(first):
        return opened[pl.ds(first, ranks, stride=message), :]

    opened[...] = given[...].astype(jnp.float32)
    kept = share * places
    field = jnp.concatenate([received(i) + received(kept + i) for i in range(kept)], axis=0)
    pair = jnp.concatenate([received(2 * kept + p) for p in range(places)], axis=0)
    adjoint = pair[:, :subs].T
    pair_adjoint = jnp.concatenate([adjoint, adjoint], axis=1)

    def choose(goal, table):
        value = (iota((1, 2 * subs), 1) // subs).astype(jnp.float32)
        for v in range(0, values, 2):
            goal[:, v * subs : (v + 2) * subs] = (
                (table == value + v).astype(jnp.float32).astype(jnp.bfloat16)
            )

    choose(chosen, pair)
    choose(chosen_adj, pair_adjoint)

    def multiply(x, y):
        return x[0] * y[0] - x[1] * y[1], x[0] * y[1] + x[1] * y[0]

    half_x = (col_count * place_cols * side - 1) / 2.0
    half_y = (row_count * place_rows * side - 1) / 2.0

    def sub_turns(along, count, kept, half):
        r = iota((count * kept, 1), 0)
        position = ((r % count) * kept + r // count) * side
        return turn(along * (position.astype(jnp.float32) - half))

    for i in range(chunks):
        cut = slice(i * chunk, (i + 1) * chunk)
        u, v = dirs[0:1, cut], dirs[1:2, cut]
        x_turn = sub_turns(u, col_count, place_cols, half_x)
        y_turn = sub_turns(v, row_count, place_rows, half_y)
        for p in range(places):
            x0 = (p % place_cols) * col_count
            y0 = (p // place_cols) * row_count
            xs = [
                jnp.concatenate(
                    [
                        jnp.broadcast_to(t[x0 + k : x0 + k + 1], (row_count, chunk))
                        for k in range(col_count)
                    ],
                    axis=0,
                )
                for t in x_turn
            ]
            ys = [jnp.concatenate([t[y0 : y0 + row_count]] * col_count, axis=0) for t in y_turn]
            cosine, sine = multiply(xs, ys)
            sub_re[p * ranks : (p + 1) * ranks, cut] = cosine
            sub_im[p * ranks : (p + 1) * ranks, cut] = -sine
        steps = iota((side, 1), 0).astype(jnp.float32)
        x_turn, y_turn = turn(u * steps), turn(v * steps)
        cosine, sine = multiply(
            [jnp.concatenate([t] * side, axis=0) for t in x_turn],
            [
                jnp.concatenate(
                    [jnp.broadcast_to(t[k : k + 1], (side, chunk)) for k in range(side)], axis=0
                )
                for t in y_turn
            ],
        )
        both = jnp.concatenate([cosine, -sine], axis=0)
        high = both.astype(jnp.bfloat16)
        off[0:lanes, cut] = high
        off[lanes : 2 * lanes, cut] = (both - high.astype(jnp.float32)).astype(jnp.bfloat16)

    for v in range(values):
        block = library[v].astype(jnp.float32)
        upper = jnp.where(real_lane, block, -block).astype(jnp.bfloat16)
        lower = jnp.concatenate([block[:, elems:], block[:, :elems]], axis=1).astype(jnp.bfloat16)
        both = jnp.concatenate([upper, lower], axis=0)
        blocks_tall[v * lanes : (v + 1) * lanes, :] = both
        blocks_wide[:, v * lanes : (v + 1) * lanes] = both

    def spread(every):
        every = every.astype(jnp.bfloat16)
        for v in range(values):
            for i in range(share):
                gathered[v * subs : (v + 1) * subs, i * lanes : (i + 1) * lanes] = every[
                    i * subs : (i + 1) * subs, v * lanes : (v + 1) * lanes
                ]

    def collect(source):
        sums = jnp.dot(source[...], gathered[...], preferred_element_type=jnp.float32)
        return jnp.concatenate([sums[:, i * lanes : (i + 1) * lanes] for i in range(share)], axis=0)

    def couple(x):
        spread(
            lax.dot_general(
                x.astype(jnp.bfloat16),
                blocks_tall[...],
                (((1,), (1,)), ((), ())),
                preferred_element_type=jnp.float32,
            )
        )
        return collect(chosen)

    def couple_adj(x):
        spread(jnp.dot(x.astype(jnp.bfloat16), blocks_wide[...], preferred_element_type=jnp.float32))
        return collect(chosen_adj)

    def swap(x):
        return jnp.concatenate([x[:, elems:], x[:, :elems]], axis=1)

    def radiate(x):
        total_field = x + couple(x)
        real = jnp.where(real_lane, total_field, -total_field)
        both = jnp.concatenate([real, swap(total_field)], axis=0).astype(jnp.bfloat16)
        return jnp.concatenate([both, both], axis=1)

    def project(part, cut):
        s_re, s_im = sub_re[:, cut], sub_im[:, cut]
        re, im = [], []
        for bl in range(share):
            p_re = part[bl * subs : (bl + 1) * subs]
            p_im = part[field_rows + bl * subs : field_rows + (bl + 1) * subs]
            re.append(jnp.sum(s_re * p_re - s_im * p_im, axis=0, keepdims=True))
            im.append(jnp.sum(s_re * p_im + s_im * p_re, axis=0, keepdims=True))
        return scale * jnp.concatenate(re + im, axis=0)

    radiated = radiate(field)
    place = aims[0 : 2 * share, 0:1]
    for i in range(chunks):
        cut = slice(i * chunk, (i + 1) * chunk)
        if i % span == 0:
            parts = jnp.dot(
                radiated,
                off[:, i * chunk : (i + span) * chunk],
                preferred_element_type=jnp.float32,
            )
        found = project(parts[:, (i % span) * chunk : (i % span + 1) * chunk], cut)
        pattern[:, cut] = found
        rest = found - jnp.where(iota((1, chunk), 1) + i * chunk == place, amplitude, 0.0)
        residual[:, cut] = rest
        rounded = rest.astype(jnp.bfloat16).astype(jnp.float32)
        s_re, s_im = sub_re[:, cut], sub_im[:, cut]
        for bl in range(share):
            r_re = rounded[bl : bl + 1]
            r_im = rounded[share + bl : share + bl + 1]
            phased[bl * subs : (bl + 1) * subs, cut] = (s_re * r_re + s_im * r_im).astype(
                jnp.bfloat16
            )
            phased[field_rows + bl * subs : field_rows + (bl + 1) * subs, cut] = (
                s_re * r_im - s_im * r_re
            ).astype(jnp.bfloat16)
    sums = lax.dot_general(
        phased[...], off[...], (((1,), (1,)), ((), ())), preferred_element_type=jnp.float32
    )
    sums = sums[:, :lanes] + sums[:, lanes:]
    upper, lower = sums[:field_rows], sums[field_rows:]
    back = scale * (jnp.where(real_lane, upper, -upper) + swap(lower))
    gradient = back + couple_adj(back)
    radiated = radiate(gradient)
    products = jnp.zeros((2 * share, chunk), jnp.float32)
    squares = jnp.zeros((2 * share, chunk), jnp.float32)
    for i in range(chunks):
        cut = slice(i * chunk, (i + 1) * chunk)
        if i % span == 0:
            parts = jnp.dot(
                radiated,
                off[:, i * chunk : (i + span) * chunk],
                preferred_element_type=jnp.float32,
            )
        found = project(parts[:, (i % span) * chunk : (i % span + 1) * chunk], cut)
        image[:, cut] = found
        products = products + found * residual[:, cut]
        squares = squares + found * found
    products = jnp.sum(products, axis=1, keepdims=True)
    squares = jnp.sum(squares, axis=1, keepdims=True)
    step = (products[:share] + products[share:]) / (squares[:share] + squares[share:] + 1e-06)
    for bl in range(share):
        for p in range(places):
            first = bl * subs + p * ranks
            work[pl.ds(bl * places + p, ranks, stride=16), :] = (
                gradient[first : first + ranks] * step[bl : bl + 1]
            )
    final = pattern[...] - image[...] * jnp.concatenate([step, step], axis=0)
    high = final.astype(jnp.bfloat16).astype(jnp.float32)
    both = jnp.concatenate([high, final - high], axis=0)
    piece = total // ranks
    for m in range(ranks):
        owner = (m % row_count) * col_count + m // row_count
        work[m * 16 + 8 : m * 16 + 16, :] = both[:, owner * piece : (owner + 1) * piece]
    out[...] = work[...].astype(jnp.bfloat16)


def by_beams(currents, library, block_ids, dirs, beam_dir):
    beams = beam_dir.shape[0]
    _, rows_here, cols_here, packed = currents.shape
    values, elems, _ = library.shape
    counts = (lax.axis_size("row"), lax.axis_size("col"))
    ranks = counts[0] * counts[1]
    share = beams // ranks
    subs = ranks * rows_here * cols_here
    all_elems = subs * elems
    total = dirs.shape[1]
    f32, bf16 = jnp.float32, jnp.bfloat16
    params = pltpu.CompilerParams(vmem_limit_bytes=24 * 2**20)

    def keep(x):
        return pltpu.with_memory_space_constraint(x, pltpu.HBM)

    def exchange(x):
        cut = x.reshape(ranks, -1, lanes)
        return lax.all_to_all(cut, ("col", "row"), 0, 0, tiled=False).reshape(x.shape)

    sent, library_near, dirs_near, aims, order = pl.pallas_call(
        functools.partial(split_kernel, counts, beams, elems),
        in_specs=[pl.BlockSpec(memory_space=pltpu.HBM)] * 5,
        out_shape=(
            jax.ShapeDtypeStruct((message * ranks, lanes), bf16),
            jax.ShapeDtypeStruct(library.shape, bf16),
            jax.ShapeDtypeStruct(dirs.shape, f32),
            jax.ShapeDtypeStruct((8, lanes), jnp.int32),
            jax.ShapeDtypeStruct((2 * packed // beams * rows_here * cols_here,) * 2, bf16),
        ),
        scratch_shapes=[
            pltpu.VMEM(currents.shape, f32),
            pltpu.VMEM(block_ids.shape, jnp.int32),
            pltpu.SMEM(beam_dir.shape, jnp.int32),
            pltpu.VMEM((message * ranks, lanes), f32),
            pltpu.SemaphoreType.DMA((5,)),
        ],
        compiler_params=params,
    )(keep(currents), keep(block_ids), keep(library), keep(dirs), keep(beam_dir))
    results = pl.pallas_call(
        functools.partial(
            beam_kernel,
            counts,
            beams,
            math.sqrt(all_elems) / 16.0,
            1.0 / math.sqrt(all_elems),
        ),
        out_shape=jax.ShapeDtypeStruct((16 * ranks, lanes), bf16),
        scratch_shapes=[
            pltpu.VMEM((lanes, values * lanes), bf16),
            pltpu.VMEM((values * lanes, lanes), bf16),
            pltpu.VMEM((2 * lanes, total), bf16),
            pltpu.VMEM((subs, total), f32),
            pltpu.VMEM((subs, total), f32),
            pltpu.VMEM((subs, values * subs), bf16),
            pltpu.VMEM((subs, values * subs), bf16),
            pltpu.VMEM((values * subs, share * lanes), bf16),
            pltpu.VMEM((2 * share * subs, total), bf16),
            pltpu.VMEM((2 * share, total), f32),
            pltpu.VMEM((2 * share, total), f32),
            pltpu.VMEM((2 * share, total), f32),
            pltpu.VMEM((message * ranks, lanes), f32),
            pltpu.VMEM((16 * ranks, lanes), f32),
        ],
        compiler_params=params,
    )(exchange(sent), library_near, dirs_near, aims)
    new_currents, far = pl.pallas_call(
        functools.partial(join_kernel, ranks, beams),
        out_shape=(
            jax.ShapeDtypeStruct(currents.shape, f32),
            jax.ShapeDtypeStruct((2 * beams, total // ranks), f32),
        ),
        out_specs=[pl.BlockSpec(memory_space=pltpu.HBM)] * 2,
        scratch_shapes=[
            pltpu.VMEM((16 * ranks, lanes), f32),
            pltpu.VMEM(currents.shape, f32),
            pltpu.VMEM((2 * beams, total // ranks), f32),
            pltpu.SemaphoreType.DMA((2,)),
        ],
        compiler_params=params,
    )(currents, exchange(results), order)
    return new_currents, far.T


def local(currents, library, block_ids, dirs, beam_dir):
    beams = beam_dir.shape[0]
    _, rows_here, cols_here, packed = currents.shape
    elems = library.shape[1]
    ranks = lax.axis_size(("row", "col"))
    fits = (
        beams == 2 * ranks
        and (rows_here, cols_here) == (2, 2)
        and 2 * elems == lanes
        and 2 * packed * rows_here * cols_here == lanes * lanes
        and dirs.shape[1] == ranks * lanes
    )
    plan = by_beams if fits else by_elements
    return plan(currents, library, block_ids, dirs, beam_dir)


def solution(mesh):
    return jax.shard_map(
        local,
        mesh=mesh,
        in_specs=(
            P(None, ("groups", "row"), "col", None),
            P(),
            P(("groups", "row"), "col", None),
            P(),
            P("groups"),
        ),
        out_specs=(P(None, ("groups", "row"), "col", None), P(("groups", "row", "col"), None)),
        check_vma=False,
    )
```
